32 devices in a mesh: dp: 8 (over z, x), tensor: 4 (over y, core).
Axes of the slice: x: 2, y: 2, z: 4, core: 2. Of those that a mesh axis runs over, the one named last changes fastest.
Arguments:
- tokens: bfloat16 [24576, 512], P(('dp', 'tensor')), may hold values from -6 to 6
- lengths: int32 [16, 4], P('dp'), may hold values from 1 to 768, 1536 in all within a row
- w_qkv: bfloat16 [512, 3, 512], P(None, None, 'tensor'), may hold values from -0.25 to 0.25
- w_out: bfloat16 [512, 512], P('tensor'), may hold values from -1 to 1
- w_up: bfloat16 [512, 2048], P(None, 'tensor'), may hold values from -0.25 to 0.25
- w_down: bfloat16 [2048, 512], P('tensor'), may hold values from -0.125 to 0.125
- w_pool: bfloat16 [1536, 512], replicated, may hold values from -0.15625 to 0.15625
- gain_one: float32 [512], replicated, may hold values from 0.5 to 1.5
- gain_two: float32 [512], replicated, may hold values from 0.5 to 1.5
- pooled_grad: bfloat16 [8192, 512], P(('dp', 'tensor')), may hold values from -6 to 6
Outputs:
- pooled: bfloat16 [8192, 512], P(('dp', 'tensor'))
- rms_block: float32 [], replicated
- rms_pool: float32 [], replicated
- grad_tokens: bfloat16 [24576, 512], P(('dp', 'tensor'))
- grad_qkv: float32 [512, 3, 512], P(None, None, 'tensor')
- grad_out: float32 [512, 512], P('tensor')
- grad_up: float32 [512, 2048], P(None, 'tensor')
- grad_down: float32 [2048, 512], P('tensor')
- grad_pool: float32 [1536, 512], replicated
- grad_gain_one: float32 [512], replicated
- grad_gain_two: float32 [512], replicated
The draws below stay inside these ranges and needn't reach their ends.
Inputs may be any that keep to these rules, and one draw needn't show every extreme that they name: Each row holds 4 sequences whose lengths sum to 1536; the longest of every row is exactly 768.
All inputs are finite; a program needn't handle non-finite values.
Results may differ from the reference program's by a relative error of at most 0.018.
Values may be sent and summed in bfloat16 or wider, within the bound.
A program may use at most 256 MiB of HBM per device.

```python
import math
import jax
import jax.numpy as jnp
import numpy as np
from jax import lax

D = 512
HEADS = 8
HEAD = 64
FF = 2048
POOL = 3
SEGS = 4
ROW = 1536
ROWS = 16
TOKENS = 24576
POOLED = 8192


def block_scale(stream_key, extent, shards, low, top_value):
    level = 1.0
    for dim, shards_of in shards:
        steps = jax.random.uniform(jax.random.fold_in(jax.random.fold_in(stream_key, 6), dim), (shards_of,), jnp.float32, low / len(shards), top_value / len(shards))
        level = level * jnp.repeat(jnp.exp(steps), extent[dim] // shards_of).reshape((-1,) + (1,) * (len(extent) - 1 - dim))
    return level


def profile(count, total, most, lean):
    loads = [(1 << 20) // math.isqrt(standing ** lean) + 1 for standing in range(2, count + 1)]
    rest, counts = total - most - (count - 1), [1] * (count - 1)
    while rest > 0:
        candidates = [i for i in range(count - 1) if counts[i] < most]
        whole, left = sum([loads[i] for i in candidates]), rest
        for i in candidates:
            more = min(most - counts[i], max(1, left * loads[i] // whole), rest)
            counts[i] = counts[i] + more
            rest = rest - more
    return np.array([most] + counts)


def uneven_parts(stream_key, number_of, total, limit, lean):
    if number_of == 2:
        one = jax.random.randint(stream_key, (), max(1, total - limit), min(limit, total - 1) + 1)
        return jnp.stack([one, total - one])
    tallies = jnp.asarray(profile(number_of, total, limit, lean), jnp.int32)
    pairs = (number_of - 1) // 2
    giver, sink = tallies[1:1 + 2 * pairs:2], tallies[2:2 + 2 * pairs:2]
    room = jnp.minimum(giver - 1, limit - sink)
    moved = jax.random.randint(jax.random.fold_in(stream_key, 1), (pairs,), 0, 1 << 20) % (room + 1)
    tallies = tallies.at[1:1 + 2 * pairs:2].set(giver - moved).at[2:2 + 2 * pairs:2].set(sink + moved)
    return tallies[jax.random.permutation(jax.random.fold_in(stream_key, 2), number_of)]


def noise(key, shape, deviation, bound, pieces=(), kind=jnp.bfloat16):
    gain = block_scale(key, shape, pieces, -0.22, 0.18) if pieces else 1.0
    values = jax.random.normal(key, shape, jnp.float32) * deviation * gain
    return jnp.minimum(jnp.maximum(values, -bound), bound).astype(kind)


def setup_inputs(seed: int = 0) -> dict:
    seeds = jax.random.split(jax.random.key(seed), 11)
    tokens = noise(seeds[0], (TOKENS, D), 1.0, 6.0, ((0, 32),))
    lengths = jax.vmap(lambda own: uneven_parts(own, SEGS, ROW, ROW // 2, 0))(jax.random.split(seeds[1], ROWS)).reshape((ROWS, SEGS)).astype(jnp.int32)
    w_qkv = noise(seeds[2], (D, 3, HEADS * HEAD), D ** -0.5, 0.25, ((2, 4),))
    w_out = noise(seeds[3], (HEADS * HEAD, D), (HEADS * HEAD // 16) ** -0.5, 1.0, ((0, 4),))
    w_up = noise(seeds[4], (D, FF), D ** -0.5, 0.25, ((1, 4),))
    w_down = noise(seeds[5], (FF, D), FF ** -0.5, 0.125, ((0, 4),))
    w_pool = noise(seeds[6], (POOL * D, D), (POOL * D) ** -0.5, 0.15625)
    gain_one = jnp.clip(1.0 + 0.1 * jax.random.normal(seeds[7], (D,), jnp.float32), 0.5, 1.5)
    gain_two = jnp.clip(1.0 + 0.1 * jax.random.normal(seeds[8], (D,), jnp.float32), 0.5, 1.5)
    pooled_grad = noise(seeds[9], (POOLED, D), 1.0, 6.0, ((0, 32),))
    return {"tokens": tokens, "lengths": lengths, "w_qkv": w_qkv, "w_out": w_out, "w_up": w_up, "w_down": w_down, "w_pool": w_pool, "gain_one": gain_one, "gain_two": gain_two, "pooled_grad": pooled_grad}


EPS = 1e-06
NEG = -1000000000.0
HIGH = lax.Precision.HIGHEST

@jax.custom_vjp
def low(v):
    return lax.optimization_barrier(v.astype(jnp.bfloat16)).astype(jnp.float32)

@jax.custom_vjp
def low_back(v):
    return v

def low_keep(v):
    return (low(v), None)

def low_pass(kept, grad):
    return (grad,)

def back_keep(v):
    return (v, None)

def back_low(kept, grad):
    return (low(grad),)
low.defvjp(low_keep, low_pass)
low_back.defvjp(back_keep, back_low)

def doc_table(lengths, row_len):
    seg_ends = jnp.cumsum(lengths, axis=1).astype(jnp.int32)
    position = jnp.arange(row_len, dtype=jnp.int32)
    in_row = lax.optimization_barrier(jnp.sum((position[None, :, None] >= seg_ends[:, None, :]).astype(jnp.int32), axis=2))
    row_ids = jnp.arange(lengths.shape[0], dtype=jnp.int32)[:, None] * lengths.shape[1]
    return (in_row + row_ids).astype(jnp.int32)

def rotation(positions, head_size):
    half_size = head_size // 2
    frequency = jnp.exp(-math.log(10000.0) * jnp.arange(half_size, dtype=jnp.float32) / half_size)
    phase_angle = positions.astype(jnp.float32)[:, None, None] * frequency
    return (jnp.cos(phase_angle), jnp.sin(phase_angle))

def rotate(vectors, cosine, sine_part):
    half_size = vectors.shape[-1] // 2
    front_half = vectors[..., :half_size]
    back_half = vectors[..., half_size:]
    return jnp.concatenate([front_half * cosine - back_half * sine_part, front_half * sine_part + back_half * cosine], axis=-1)

def layer_row(weights, row_tokens, row_docs):
    w_qkv, w_out, w_up, w_down, w_pool, gain_one, gain_two = weights
    row_len, width = row_tokens.shape
    head_cols = w_qkv.shape[2]
    normed_one = low(row_tokens * lax.rsqrt(lax.optimization_barrier(jnp.mean(row_tokens * row_tokens, axis=1, keepdims=True)) + EPS) * gain_one)
    projected = low_back(jnp.einsum('td,dcf->tcf', normed_one, w_qkv, precision=HIGH))
    cosine, sine_part = rotation(jnp.arange(row_len, dtype=jnp.int32), HEAD)
    queries = low(rotate(projected[:, 0].reshape(row_len, HEADS, HEAD), cosine, sine_part))
    key_rows = low(rotate(projected[:, 1].reshape(row_len, HEADS, HEAD), cosine, sine_part))
    values = low(projected[:, 2].reshape(row_len, HEADS, HEAD))
    scores = low_back(jnp.einsum('qhe,khe->hqk', queries, key_rows, precision=HIGH) * HEAD ** (-0.5))
    position = jnp.arange(row_len, dtype=jnp.int32)
    allowed = (position[None, :] <= position[:, None]) & (row_docs[None, :] == row_docs[:, None])
    scores = jnp.where(allowed[None], scores, NEG)
    row_max = lax.optimization_barrier(jnp.max(scores, axis=2, keepdims=True))
    exp_scores = jnp.exp(scores - row_max)
    attn_probs = low(exp_scores / lax.optimization_barrier(jnp.sum(exp_scores, axis=2, keepdims=True)))
    mixed = jnp.einsum('hqk,khe->qhe', attn_probs, values, precision=HIGH).reshape(row_len, head_cols)
    mixed_heads = low_back(low(mixed))
    hidden_one = row_tokens + low_back(jnp.dot(mixed_heads, w_out, precision=HIGH))
    normed_two = low(hidden_one * lax.rsqrt(lax.optimization_barrier(jnp.mean(hidden_one * hidden_one, axis=1, keepdims=True)) + EPS) * gain_two)
    pre_act = low_back(jnp.dot(normed_two, w_up, precision=HIGH))
    activated = low(jax.nn.gelu(pre_act, approximate=True))
    hidden_two = hidden_one + low_back(jnp.dot(activated, w_down, precision=HIGH))
    shifted = jnp.concatenate([jnp.zeros((POOL - 1, width), hidden_two.dtype), hidden_two[:row_len - (POOL - 1)]], axis=0)
    prev_docs = jnp.concatenate([jnp.full((POOL - 1,), -1, jnp.int32), row_docs[:row_len - (POOL - 1)]])
    shifted = low(jnp.where((prev_docs == row_docs)[:, None], shifted, jnp.zeros_like(shifted)))
    pooled = jnp.dot(shifted.reshape(row_len // POOL, POOL * width), w_pool, precision=HIGH)
    return (pooled, jnp.sum(hidden_two * hidden_two))

def reference(tokens, lengths, w_qkv, w_out, w_up, w_down, w_pool, gain_one, gain_two, pooled_grad):
    row_total = lengths.shape[0]
    row_len = tokens.shape[0] // row_total
    width = tokens.shape[1]
    doc_ids = doc_table(lengths, row_len)

    def forward(tokens_f, *weights):

        def one_row(pair):
            return layer_row(weights, pair[0], pair[1])
        pooled_rows, squares = lax.map(jax.checkpoint(one_row), (tokens_f.reshape(row_total, row_len, width), doc_ids))
        return (pooled_rows.reshape(row_total * row_len // POOL, width), jnp.sum(squares))
    float_args = [item.astype(jnp.float32) for item in (tokens, w_qkv, w_out, w_up, w_down, w_pool, gain_one, gain_two)]
    pooled, back_fn, block_square = jax.vjp(forward, *float_args, has_aux=True)
    grads = back_fn(pooled_grad.astype(jnp.float32))
    rms_block = jnp.sqrt(block_square / (tokens.shape[0] * width))
    rms_pool = jnp.sqrt(jnp.sum(pooled * pooled) / (pooled.shape[0] * width))
    return (pooled.astype(jnp.bfloat16), rms_block, rms_pool, grads[0].astype(jnp.bfloat16), grads[1], grads[2], grads[3], grads[4], grads[5], grads[6], grads[7])
```

```python
import functools
import math
from types import SimpleNamespace

import jax
import jax.numpy as jnp
import numpy as np
from jax import lax
from jax.experimental import pallas as pl
from jax.experimental.pallas import tpu as pltpu
from jax.sharding import PartitionSpec as P

HEAD = 64
POOL = 3
EPS = 1e-06
BIG = float(2**30)
NEG = -1000000000.0
BLOCK = 256
LEFT = 3
F32, BF16 = jnp.float32, jnp.bfloat16
MESH = pl.DeviceIdType.MESH


def dot(a, b, ca=1, cb=0):
    return lax.dot_general(a, b, (((ca,), (cb,)), ((), ())), preferred_element_type=F32)


def part(ref, dim, start, count):
    index = [slice(None)] * len(ref.shape)
    index[dim] = pl.ds(start, count)
    return ref.at[tuple(index)]


def wide(ref, start, count):
    return jnp.concatenate([ref[i, pl.ds(start, count), :] for i in range(ref.shape[0])], axis=1)


def put_wide(ref, start, count, value, stride=None):
    for i in range(ref.shape[0]):
        ref[i, pl.ds(start, count, stride=stride), :] = value[:, i * 128 : (i + 1) * 128]


class Links:
    def __init__(self, send, recv):
        self.send, self.recv, self.sent = send, recv, []

    def copy(self, src, dst, to):
        k = len(self.sent)
        move = pltpu.make_async_remote_copy(
            src, dst, self.send.at[k], self.recv.at[k], device_id=to, device_id_type=MESH
        )
        move.start()
        self.sent.append([move, False])
        return k

    def arrived(self, k):
        self.sent[k][0].wait_recv()

    def left(self, k):
        if not self.sent[k][1]:
            self.sent[k][0].wait_send()
            self.sent[k][1] = True

    def finish(self):
        for k in range(len(self.sent)):
            self.left(k)


class Loads:
    def __init__(self, sems):
        self.sems, self.moves = sems, []

    def copy(self, src, dst):
        move = pltpu.make_async_copy(src, dst, self.sems.at[len(self.moves)])
        move.start()
        self.moves.append([move, False])
        return len(self.moves) - 1

    def wait(self, *ks):
        for k in ks:
            if not self.moves[k][1]:
                self.moves[k][0].wait()
                self.moves[k][1] = True

    def finish(self):
        self.wait(*range(len(self.moves)))


def step(*gens):
    for gen in gens:
        next(gen, None)


def drain(*gens):
    live = list(gens)
    while live:
        live = [gen for gen in live if next(gen, "end") != "end"]


def gathered(links, shard, buf, dim, size, xbit, to_y, to_x, to_core):
    half = size // 2
    start = pl.multiple_of(xbit * half, 16)
    by_y = links.copy(part(shard, dim, start, half), part(buf.at[1], dim, start, half), to_y)
    if to_core is not None:
        own = links.copy(shard, buf.at[2], to_core)
    yield 1
    links.arrived(by_y)
    by_x = links.copy(part(buf.at[1], dim, start, half), part(buf.at[1], dim, start, half), to_x)
    yield 1
    links.arrived(by_x)
    if to_core is not None:
        other = links.copy(buf.at[1], buf.at[3], to_core)
        yield 1
        links.arrived(own)
        links.arrived(other)


def reduced(links, loads, acc, dim, size, halves, swaps, bufs, out):
    lo, n, spans = 0, size, []
    bufs = iter(bufs)
    for to, bit in halves:
        half = n // 2
        buf = next(bufs)
        there = pl.multiple_of(lo + (1 - bit) * half, 16)
        here = pl.multiple_of(lo + bit * half, 16)
        k = links.copy(part(acc, dim, there, half), buf, to)
        yield 1
        links.arrived(k)
        mine = part(acc, dim, here, half)
        mine[...] = mine[...] + buf[...]
        spans.append((to, lo))
        lo, n = here, half
    mine = part(acc, dim, lo, n)
    for to in swaps:
        buf = next(bufs)
        k = links.copy(mine, buf, to)
        yield 1
        links.arrived(k)
        links.left(k)
        mine[...] = mine[...] + buf[...]
    own = loads.copy(mine, part(out, dim, lo, n))
    src = mine
    for to, before in reversed(spans):
        k = links.copy(src, part(out, dim, lo, n), to)
        yield 1
        links.arrived(k)
        loads.wait(own)
        lo, n = before, 2 * n
        src = part(out, dim, lo, n)


def from_y(links, other, buf, own, to_y, rest):
    k = links.copy(other, buf, to_y)
    yield 1
    links.arrived(k)
    own[...] = own[...] + buf[...]
    yield from rest()


def summed(links, terms, bufs, partners):
    for i, to in enumerate(partners):
        k = links.copy(terms.at[i], bufs.at[i], to)
        yield 1
        links.arrived(k)
        terms[i + 1] = terms[i] + bufs[i]


def scratch_list(T, D, HC, U, bits):
    L, heads, qb = 2 * T, 2 * HC // HEAD, 2 * T // BLOCK
    blocks = sum(min(i, LEFT) + 1 for i in range(qb))
    kd = POOL * D
    halves, swaps = min(bits, 2), max(bits - 2, 0)

    def stages(rows, count):
        return [rows >> (i + 1) for i in range(count)]

    out = [
        ("xb", (T, D), BF16),
        ("nrm", (L, D), BF16),
        ("wq", (2, 3, D, HC), BF16),
        ("wqt", (6 * HC, D), BF16),
        ("wo", (4, HC, D), BF16),
        ("wu", (4, D, U), BF16),
        ("wd", (4, U, D), BF16),
        ("wp", (kd, D), BF16),
        ("pg", (T // POOL, D), BF16),
        ("cos", (HEAD // 2, L), F32),
        ("sin", (HEAD // 2, L), F32),
        ("qxt", (heads, 2 * HEAD, L), BF16),
        ("kt", (heads, HEAD, L), BF16),
        ("vt", (heads, HEAD, L), BF16),
        ("kx", (heads, L, 2 * HEAD), BF16),
        ("vx", (heads, L, 2 * HEAD), BF16),
        ("probs", (heads, blocks * BLOCK, BLOCK), BF16),
        ("rl", (heads, 8, L), F32),
        ("ot", (2 * HC, L), BF16),
        ("otf", (4 * HC, T), BF16),
        ("gox", (heads, 2 * HEAD, L), BF16),
        ("gpt", (6 * HC, L), BF16),
        ("h1", (T, D), F32),
        ("h2", (D // 128, T + 8, 128), F32),
        ("g2t", (D // 128, T + 8, 128), F32),
        ("rim", (D // 128, 8, 128), F32),
        ("n2", (T, D), BF16),
        ("act", (T, U), BF16),
        ("gpre", (T, U), BF16),
        ("gn", (T, D), F32),
        ("gatt", (L, D), BF16),
        ("pns", (T, D), BF16),
        ("pnr", (T, D), BF16),
        ("dk", (2, HEAD, L), F32),
        ("dv", (2, HEAD, L), F32),
        ("dq", (2, HEAD, L), F32),
        ("pool_in", (T // POOL, kd), BF16),
        ("pool_b", (T // POOL, D), BF16),
        ("gtok", (T, D), BF16),
        ("gd", (4, U, D), BF16),
        ("gu", (4, D, U), BF16),
        ("gq", (2, 3, D, HC), BF16),
        ("go", (2, HC, D), BF16),
        ("gp", (kd, D), BF16),
        ("cd", (2, U, D), BF16),
        ("cu", (2, D, U), BF16),
        ("yd", (U, D), BF16),
        ("yu", (D, U), BF16),
        ("yq", (3, D, HC), BF16),
        ("yo", (HC, D), BF16),
        ("terms", (bits + 3, 8, D), F32),
        ("term_in", (bits + 2, 8, D), F32),
    ]
    for name, rows, shape in (
        ("rd", U, lambda n: (n, D)),
        ("ru", D, lambda n: (n, U)),
        ("rq", D, lambda n: (3, n, HC)),
        ("ro", HC, lambda n: (n, D)),
    ):
        sizes = stages(rows, halves)
        sizes += [sizes[-1]] * swaps
        out += [(f"{name}{i}", shape(n), BF16) for i, n in enumerate(sizes)]
    sizes = stages(kd, 2 + halves)
    sizes += [sizes[-1]] * swaps
    out += [(f"rp{i}", (n, D), BF16) for i, n in enumerate(sizes)]
    return out


def kernel(bits, names, *refs):
    s = SimpleNamespace(**dict(zip(names, refs)))
    T, D = s.xb.shape
    HC, U = s.wo.shape[1], s.wu.shape[2]
    L, QB = 2 * T, 2 * T // BLOCK
    half_head = HEAD // 2
    RC = 64
    links, loads = Links(s.send_sems, s.recv_sems), Loads(s.load_sems)

    d, t = lax.axis_index("dp"), lax.axis_index("tensor")
    c, y = t % 2, t // 2
    to_core, to_y = (d, t + 1 - 2 * c), (d, t + 2 - 4 * y)
    bit = [(d // (1 << i)) % 2 for i in range(bits)]
    to_bit = [(d + (1 - 2 * bit[i]) * (1 << i), t) for i in range(bits)]
    halves = [(to_bit[i], bit[i]) for i in range(min(bits, 2))]
    swaps = to_bit[2:]
    mine = pl.multiple_of(c * T, T)
    theirs = pl.multiple_of((1 - c) * T, T)

    in_x = loads.copy(s.tokens, s.xb)
    in_q = loads.copy(s.w_qkv, s.wq.at[0])
    in_pool = loads.copy(s.w_pool, s.wp)
    in_pg = loads.copy(s.pooled_grad, s.pg)
    in_cos, in_sin = loads.copy(s.cos_in, s.cos), loads.copy(s.sin_in, s.sin)
    in_out = loads.copy(s.w_out, s.wo.at[0])
    in_up = loads.copy(s.w_up, s.wu.at[0])
    in_down = loads.copy(s.w_down, s.wd.at[0])

    partners = [to_core, to_y] + to_bit
    barrier = pltpu.get_barrier_semaphore()
    for to in partners:
        pl.semaphore_signal(barrier, inc=1, device_id=to, device_id_type=MESH)
    pl.semaphore_wait(barrier, len(partners))

    get_q = gathered(links, s.w_qkv, s.wq, 1, D, bit[0], to_y, to_bit[0], None)
    step(get_q)

    gain_one, gain_two = s.gain_one[...], s.gain_two[...]
    loads.wait(in_x)
    for r in range(0, T, RC):
        x = s.xb[r : r + RC, :].astype(F32)
        scale = lax.rsqrt(jnp.mean(x * x, axis=1, keepdims=True) + EPS)
        s.nrm[pl.ds(pl.multiple_of(mine + r, RC), RC), :] = (x * scale * gain_one).astype(BF16)
    own_rows = s.nrm.at[pl.ds(mine, T), :]
    sent_norm = links.copy(own_rows, own_rows, to_core)

    starts, ends, total = [], [], 0
    for j in range(4):
        starts.append(total)
        total = total + s.lengths[y, j]
        ends.append(total)

    def kept(j):
        p = mine + POOL * lax.broadcasted_iota(jnp.int32, (T // POOL, 1), 0) + j
        bad = (p - 1) <= 0
        for e in ends[:3]:
            bad = bad | ((p >= e) & (p - 1 <= e))
        return jnp.logical_not(bad)

    loads.wait(in_pool, in_pg)
    s.g2t[:, 0:8, :] = jnp.zeros((D // 128, 8, 128), F32)
    s.g2t[:, T : T + 8, :] = jnp.zeros((D // 128, 8, 128), F32)
    for j in range(POOL):
        grad_shift = dot(s.pg[...], s.wp[j * D : (j + 1) * D, :], 1, 1)
        put_wide(s.g2t, 8 - (POOL - 1) + j, T // POOL, jnp.where(kept(j), grad_shift, 0.0), POOL)
    sent_rim = links.copy(s.g2t.at[:, 0:8, :], s.rim, to_core)

    loads.wait(in_q, in_cos, in_sin)
    row = lax.broadcasted_iota(jnp.int32, (HEAD, L), 0)
    pos = lax.broadcasted_iota(jnp.int32, (HEAD, L), 1)
    same = jnp.zeros((HEAD, L), F32)
    for j in range(4):
        same = jnp.where((row == j) & (pos >= starts[j]) & (pos < ends[j]), 1.0, same)
    key_rows_doc = same.astype(BF16)
    query_rows_doc = jnp.where(row < 4, BIG * (same - 1.0), 0.0).astype(BF16)
    value_rows = jnp.where(row < 2, -1.0, 0.0).astype(BF16)
    for h in range(4):
        s.qxt[h, HEAD : 2 * HEAD, :] = query_rows_doc

    def turn_weights(slot):
        for i in range(3):
            s.wqt[(3 * slot + i) * HC : (3 * slot + i + 1) * HC, :] = s.wq[slot, i].T

    def project(slot, start):
        cols = pl.ds(start, T)
        cosine, sine = s.cos[:, cols], s.sin[:, cols]
        rows = s.nrm[cols, :]
        for i in range(3):
            r = dot(s.wqt[(3 * slot + i) * HC : (3 * slot + i + 1) * HC, :], rows, 1, 1)
            for h in range(2):
                u = r[h * HEAD : (h + 1) * HEAD, :]
                head = 2 * slot + h
                if i == 2:
                    s.vt[head, :, cols] = u.astype(BF16)
                    continue
                a, b = u[:half_head], u[half_head:]
                turned = jnp.concatenate([a * cosine - b * sine, a * sine + b * cosine], axis=0)
                if i == 0:
                    s.qxt[head, 0:HEAD, cols] = (turned * HEAD**-0.5).astype(BF16)
                else:
                    s.kt[head, :, cols] = turned.astype(BF16)

    def turn_keys(head):
        s.kx[head] = jnp.concatenate([s.kt[head], key_rows_doc], axis=0).T
        s.vx[head] = jnp.concatenate([s.vt[head], value_rows], axis=0).T

    turn_weights(0)
    project(0, mine)
    links.arrived(sent_norm)
    project(0, theirs)
    turn_keys(0)
    turn_keys(1)
    step(get_q)

    def fwd(head, qb):
        k0 = max(0, qb - LEFT)
        n = qb - k0 + 1
        off = sum(min(i, LEFT) + 1 for i in range(qb)) * BLOCK
        q = slice(qb * BLOCK, (qb + 1) * BLOCK)
        k = slice(k0 * BLOCK, (qb + 1) * BLOCK)
        scores = dot(s.kx[head, k, :], s.qxt[head, :, q])
        ki = lax.broadcasted_iota(jnp.int32, (BLOCK, BLOCK), 0)
        qi = lax.broadcasted_iota(jnp.int32, (BLOCK, BLOCK), 1)
        last = jnp.where(ki <= qi, scores[(n - 1) * BLOCK :], NEG)
        scores = last if n == 1 else jnp.concatenate([scores[: (n - 1) * BLOCK], last], axis=0)
        e = jnp.exp(scores - jnp.max(scores, axis=0, keepdims=True))
        inverse = 1.0 / jnp.sum(e, axis=0, keepdims=True)
        low = e.astype(BF16)
        s.probs[head, off : off + n * BLOCK, :] = low
        s.rl[head, 0:1, q] = inverse
        s.ot[pl.ds(pl.multiple_of(head * HEAD, HEAD), HEAD), q] = (dot(s.vt[head, :, k], low) * inverse).astype(BF16)

    def fwd_slot(slot):
        def one(h, _):
            for qb in range(QB):
                fwd(2 * slot + h, qb)
            return 0

        lax.fori_loop(0, 2, one, 0)

    def send_heads(slot):
        rows = slice(slot * HC, (slot + 1) * HC)
        s.otf[rows, :] = s.ot[rows, pl.ds(mine, T)]
        return links.copy(
            s.ot.at[rows, pl.ds(theirs, T)],
            s.otf.at[(2 + slot) * HC : (3 + slot) * HC, :],
            to_core,
        )

    fwd_slot(0)
    step(get_q)
    get_out = gathered(links, s.w_out, s.wo, 0, HC, bit[0], to_y, to_bit[0], to_core)
    get_up = gathered(links, s.w_up, s.wu, 0, D, bit[0], to_y, to_bit[0], to_core)
    get_down = gathered(links, s.w_down, s.wd, 0, U, bit[0], to_y, to_bit[0], to_core)
    step(get_out, get_up, get_down)
    turn_weights(1)
    project(1, mine)
    project(1, theirs)
    turn_keys(2)
    turn_keys(3)
    sent_heads = [send_heads(0)]
    step(get_out)
    step(get_out, get_up)
    fwd_slot(1)
    sent_heads.append(send_heads(1))
    step(get_up, get_down)
    drain(get_out)
    loads.wait(in_out)
    for k in sent_heads:
        links.arrived(k)

    wo = s.wo[...].reshape(4 * HC, D)
    s.h1[...] = dot(s.otf[...], wo, 0, 0)
    for r in range(0, T, RC):
        rows = slice(r, r + RC)
        h = s.h1[rows, :] + s.xb[rows, :].astype(F32)
        s.h1[rows, :] = h
        put_wide(s.h2, 8 + r, RC, h)
        scale = lax.rsqrt(jnp.mean(h * h, axis=1, keepdims=True) + EPS)
        s.n2[rows, :] = (h * scale * gain_two).astype(BF16)
    links.arrived(sent_rim)
    tail = lax.broadcasted_iota(jnp.int32, (D // 128, 8, 128), 1) >= 8 - (POOL - 1)
    s.g2t[:, T : T + 8, :] = s.g2t[:, T : T + 8, :] + jnp.where(tail, s.rim[...], 0.0)
    drain(get_up, get_down)
    loads.wait(in_up, in_down)

    root = math.sqrt(2.0 / math.pi)

    def feed_forward(slot, first):
        for r in range(0, T, BLOCK):
            rows = slice(r, r + BLOCK)
            v = dot(s.n2[rows, :], s.wu[slot])
            square = v * v
            th = jnp.tanh(root * v * (1.0 + 0.044715 * square))
            up = 0.5 * (1.0 + th)
            act = (v * up).astype(BF16)
            slope = up + 0.5 * v * (1.0 - th * th) * (root * (1.0 + 3 * 0.044715 * square))
            grad_act = dot(wide(s.g2t, 8 + r, BLOCK).astype(BF16), s.wd[slot], 1, 1)
            gpre = (grad_act * slope).astype(BF16)
            s.act[rows, :] = act
            s.gpre[rows, :] = gpre
            put_wide(s.h2, 8 + r, BLOCK, wide(s.h2, 8 + r, BLOCK) + dot(act, s.wd[slot]))
            grad_normed = dot(gpre, s.wu[slot], 1, 1)
            s.gn[rows, :] = grad_normed if first else s.gn[rows, :] + grad_normed
        s.gd[slot] = dot(s.act[...], wide(s.g2t, 8, T).astype(BF16), 0, 0).astype(BF16)
        s.gu[slot] = dot(s.n2[...], s.gpre[...], 0, 0).astype(BF16)

    def to_other_core(slot):
        return (
            links.copy(s.gd.at[slot], s.cd.at[slot - 2], to_core),
            links.copy(s.gu.at[slot], s.cu.at[slot - 2], to_core),
        )

    def from_other_core(slot, sent):
        links.arrived(sent[0])
        s.gd[slot] = s.gd[slot] + s.cd[slot]
        links.arrived(sent[1])
        s.gu[slot] = s.gu[slot] + s.cu[slot]

    def shard_sum(name, acc, dim, size, out):
        bufs = [getattr(s, f"{name}{i}") for i in range(bits)]
        return lambda: reduced(links, loads, acc, dim, size, halves, swaps, bufs, out)

    feed_forward(3, True)
    sent3 = to_other_core(3)
    feed_forward(1, False)
    from_other_core(1, sent3)
    sum_d = from_y(links, s.gd.at[1], s.yd, s.gd.at[0], to_y, shard_sum("rd", s.gd.at[0], 0, U, s.gd_out))
    sum_u = from_y(links, s.gu.at[1], s.yu, s.gu.at[0], to_y, shard_sum("ru", s.gu.at[0], 0, D, s.gu_out))
    step(sum_d, sum_u)
    feed_forward(2, False)
    sent2 = to_other_core(2)
    feed_forward(0, False)

    gain_grad_two = jnp.zeros((8, D), F32)
    for r in range(0, T, RC):
        rows = slice(r, r + RC)
        h, gn = s.h1[rows, :], s.gn[rows, :]
        scale = lax.rsqrt(jnp.mean(h * h, axis=1, keepdims=True) + EPS)
        e = gain_two * gn
        hs = h * scale
        grad = wide(s.g2t, 8 + r, RC) + scale * (e - hs * jnp.mean(e * hs, axis=1, keepdims=True))
        s.h1[rows, :] = grad
        s.gatt[pl.ds(pl.multiple_of(mine + r, RC), RC), :] = grad.astype(BF16)
        gain_grad_two = gain_grad_two + jnp.sum((gn * hs).reshape(RC // 8, 8, D), axis=0)
    own_rows = s.gatt.at[pl.ds(mine, T), :]
    sent_gatt = links.copy(own_rows, own_rows, to_core)
    sent_rim = links.copy(s.h2.at[:, T : T + 8, :], s.h2.at[:, 0:8, :], to_core)
    from_other_core(0, sent2)
    step(sum_d, sum_u)

    block_square = jnp.zeros((8, D), F32)
    for r in range(0, T, RC):
        h = wide(s.h2, 8 + r, RC)
        block_square = block_square + jnp.sum((h * h).reshape(RC // 8, 8, D), axis=0)
    links.arrived(sent_rim)
    for j in range(POOL):
        rows = pl.ds(8 - (POOL - 1) + j, T // POOL, stride=POOL)
        taken = jnp.concatenate([s.h2[i, rows, :] for i in range(D // 128)], axis=1)
        s.pool_in[:, j * D : (j + 1) * D] = jnp.where(kept(j), taken, 0.0).astype(BF16)
    pooled = dot(s.pool_in[...], s.wp[...])
    pool_square = jnp.sum((pooled * pooled).reshape(T // POOL // 8, 8, D), axis=0)
    s.pool_b[...] = pooled.astype(BF16)
    loads.copy(s.pool_b, s.pooled_out)
    for j in range(POOL):
        s.gp[j * D : (j + 1) * D, :] = dot(s.pool_in[:, j * D : (j + 1) * D], s.pg[...], 0, 0).astype(BF16)
    pool_halves = [(to_core, c), halves[0], (to_y, y)] + halves[1:]
    sum_p = reduced(
        links, loads, s.gp, 0, POOL * D, pool_halves, swaps,
        [getattr(s, f"rp{i}") for i in range(2 + bits)], s.gp_out,
    )
    step(sum_p)

    def grad_heads(start):
        cols = pl.ds(start, T)
        g = dot(s.wo[0:2].reshape(2 * HC, D), s.gatt[cols, :], 1, 1)
        line = lax.broadcasted_iota(jnp.int32, (HEAD, T), 0)
        for head in range(4):
            low = (g[head * HEAD : (head + 1) * HEAD] * s.rl[head, 0:1, cols]).astype(BF16)
            o = s.ot[head * HEAD : (head + 1) * HEAD, cols].astype(F32)
            delta = jnp.sum(low.astype(F32) * o, axis=0, keepdims=True)
            high = delta.astype(BF16).astype(F32)
            rest = jnp.where(line == 0, high, jnp.where(line == 1, delta - high, 0.0))
            s.gox[head, 0:HEAD, cols] = low
            s.gox[head, HEAD : 2 * HEAD, cols] = rest.astype(BF16)

    grad_heads(mine)
    links.arrived(sent_gatt)
    grad_heads(theirs)
    s.go[...] = dot(s.ot[...], s.gatt[...]).astype(BF16).reshape(2, HC, D)
    sum_o = from_y(links, s.go.at[1], s.yo, s.go.at[0], to_y, shard_sum("ro", s.go.at[0], 0, HC, s.go_out))
    step(sum_p, sum_o)

    def back(head, at, qb):
        k0 = max(0, qb - LEFT)
        n = qb - k0 + 1
        off = sum(min(i, LEFT) + 1 for i in range(qb)) * BLOCK
        q = slice(qb * BLOCK, (qb + 1) * BLOCK)
        k = slice(k0 * BLOCK, (qb + 1) * BLOCK)
        probs = s.probs[head, off : off + n * BLOCK, :]
        grad_scores = (probs.astype(F32) * dot(s.vx[head, k, :], s.gox[head, :, q])).astype(BF16)
        s.dq[at, :, q] = dot(s.kt[head, :, k], grad_scores)
        dk = dot(s.qxt[head, 0:HEAD, q], grad_scores, 1, 1)
        dv = dot(s.gox[head, 0:HEAD, q], probs, 1, 1)
        if n > 1:
            old = slice(k0 * BLOCK, qb * BLOCK)
            s.dk[at, :, old] = s.dk[at, :, old] + dk[:, : (n - 1) * BLOCK]
            s.dv[at, :, old] = s.dv[at, :, old] + dv[:, : (n - 1) * BLOCK]
        s.dk[at, :, q] = dk[:, (n - 1) * BLOCK :]
        s.dv[at, :, q] = dv[:, (n - 1) * BLOCK :]

    def back_head(slot, h):
        at = h
        for qb in range(QB):
            back(2 * slot + h, h, qb)
        cosine, sine = s.cos[...], s.sin[...]
        for i, (ref, factor) in enumerate(((s.dq, HEAD**-0.5), (s.dk, None))):
            a, b = ref[at, :half_head, :], ref[at, half_head:, :]
            turned = jnp.concatenate([a * cosine + b * sine, b * cosine - a * sine], axis=0)
            if factor is not None:
                turned = turned * factor
            s.gpt[pl.ds(pl.multiple_of((3 * slot + i) * HC + h * HEAD, HEAD), HEAD), :] = turned.astype(BF16)
        s.gpt[pl.ds(pl.multiple_of((3 * slot + 2) * HC + h * HEAD, HEAD), HEAD), :] = s.dv[at].astype(BF16)

    def back_slot(slot):
        def one(h, _):
            back_head(slot, h)
            return 0

        lax.fori_loop(0, 2, one, 0)

    def grad_weights(slot):
        for i in range(3):
            g = dot(s.gpt[(3 * slot + i) * HC : (3 * slot + i + 1) * HC, :], s.nrm[...])
            s.gq[slot, i] = g.astype(BF16).T

    back_slot(1)
    step(sum_d, sum_u, sum_p, sum_o)
    grad_weights(1)
    sum_q = from_y(links, s.gq.at[1], s.yq, s.gq.at[0], to_y, shard_sum("rq", s.gq.at[0], 1, D, s.gq_out))
    step(sum_q)
    back_slot(0)
    step(sum_d, sum_u, sum_p, sum_o)
    grad_weights(0)
    step(sum_q)

    s.pns[...] = dot(s.gpt[:, pl.ds(theirs, T)], s.wqt[...], 0, 0).astype(BF16)
    sent_pn = links.copy(s.pns, s.pnr, to_core)
    s.gn[...] = dot(s.gpt[:, pl.ds(mine, T)], s.wqt[...], 0, 0)
    step(sum_d, sum_u, sum_p, sum_o)
    links.arrived(sent_pn)
    gain_grad_one = jnp.zeros((8, D), F32)
    for r in range(0, T, RC):
        rows = slice(r, r + RC)
        x, gn = s.xb[rows, :].astype(F32), s.gn[rows, :] + s.pnr[rows, :].astype(F32)
        scale = lax.rsqrt(jnp.mean(x * x, axis=1, keepdims=True) + EPS)
        e = gain_one * gn
        xs = x * scale
        grad = s.h1[rows, :] + scale * (e - xs * jnp.mean(e * xs, axis=1, keepdims=True))
        s.gtok[rows, :] = grad.astype(BF16)
        gain_grad_one = gain_grad_one + jnp.sum((gn * xs).reshape(RC // 8, 8, D), axis=0)
    loads.copy(s.gtok, s.gtok_out)

    line = lax.broadcasted_iota(jnp.int32, (8, D), 0)
    small = jnp.zeros((8, D), F32)
    for i, v in enumerate((gain_grad_one, gain_grad_two, block_square, pool_square)):
        v = jnp.sum(v, axis=0, keepdims=True)
        if i >= 2:
            v = jnp.sum(v, axis=1, keepdims=True)
        small = jnp.where(line == i, v, small)
    s.terms[0] = small
    sum_s = summed(links, s.terms, s.term_in, partners)
    step(sum_s)
    drain(sum_q, sum_s, sum_d, sum_u, sum_p, sum_o)
    loads.copy(s.terms.at[len(partners)], s.small_out)
    links.finish()
    loads.finish()


IN_NAMES = (
    "tokens", "lengths", "w_qkv", "w_out", "w_up", "w_down", "w_pool",
    "gain_one", "gain_two", "pooled_grad", "cos_in", "sin_in",
)
OUT_NAMES = ("pooled_out", "gtok_out", "gq_out", "go_out", "gu_out", "gd_out", "gp_out", "small_out")


def tables(length):
    half = HEAD // 2
    frequency = np.exp(-math.log(10000.0) * np.arange(half) / half)
    angle = frequency[:, None] * np.arange(length)[None, :]
    return np.cos(angle).astype(np.float32), np.sin(angle).astype(np.float32)


def shards(tokens, lengths, w_qkv, w_out, w_up, w_down, w_pool, gain_one, gain_two, pooled_grad):
    T, D = tokens.shape
    HC, U = w_out.shape[0], w_up.shape[1]
    dp = lax.axis_size("dp")
    bits = dp.bit_length() - 1
    assert lax.axis_size("tensor") == 4 and lengths.shape == (2, 4) and dp == 1 << bits and bits > 0
    cos, sin = tables(2 * T)
    scratch = scratch_list(T, D, HC, U, bits)
    names = IN_NAMES + OUT_NAMES + tuple(n for n, _, _ in scratch) + ("send_sems", "recv_sems", "load_sems")
    hbm, vmem, smem = pl.BlockSpec(memory_space=pl.ANY), pl.BlockSpec(memory_space=pltpu.VMEM), pl.BlockSpec(memory_space=pltpu.SMEM)
    copies = 96 + 8 * bits
    outs = pl.pallas_call(
        functools.partial(kernel, bits, names),
        out_shape=[
            jax.ShapeDtypeStruct((T // POOL, D), BF16),
            jax.ShapeDtypeStruct((T, D), BF16),
            jax.ShapeDtypeStruct((3, D, HC), BF16),
            jax.ShapeDtypeStruct((HC, D), BF16),
            jax.ShapeDtypeStruct((D, U), BF16),
            jax.ShapeDtypeStruct((U, D), BF16),
            jax.ShapeDtypeStruct((POOL * D, D), BF16),
            jax.ShapeDtypeStruct((8, D), F32),
        ],
        in_specs=[hbm, smem, hbm, hbm, hbm, hbm, hbm, vmem, vmem, hbm, hbm, hbm],
        out_specs=[hbm] * 8,
        scratch_shapes=[pltpu.VMEM(shape, kind) for _, shape, kind in scratch]
        + [pltpu.SemaphoreType.DMA((copies,)), pltpu.SemaphoreType.DMA((copies,)), pltpu.SemaphoreType.DMA((32,))],
        compiler_params=pltpu.CompilerParams(
            collective_id=0, has_side_effects=True, vmem_limit_bytes=64 * 2**20 - 2**16
        ),
    )(
        tokens, lengths, jnp.transpose(w_qkv, (1, 0, 2)), w_out, w_up, w_down, w_pool,
        gain_one.reshape(1, D), gain_two.reshape(1, D), pooled_grad, cos, sin,
    )
    pooled, gtok, gq, go, gu, gd, gp, small = outs
    group = dp * 4 * T * D
    return (
        pooled,
        jnp.sqrt(small[2, 0] / group),
        jnp.sqrt(small[3, 0] / (group // POOL)),
        gtok,
        jnp.transpose(gq, (1, 0, 2)).astype(F32),
        go.astype(F32),
        gu.astype(F32),
        gd.astype(F32),
        gp.astype(F32),
        small[0],
        small[1],
    )


def solution(mesh):
    rows = P(("dp", "tensor"), None)
    placed = (
        rows, P("dp", None), P(None, None, "tensor"), P("tensor", None), P(None, "tensor"),
        P("tensor", None), P(), P(), P(), rows,
    )
    return jax.shard_map(
        shards,
        mesh=mesh,
        in_specs=placed,
        out_specs=(
            rows, P(), P(), rows, P(None, None, "tensor"), P("tensor", None), P(None, "tensor"),
            P("tensor", None), P(), P(), P(),
        ),
        check_vma=False,
    )
```

```python
import functools
import math
from types import SimpleNamespace

import jax
import jax.numpy as jnp
import numpy as np
from jax import lax
from jax.experimental import pallas as pl
from jax.experimental.pallas import tpu as pltpu
from jax.sharding import PartitionSpec as P

HEAD = 64
POOL = 3
EPS = 1e-06
BIG = float(2**30)
NEG = -1000000000.0
BLOCK = 256
LEFT = 3
WINDOW = LEFT + 1
CHUNK = 128
F32, BF16 = jnp.float32, jnp.bfloat16
MESH = pl.DeviceIdType.MESH


def dot(a, b, ca=1, cb=0):
    return lax.dot_general(a, b, (((ca,), (cb,)), ((), ())), preferred_element_type=F32)


def part(ref, dim, start, count):
    index = [slice(None)] * len(ref.shape)
    index[dim] = pl.ds(start, count)
    return ref.at[tuple(index)]


def wide(ref, start, count):
    return jnp.concatenate([ref[i, pl.ds(start, count), :] for i in range(ref.shape[0])], axis=1)


def put_wide(ref, start, count, value, stride=None):
    for i in range(ref.shape[0]):
        ref[i, pl.ds(start, count, stride=stride), :] = value[:, i * 128 : (i + 1) * 128]


class Links:
    def __init__(self, send, recv, free, partners):
        self.send, self.recv, self.sent, self.partners = send, recv, [], partners
        self.free, self.freed = free, 0

    def copy(self, src, dst, to):
        k = len(self.sent)
        move = pltpu.make_async_remote_copy(
            src, dst, self.send.at[k], self.recv.at[k], device_id=to, device_id_type=MESH
        )
        move.start()
        self.sent.append([move, False, False])
        return k

    def arrived(self, k):
        if not self.sent[k][2]:
            self.sent[k][0].wait_recv()
            self.sent[k][2] = True

    def left(self, k):
        if not self.sent[k][1]:
            self.sent[k][0].wait_send()
            self.sent[k][1] = True

    def give(self, to):
        self.freed += 1
        pl.semaphore_signal(self.free.at[self.freed - 1], inc=1, device_id=to, device_id_type=MESH)
        return self.freed - 1

    def granted(self, i):
        pl.semaphore_wait(self.free.at[i], 1)

    def finish(self):
        for k in range(len(self.sent)):
            self.left(k)


class Loads:
    def __init__(self, sems):
        self.sems, self.moves = sems, []

    def copy(self, src, dst):
        move = pltpu.make_async_copy(src, dst, self.sems.at[len(self.moves)])
        move.start()
        self.moves.append([move, False])
        return len(self.moves) - 1

    def wait(self, *ks):
        for k in ks:
            if not self.moves[k][1]:
                self.moves[k][0].wait()
                self.moves[k][1] = True

    def finish(self):
        self.wait(*range(len(self.moves)))


class Flow:
    def __init__(self):
        self.gens, self.waits, self.at = {}, {}, 0

    def step(self, name):
        self.waits[name] = next(self.gens[name], None)
        return self.waits[name] is not None

    def start(self, name, gen, held=False):
        self.gens[name] = gen
        self.step(name)

    def release(self, *names):
        pass

    def tick(self):
        for name in PLAN[self.at] if self.at < len(PLAN) else ():
            self.step(name)
        self.at += 1

    def need(self, *names):
        for name in names:
            while self.step(name):
                pass

    def finish(self):
        self.tick()
        live = list(self.gens)
        while live:
            live = [name for name in live if self.step(name)]


def gathered(links, way, shard, buf, dim, size, bit, to_y, to_bit, to_core, owns):
    def rows(ref, start, count):
        return part(ref, dim, pl.multiple_of(start, 16), count)

    near, own = buf.at[1], None
    if way == "y":
        k = links.copy(shard, near, to_y)
        yield (k,)
        if to_core is not None:
            own = links.copy(shard, buf.at[2], to_core)
            owns.append(own)
        links.arrived(k)
        ks = first = ()
    elif len(bit) == 1:
        half = size // 2
        k = links.copy(rows(shard, bit[0] * half, half), rows(near, bit[0] * half, half), to_y)
        yield (k,)
        if to_core is not None:
            own = links.copy(shard, buf.at[2], to_core)
            owns.append(own)
        links.arrived(k)
        piece = rows(near, bit[0] * half, half)
        ks, first = (links.copy(piece, piece, to_bit[0]),), ()
    else:
        quarter = size // 4
        at = (2 * bit[1] + bit[0]) * quarter
        over_x = (2 * bit[1] + 1 - bit[0]) * quarter
        over_z = (2 - 2 * bit[1] + bit[0]) * quarter
        k = links.copy(rows(shard, at, quarter), rows(near, at, quarter), to_y)
        yield (k,)
        if to_core is not None:
            own = links.copy(shard, buf.at[2], to_core)
            owns.append(own)
        links.arrived(k)
        piece = rows(near, at, quarter)
        by_x, by_z = first = links.copy(piece, piece, to_bit[0]), links.copy(piece, piece, to_bit[1])
        yield (by_x, by_z)
        links.arrived(by_x)
        piece = rows(near, over_x, quarter // 2)
        second = links.copy(piece, piece, to_bit[1])
        links.arrived(by_z)
        piece = rows(near, over_z + quarter // 2, quarter // 2)
        ks = (links.copy(piece, piece, to_bit[0]), second)
    if ks:
        yield ks
    for k in ks:
        links.arrived(k)
    if to_core is None:
        for k in ks + first:
            links.left(k)
        return
    k = links.copy(near, buf.at[3], to_core)
    yield (k, own)
    links.arrived(own)
    links.arrived(k)


def reduced(links, loads, acc, dim, base, size, stages, bufs, out, ahead):
    lo, n, spans = base, size, []
    two = any(kind == "slot" for kind, _, _ in stages)

    def rows(ref, start, count, slots=False):
        return part(ref, dim + 1 if slots else dim, start if isinstance(start, int) else pl.multiple_of(start, 16), count)

    for (kind, to, bit), buf in zip(stages, bufs):
        if kind == "slot":
            k = links.copy(rows(acc.at[1], lo, n), buf, to)
            acc, two = acc.at[0], False
            mine = rows(acc, lo, n)
        elif kind == "half":
            half = n // 2
            there, here = lo + (1 - bit) * half, lo + bit * half
            if two:
                early = links.copy(rows(acc.at[ahead], there, half), buf.at[ahead], to)
                yield (early,)
                k = links.copy(rows(acc.at[1 - ahead], there, half), buf.at[1 - ahead], to)
            else:
                k = links.copy(rows(acc, there, half), buf, to)
            before = lo
            lo, n = here, half
            mine = rows(acc, lo, n, two)
        else:
            mine = rows(acc, lo, n)
            k = links.copy(mine, buf, to)
        yield (k,)
        if kind == "half" and two:
            links.arrived(early)
            links.left(early)
        links.arrived(k)
        if kind != "slot":
            links.left(k)
        if kind == "half":
            spans.append((to, before, links.give(to)))
        mine[...] = mine[...] + buf[...]
    for to, before, credit in reversed(spans):
        mine = rows(acc, lo, n)
        links.granted(credit)
        k = links.copy(mine, mine, to)
        yield (k,)
        links.arrived(k)
        lo, n = before, 2 * n
    loads.copy(rows(acc, lo, n), rows(out, lo, n))


def summed(links, terms, bufs, partners):
    for i, to in enumerate(partners):
        k = links.copy(terms.at[i], bufs.at[i], to)
        yield (k,)
        links.arrived(k)
        terms[i + 1] = terms[i] + bufs[i]


ORDER = {
    "d0": ("0y1s", 0, 2),
    "d1": ("01ys", 1, 2),
    "u0": ("10ys", 0, 2),
    "u1": ("1y0s", 1, 2),
    "o": ("y01s", 0, 1),
    "q0": ("0y1s", 0, 2),
    "q1": ("10ys", 1, 2),
    "p0": ("c0Y1s", 0, 2),
    "p1": ("c10Ys", 1, 2),
}
WAY = {"wq": "yxz", "wo": "yxz", "wu": "yxz", "wd": "yxz"}
SLOTS = (2, 0, 3, 1)
PLAN = (
    (), (), (), (), ("wq",), ("wo",), (), (), (), (), (), (), ("wu",), (), ("wq",), (), ("wo", "wd", "wu",), (), (),
    (), (), ("wo",), (), (), ("wo",), (), (), ("wd",), (), (), (), ("wu",), ("wd",), ("wu",), ("wd",), (), (), (),
    (), (), (), (), (), (), (), (), (), (), (), (), (), (), ("d0", "u0",), ("d1", "u1",), ("p0", "d0", "u0",),
    ("p1",), (), (), (), (), ("d1", "u1",), (), (), ("o",), (), (), (), ("p0", "d0", "p1",), (), ("u0", "d1",),
    ("o", "u1",), (), (), (), ("p0",), (), ("d0",), ("p1", "d1",), ("o", "u0",), ("q1", "q0", "p0", "u1",),
    ("p1", "d1", "d0", "u0", "o", "q1", "q0",),
    ("s", "p0", "q1", "u1", "q0", "s", "q1", "d0", "p1", "o", "u1", "s", "q1", "p0", "d1", "q0", "p1", "d0", "u0",
     "o", "p0", "u1", "s", "q1", "p1", "q0", "u0", "d1", "s", "p0", "q1", "p1", "p0", "q0", "p1", "d1", "u0", "q0",
     "q1",),
)


def stage_kinds(order, bits):
    kinds = []
    for letter in order:
        if letter == "y":
            kinds.append(("slot", 1))
        elif letter in "cY":
            kinds.append(("half", "cY".index(letter)))
        elif letter in "01":
            kinds += [("half", 2 + int(letter))] if int(letter) < bits else []
        else:
            kinds += [("swap", 2 + i) for i in range(2, bits)]
    return kinds


def buffer_shapes(order, rows, shape, bits):
    kinds, out = stage_kinds(order, bits), []
    two = any(kind == "slot" for kind, _ in kinds)
    for kind, _ in kinds:
        if kind == "slot":
            two = False
        elif kind == "half":
            rows //= 2
        out.append(((2,) if two else ()) + shape(rows))
    return out


def scratch_list(T, D, HC, U, bits):
    L, heads, qb = 2 * T, 2 * HC // HEAD, 2 * T // BLOCK
    blocks = sum(min(i, LEFT) + 1 for i in range(qb))
    kd = POOL * D
    out = [
        ("xb", (T, D), BF16),
        ("nrm", (L, D), BF16),
        ("wq", (2, 3, D, HC), BF16),
        ("wqt", (6 * HC, D), BF16),
        ("wo", (4, HC, D), BF16),
        ("wu", (4, D, U), BF16),
        ("wd", (4, U, D), BF16),
        ("wp", (kd, D), BF16),
        ("pg", (T // POOL, D), BF16),
        ("cos", (HEAD // 2, L), F32),
        ("sin", (HEAD // 2, L), F32),
        ("qxt", (heads, 2 * HEAD, L), BF16),
        ("kt", (heads, HEAD, L), BF16),
        ("vt", (heads, HEAD, L), BF16),
        ("kx", (heads, L, 2 * HEAD), BF16),
        ("vx", (heads, L, 2 * HEAD), BF16),
        ("probs", (heads, blocks * BLOCK, BLOCK), BF16),
        ("rl", (8, L), F32),
        ("ot", (2 * HC, L), BF16),
        ("otf", (4 * HC, T), BF16),
        ("gox", (heads, 2 * HEAD, L), BF16),
        ("gpt", (6 * HC, L), BF16),
        ("h1", (T, D), F32),
        ("h2", (D // 128, T + 8, 128), F32),
        ("g2t", (D // 128, T + 8, 128), F32),
        ("rim", (D // 128, 8, 128), F32),
        ("n2", (T, D), BF16),
        ("act", (T, U), BF16),
        ("gpre", (T, U), BF16),
        ("gn", (T, D), F32),
        ("gatt", (L, D), BF16),
        ("dk", (HEAD, L), F32),
        ("dv", (HEAD, L), F32),
        ("dq", (HEAD, L), F32),
        ("gd", (4, U, D), BF16),
        ("gu", (4, D, U), BF16),
        ("go", (2, HC, D), BF16),
        ("cd", (2, U, D), BF16),
        ("cu", (2, D, U), BF16),
        ("sc0", (WINDOW * BLOCK, BLOCK), F32),
        ("sc1", (WINDOW * BLOCK, BLOCK), F32),
        ("ds0", (WINDOW * BLOCK, BLOCK), BF16),
        ("ds1", (WINDOW * BLOCK, BLOCK), BF16),
        ("terms", (bits + 3, 8, D), F32),
        ("term_in", (bits + 2, 8, D), F32),
    ]
    rows_of = {"d": U, "u": D, "o": HC, "q": D, "p": kd}
    shape_of = {
        "d": lambda n: (n, D),
        "u": lambda n: (n, U),
        "o": lambda n: (n, D),
        "q": lambda n: (3, n, HC),
        "p": lambda n: (n, D),
    }
    for name, (order, _, parts) in ORDER.items():
        shapes = buffer_shapes(order, rows_of[name[0]] // parts, shape_of[name[0]], bits)
        out += [(f"in_{name}_{i}", shape, BF16) for i, shape in enumerate(shapes)]
    return out


def kernel(bits, names, *refs):
    s = SimpleNamespace(**dict(zip(names, refs)))
    T, D = s.xb.shape
    HC, U = s.wo.shape[1], s.wu.shape[2]
    L, QB = 2 * T, 2 * T // BLOCK
    half_head = HEAD // 2
    RC = 32
    loads = Loads(s.load_sems)

    d, t = lax.axis_index("dp"), lax.axis_index("tensor")
    c, y = t % 2, t // 2
    to_core, to_y = (d, t + 1 - 2 * c), (d, t + 2 - 4 * y)
    bit = [(d // (1 << i)) % 2 for i in range(bits)]
    to_bit = [(d + (1 - 2 * bit[i]) * (1 << i), t) for i in range(bits)]
    partners = [to_core, to_y] + to_bit
    links, flow = Links(s.send_sems, s.recv_sems, s.free_sems, partners), Flow()
    sides = [c, y] + bit
    tick = flow.tick

    def start_sum(name, acc, dim, out, held=False, ahead=1):
        order, piece, parts = ORDER[name]
        size = {"d": U, "u": D, "o": HC, "q": D, "p": POOL * D}[name[0]] // parts
        stages = [(kind, partners[i], sides[i]) for kind, i in stage_kinds(order, bits)]
        bufs = [getattr(s, f"in_{name}_{i}") for i in range(len(stages))]
        flow.start(name, reduced(links, loads, acc, dim, piece * size, size, stages, bufs, out, ahead), held)

    mine = pl.multiple_of(c * T, T)
    theirs = pl.multiple_of((1 - c) * T, T)

    in_x = loads.copy(s.tokens, s.xb)
    in_q = loads.copy(s.w_qkv, s.wq.at[0])
    in_pool = loads.copy(s.w_pool, s.wp)
    in_pg = loads.copy(s.pooled_grad, s.pg)
    in_cos, in_sin = loads.copy(s.cos_in, s.cos), loads.copy(s.sin_in, s.sin)
    in_out = loads.copy(s.w_out, s.wo.at[0])
    in_up = loads.copy(s.w_up, s.wu.at[0])
    in_down = loads.copy(s.w_down, s.wd.at[0])

    barrier = pltpu.get_barrier_semaphore()
    for to in partners:
        pl.semaphore_signal(barrier, inc=1, device_id=to, device_id_type=MESH)
    pl.semaphore_wait(barrier, len(partners))

    owns = {"wq": [], "wo": [], "wu": [], "wd": []}

    def get(name, shard, buf, dim, size, core):
        flow.start(name, gathered(links, WAY[name], shard, buf, dim, size, bit, to_y, to_bit, core, owns[name]))

    get("wq", s.w_qkv, s.wq, 1, D, None)
    get("wo", s.w_out, s.wo, 0, HC, to_core)
    get("wu", s.w_up, s.wu, 0, D, to_core)
    get("wd", s.w_down, s.wd, 0, U, to_core)

    gain_one, gain_two = s.gain_one[...], s.gain_two[...]
    loads.wait(in_x)
    for r in range(0, T, RC):
        x = s.xb[r : r + RC, :].astype(F32)
        scale = lax.rsqrt(jnp.mean(x * x, axis=1, keepdims=True) + EPS)
        s.nrm[pl.ds(pl.multiple_of(mine + r, RC), RC), :] = (x * scale * gain_one).astype(BF16)
    own_rows = s.nrm.at[pl.ds(mine, T), :]
    sent_norm = links.copy(own_rows, own_rows, to_core)

    starts, ends, total = [], [], 0
    for j in range(4):
        starts.append(total)
        total = total + s.lengths[y, j]
        ends.append(total)

    def kept(j):
        p = mine + POOL * lax.broadcasted_iota(jnp.int32, (T // POOL, 1), 0) + j
        bad = (p - 1) <= 0
        for e in ends[:3]:
            bad = bad | ((p >= e) & (p - 1 <= e))
        return jnp.logical_not(bad)

    loads.wait(in_q, in_cos, in_sin)
    row = lax.broadcasted_iota(jnp.int32, (HEAD, L), 0)
    pos = lax.broadcasted_iota(jnp.int32, (HEAD, L), 1)
    same = jnp.zeros((HEAD, L), F32)
    for j in range(4):
        same = jnp.where((row == j) & (pos >= starts[j]) & (pos < ends[j]), 1.0, same)
    key_rows_doc = same.astype(BF16)
    query_rows_doc = jnp.where(row < 4, BIG * (same - 1.0), 0.0).astype(BF16)
    value_rows = jnp.where(row < 2, -1.0, 0.0).astype(BF16)
    for h in range(4):
        s.qxt[h, HEAD : 2 * HEAD, :] = query_rows_doc

    def turn_weights(slot):
        for i in range(3):
            s.wqt[(3 * slot + i) * HC : (3 * slot + i + 1) * HC, :] = s.wq[slot, i].T

    def project(slot, start):
        for j in range(0, T, BLOCK):
            cols = pl.ds(pl.multiple_of(start + j, BLOCK), BLOCK)
            cosine, sine = s.cos[:, cols], s.sin[:, cols]
            r = dot(s.wqt[3 * slot * HC : 3 * (slot + 1) * HC, :], s.nrm[cols, :], 1, 1)
            for i in range(3):
                for h in range(2):
                    u = r[i * HC + h * HEAD : i * HC + (h + 1) * HEAD, :]
                    head = 2 * slot + h
                    if i == 2:
                        s.vt[head, :, cols] = u.astype(BF16)
                        continue
                    a, b = u[:half_head], u[half_head:]
                    turned = jnp.concatenate([a * cosine - b * sine, a * sine + b * cosine], axis=0)
                    if i == 0:
                        s.qxt[head, 0:HEAD, cols] = (turned * HEAD**-0.5).astype(BF16)
                    else:
                        s.kt[head, :, cols] = turned.astype(BF16)

    def turn_keys(head):
        s.kx[head] = jnp.concatenate([s.kt[head], key_rows_doc], axis=0).T
        s.vx[head] = jnp.concatenate([s.vt[head], value_rows], axis=0).T

    turn_weights(0)
    project(0, mine)
    tick()

    loads.wait(in_pool, in_pg)
    s.g2t[:, 0:8, :] = jnp.zeros((D // 128, 8, 128), F32)
    s.g2t[:, T : T + 8, :] = jnp.zeros((D // 128, 8, 128), F32)
    for j in range(POOL):
        grad_shift = dot(s.pg[...], s.wp[j * D : (j + 1) * D, :], 1, 1)
        put_wide(s.g2t, 8 - (POOL - 1) + j, T // POOL, jnp.where(kept(j), grad_shift, 0.0), POOL)
    sent_rim = links.copy(s.g2t.at[:, 0:8, :], s.rim, to_core)

    tick()
    links.arrived(sent_norm)
    project(0, theirs)
    tick()
    turn_keys(0)
    turn_keys(1)
    tick()

    def window(qb):
        first = max(0, qb - LEFT)
        blocks = qb - first + 1
        offset = sum(min(i, LEFT) + 1 for i in range(qb)) * BLOCK
        return first * BLOCK, blocks, offset, slice(qb * BLOCK, (qb + 1) * BLOCK)

    def score(head, qb, i, into):
        first, blocks, _, q = window(qb)
        rows = slice(i * CHUNK, (i + 1) * CHUNK)
        scores = dot(s.kx[head, first + rows.start : first + rows.stop, :], s.qxt[head, :, q])
        below = rows.start - (blocks - 1) * BLOCK
        if below >= 0:
            ki = lax.broadcasted_iota(jnp.int32, (CHUNK, BLOCK), 0) + below
            qi = lax.broadcasted_iota(jnp.int32, (CHUNK, BLOCK), 1)
            scores = jnp.where(ki <= qi, scores, NEG)
        into[rows, :] = scores
        return jnp.max(scores.reshape(CHUNK // 8, 8, BLOCK), axis=0)

    def attend(head):
        order = list(range(1, QB)) + [0]
        pieces = [window(qb)[1] * BLOCK // CHUNK for qb in order]
        bufs = (s.sc0, s.sc1)
        tops = [score(head, order[0], i, bufs[0]) for i in range(pieces[0])]
        for at, qb in enumerate(order):
            first, blocks, offset, q = window(qb)
            now, later = bufs[at % 2], bufs[(at + 1) % 2]
            top = jnp.max(functools.reduce(jnp.maximum, tops), axis=0, keepdims=True)
            more = pieces[at + 1] if at + 1 < QB else 0
            tops, total = [], jnp.zeros((8, BLOCK), F32)
            for i in range(pieces[at]):
                while len(tops) < (i + 1) * more // pieces[at]:
                    tops.append(score(head, order[at + 1], len(tops), later))
                e = jnp.exp(now[i * CHUNK : (i + 1) * CHUNK, :] - top)
                total = total + jnp.sum(e.reshape(CHUNK // 8, 8, BLOCK), axis=0)
                s.probs[head, offset + i * CHUNK : offset + (i + 1) * CHUNK, :] = e.astype(BF16)
            inverse = 1.0 / jnp.sum(total, axis=0, keepdims=True)
            s.rl[head : head + 1, q] = inverse
            low = s.probs[head, offset : offset + blocks * BLOCK, :]
            out = dot(s.vt[head, :, first : first + blocks * BLOCK], low) * inverse
            s.ot[head * HEAD : (head + 1) * HEAD, q] = out.astype(BF16)
            tick()

    def send_heads(slot):
        rows = slice(slot * HC, (slot + 1) * HC)
        s.otf[rows, :] = s.ot[rows, pl.ds(mine, T)]
        return links.copy(
            s.ot.at[rows, pl.ds(theirs, T)],
            s.otf.at[(2 + slot) * HC : (3 + slot) * HC, :],
            to_core,
        )

    attend(0)
    attend(1)
    sent_heads = [send_heads(0)]
    flow.need("wq")
    turn_weights(1)
    project(1, mine)
    tick()
    project(1, theirs)
    turn_keys(2)
    turn_keys(3)
    tick()
    attend(2)
    attend(3)
    sent_heads.append(send_heads(1))
    tick()
    flow.need("wo")
    loads.wait(in_out)
    for k in sent_heads:
        links.arrived(k)

    for j in range(0, T, BLOCK):
        out = dot(s.otf[:, j : j + BLOCK], s.wo[...].reshape(4 * HC, D), 0, 0)
        for r in range(j, j + BLOCK, RC):
            rows = slice(r, r + RC)
            h = out[r - j : r - j + RC, :] + s.xb[rows, :].astype(F32)
            s.h1[rows, :] = h
            put_wide(s.h2, 8 + r, RC, h)
            scale = lax.rsqrt(jnp.mean(h * h, axis=1, keepdims=True) + EPS)
            s.n2[rows, :] = (h * scale * gain_two).astype(BF16)
    links.arrived(sent_rim)
    tail = lax.broadcasted_iota(jnp.int32, (D // 128, 8, 128), 1) >= 8 - (POOL - 1)
    s.g2t[:, T : T + 8, :] = s.g2t[:, T : T + 8, :] + jnp.where(tail, s.rim[...], 0.0)
    for r in range(0, T, RC):
        branch = wide(s.g2t, 8 + r, RC).astype(BF16)
        s.gatt[pl.ds(pl.multiple_of(mine + r, RC), RC), :] = branch
    tick()
    loads.wait(in_up, in_down)

    root = math.sqrt(2.0 / math.pi)

    def feed_forward(slot, first):
        for j in range(0, T, BLOCK):
            block = slice(j, j + BLOCK)
            v = dot(s.n2[block, :], s.wu[slot])
            grad_act = dot(s.gatt[pl.ds(pl.multiple_of(mine + j, BLOCK), BLOCK), :], s.wd[slot], 1, 1)
            for r in range(0, BLOCK, RC):
                u = v[r : r + RC, :]
                square = u * u
                th = jnp.tanh(u * (root + (root * 0.044715) * square))
                up = 0.5 + 0.5 * th
                slope = up + (u * (up - up * th)) * (root + (root * 3 * 0.044715) * square)
                s.act[j + r : j + r + RC, :] = (u * up).astype(BF16)
                s.gpre[j + r : j + r + RC, :] = (grad_act[r : r + RC, :] * slope).astype(BF16)
            put_wide(s.h2, 8 + j, BLOCK, wide(s.h2, 8 + j, BLOCK) + dot(s.act[block, :], s.wd[slot]))
            grad_normed = dot(s.gpre[block, :], s.wu[slot], 1, 1)
            s.gn[block, :] = grad_normed if first else s.gn[block, :] + grad_normed
            tick()
        branch = s.gatt[pl.ds(mine, T), :]
        for j in range(0, U, BLOCK):
            s.gd[slot, j : j + BLOCK, :] = dot(s.act[:, j : j + BLOCK], branch, 0, 0).astype(BF16)
        tick()
        for j in range(0, D, BLOCK):
            s.gu[slot, j : j + BLOCK, :] = dot(s.n2[:, j : j + BLOCK], s.gpre[...], 0, 0).astype(BF16)
        tick()

    def to_other_core(slot):
        return (
            links.copy(s.gd.at[slot], s.cd.at[slot - 2], to_core),
            links.copy(s.gu.at[slot], s.cu.at[slot - 2], to_core),
        )

    def from_other_core(slot, sent):
        links.arrived(sent[0])
        s.gd[slot] = s.gd[slot] + s.cd[slot]
        links.arrived(sent[1])
        s.gu[slot] = s.gu[slot] + s.cu[slot]

    if SLOTS[0] == 3:
        flow.need("wu", "wd")
    else:
        links.arrived(owns["wu"][0])
        links.arrived(owns["wd"][0])
    shard_sums = {"d0": (s.gd, s.gd_out), "d1": (s.gd, s.gd_out), "u0": (s.gu, s.gu_out), "u1": (s.gu, s.gu_out)}
    ahead = SLOTS[1]
    early = [name for name in shard_sums if ahead == 1 or ORDER[name][0][0] != "y"]
    feed_forward(SLOTS[0], True)
    sent_one = to_other_core(SLOTS[0])
    feed_forward(SLOTS[1], False)
    from_other_core(SLOTS[1], sent_one)
    for name in early:
        start_sum(name, shard_sums[name][0].at[0:2], 0, shard_sums[name][1], True, ahead)
    flow.need("wu", "wd")
    feed_forward(SLOTS[2], False)
    sent_two = to_other_core(SLOTS[2])
    feed_forward(SLOTS[3], False)

    gain_grad_two = jnp.zeros((8, D), F32)
    for r in range(0, T, RC):
        rows = slice(r, r + RC)
        h, gn = s.h1[rows, :], s.gn[rows, :]
        scale = lax.rsqrt(jnp.mean(h * h, axis=1, keepdims=True) + EPS)
        e = gain_two * gn
        hs = h * scale
        grad = wide(s.g2t, 8 + r, RC) + scale * (e - hs * jnp.mean(e * hs, axis=1, keepdims=True))
        s.h1[rows, :] = grad
        s.gatt[pl.ds(pl.multiple_of(mine + r, RC), RC), :] = grad.astype(BF16)
        gain_grad_two = gain_grad_two + jnp.sum((gn * hs).reshape(RC // 8, 8, D), axis=0)
    own_rows = s.gatt.at[pl.ds(mine, T), :]
    sent_gatt = links.copy(own_rows, own_rows, to_core)
    sent_rim = links.copy(s.h2.at[:, T : T + 8, :], s.h2.at[:, 0:8, :], to_core)
    from_other_core(SLOTS[3], sent_two)
    flow.release(*early)
    for name in shard_sums:
        if name not in early:
            start_sum(name, shard_sums[name][0].at[0:2], 0, shard_sums[name][1])
    tick()

    block_square = jnp.zeros((8, D), F32)
    for r in range(0, T, RC):
        h = wide(s.h2, 8 + r, RC)
        block_square = block_square + jnp.sum((h * h).reshape(RC // 8, 8, D), axis=0)
    links.arrived(sent_rim)
    for j in range(POOL):
        rows = pl.ds(8 - (POOL - 1) + j, T // POOL, stride=POOL)
        taken = jnp.concatenate([s.h2[i, rows, :] for i in range(D // 128)], axis=1)
        s.n2[j * (T // POOL) : (j + 1) * (T // POOL), :] = jnp.where(kept(j), taken, 0.0).astype(BF16)
    pool_in = [s.n2[j * (T // POOL) : (j + 1) * (T // POOL), :] for j in range(POOL)]
    pooled = sum(dot(pool_in[j], s.wp[j * D : (j + 1) * D, :]) for j in range(POOL))
    pool_square = jnp.sum((pooled * pooled).reshape(T // POOL // 8, 8, D), axis=0)
    s.gpre[0 : T // POOL, :] = pooled.astype(BF16)
    out_pooled = loads.copy(s.gpre.at[0 : T // POOL, :], s.pooled_out)
    for j in range(POOL):
        s.wp[j * D : (j + 1) * D, :] = dot(pool_in[j], s.pg[...], 0, 0).astype(BF16)
    start_sum("p0", s.wp, 0, s.gp_out)
    start_sum("p1", s.wp, 0, s.gp_out)
    tick()

    def grad_heads(start):
        for j in range(0, T, BLOCK):
            cols = pl.ds(pl.multiple_of(start + j, BLOCK), BLOCK)
            g = dot(s.wo[0:2].reshape(2 * HC, D), s.gatt[cols, :], 1, 1)
            line = lax.broadcasted_iota(jnp.int32, (HEAD, BLOCK), 0)
            for head in range(4):
                low = (g[head * HEAD : (head + 1) * HEAD] * s.rl[head : head + 1, cols]).astype(BF16)
                o = s.ot[head * HEAD : (head + 1) * HEAD, cols].astype(F32)
                delta = jnp.sum(low.astype(F32) * o, axis=0, keepdims=True)
                high = delta.astype(BF16).astype(F32)
                rest = jnp.where(line == 0, high, jnp.where(line == 1, delta - high, 0.0))
                s.gox[head, 0:HEAD, cols] = low
                s.gox[head, HEAD : 2 * HEAD, cols] = rest.astype(BF16)

    grad_heads(mine)
    links.arrived(sent_gatt)
    grad_heads(theirs)
    for slot in (1, 0):
        s.go[slot] = dot(s.ot[slot * HC : (slot + 1) * HC, :], s.gatt[...]).astype(BF16)
    start_sum("o", s.go, 0, s.go_out)
    tick()

    def grad_score(head, qb, i, into):
        first, _, offset, q = window(qb)
        rows = slice(i * BLOCK, (i + 1) * BLOCK)
        grads = dot(s.vx[head, first + rows.start : first + rows.stop, :], s.gox[head, :, q])
        probs = s.probs[head, offset + rows.start : offset + rows.stop, :]
        into[rows, :] = (probs.astype(F32) * grads).astype(BF16)

    def attend_back(head):
        slot, h = head // 2, head % 2
        bufs, seen = (s.ds0, s.ds1), set()
        for i in range(window(0)[1]):
            grad_score(head, 0, i, bufs[0])
        for qb in range(QB):
            first, blocks, offset, q = window(qb)
            now, later = bufs[qb % 2], bufs[(qb + 1) % 2]
            more, done = window(qb + 1)[1] if qb + 1 < QB else 0, 0
            s.dq[:, q] = dot(s.kt[head, :, first : first + blocks * BLOCK], now[0 : blocks * BLOCK, :])
            for i in range(blocks):
                while done < (i + 1) * more // blocks:
                    grad_score(head, qb + 1, done, later)
                    done += 1
                cols = slice(first + i * BLOCK, first + (i + 1) * BLOCK)
                probs = s.probs[head, offset + i * BLOCK : offset + (i + 1) * BLOCK, :]
                dk = dot(s.qxt[head, 0:HEAD, q], now[i * BLOCK : (i + 1) * BLOCK, :], 1, 1)
                dv = dot(s.gox[head, 0:HEAD, q], probs, 1, 1)
                s.dk[:, cols] = s.dk[:, cols] + dk if cols.start in seen else dk
                s.dv[:, cols] = s.dv[:, cols] + dv if cols.start in seen else dv
                seen.add(cols.start)
            tick()
        cosine, sine = s.cos[...], s.sin[...]
        for i, (ref, factor) in enumerate(((s.dq, HEAD**-0.5), (s.dk, 1.0))):
            a, b = ref[:half_head, :], ref[half_head:, :]
            turned = jnp.concatenate([a * cosine + b * sine, b * cosine - a * sine], axis=0) * factor
            start = (3 * slot + i) * HC + h * HEAD
            s.gpt[start : start + HEAD, :] = turned.astype(BF16)
        start = (3 * slot + 2) * HC + h * HEAD
        s.gpt[start : start + HEAD, :] = s.dv[...].astype(BF16)

    def grad_weights(slot):
        for i in range(3):
            g = dot(s.gpt[(3 * slot + i) * HC : (3 * slot + i + 1) * HC, :], s.nrm[...])
            s.wq[slot, i] = g.astype(BF16).T

    attend_back(2)
    attend_back(3)
    grad_weights(1)
    start_sum("q0", s.wq, 1, s.gq_out, True)
    start_sum("q1", s.wq, 1, s.gq_out, True)
    attend_back(0)
    attend_back(1)
    grad_weights(0)
    flow.release("q0", "q1")
    tick()

    for j in range(0, T, BLOCK):
        cols = pl.ds(pl.multiple_of(theirs + j, BLOCK), BLOCK)
        s.n2[j : j + BLOCK, :] = dot(s.gpt[:, cols], s.wqt[...], 0, 0).astype(BF16)
    sent_pn = links.copy(s.n2, s.act, to_core)
    for j in range(0, T, BLOCK):
        cols = pl.ds(pl.multiple_of(mine + j, BLOCK), BLOCK)
        s.gn[j : j + BLOCK, :] = dot(s.gpt[:, cols], s.wqt[...], 0, 0)
    tick()
    links.arrived(sent_pn)
    loads.wait(out_pooled)
    gain_grad_one = jnp.zeros((8, D), F32)
    for r in range(0, T, RC):
        rows = slice(r, r + RC)
        x, gn = s.xb[rows, :].astype(F32), s.gn[rows, :] + s.act[rows, :].astype(F32)
        scale = lax.rsqrt(jnp.mean(x * x, axis=1, keepdims=True) + EPS)
        e = gain_one * gn
        xs = x * scale
        grad = s.h1[rows, :] + scale * (e - xs * jnp.mean(e * xs, axis=1, keepdims=True))
        s.gpre[rows, :] = grad.astype(BF16)
        gain_grad_one = gain_grad_one + jnp.sum((gn * xs).reshape(RC // 8, 8, D), axis=0)
    loads.copy(s.gpre, s.gtok_out)

    line = lax.broadcasted_iota(jnp.int32, (8, D), 0)
    small = jnp.zeros((8, D), F32)
    for i, v in enumerate((gain_grad_one, gain_grad_two, block_square, pool_square)):
        v = jnp.sum(v, axis=0, keepdims=True)
        if i >= 2:
            v = jnp.sum(v, axis=1, keepdims=True)
        small = jnp.where(line == i, v, small)
    s.terms[0] = small
    flow.start("s", summed(links, s.terms, s.term_in, partners))
    flow.finish()
    loads.copy(s.terms.at[len(partners)], s.small_out)
    links.finish()
    loads.finish()


def widen(count, block_scale, pool_scale, *refs):
    small, pooled, gtok, *low = refs[: 3 + count]
    out = refs[3 + count :]
    rms_block, rms_pool, gain_one, gain_two, pooled_out, gtok_out = out[:6]
    wide_out, taken, made = out[6 : 6 + count], out[6 + count : 6 + 2 * count], out[6 + 2 * count : 6 + 3 * count]
    held, sems = out[-3:-1], out[-1]
    loads = Loads(sems)
    ks = [loads.copy(src, dst) for src, dst in zip(low, taken)]
    kept = [loads.copy(src, dst) for src, dst in zip((pooled, gtok), held)]
    rms_block[...] = jnp.sqrt(small[2:3, 0:1] * block_scale)
    rms_pool[...] = jnp.sqrt(small[3:4, 0:1] * pool_scale)
    gain_one[...] = small[0:1, :]
    gain_two[...] = small[1:2, :]
    for i, k in enumerate(ks):
        loads.wait(k)
        made[i][...] = taken[i][...].astype(F32)
        loads.copy(made[i], wide_out[i])
    for k, src, dst in zip(kept, held, (pooled_out, gtok_out)):
        loads.wait(k)
        loads.copy(src, dst)
    loads.finish()


IN_NAMES = (
    "tokens", "lengths", "w_qkv", "w_out", "w_up", "w_down", "w_pool",
    "gain_one", "gain_two", "pooled_grad", "cos_in", "sin_in",
)
OUT_NAMES = ("pooled_out", "gtok_out", "gq_out", "go_out", "gu_out", "gd_out", "gp_out", "small_out")


def tables(length):
    half = HEAD // 2
    frequency = np.exp(-math.log(10000.0) * np.arange(half) / half)
    angle = frequency[:, None] * np.arange(length)[None, :]
    return np.cos(angle).astype(np.float32), np.sin(angle).astype(np.float32)


def shards(tokens, lengths, w_qkv, w_out, w_up, w_down, w_pool, gain_one, gain_two, pooled_grad):
    T, D = tokens.shape
    HC, U = w_out.shape[0], w_up.shape[1]
    dp = lax.axis_size("dp")
    bits = dp.bit_length() - 1
    assert lax.axis_size("tensor") == 4 and lengths.shape == (2, 4) and dp == 1 << bits and bits > 0
    cos, sin = tables(2 * T)
    scratch = scratch_list(T, D, HC, U, bits)
    names = IN_NAMES + OUT_NAMES + tuple(n for n, _, _ in scratch) + ("send_sems", "recv_sems", "free_sems", "load_sems")
    hbm, vmem, smem = pl.BlockSpec(memory_space=pl.ANY), pl.BlockSpec(memory_space=pltpu.VMEM), pl.BlockSpec(memory_space=pltpu.SMEM)
    copies = 192 + 16 * bits
    outs = pl.pallas_call(
        functools.partial(kernel, bits, names),
        out_shape=[
            jax.ShapeDtypeStruct((T // POOL, D), BF16),
            jax.ShapeDtypeStruct((T, D), BF16),
            jax.ShapeDtypeStruct((3, D, HC), BF16),
            jax.ShapeDtypeStruct((HC, D), BF16),
            jax.ShapeDtypeStruct((D, U), BF16),
            jax.ShapeDtypeStruct((U, D), BF16),
            jax.ShapeDtypeStruct((POOL * D, D), BF16),
            jax.ShapeDtypeStruct((8, D), F32),
        ],
        in_specs=[hbm, smem, hbm, hbm, hbm, hbm, hbm, vmem, vmem, hbm, hbm, hbm],
        out_specs=[hbm] * 8,
        scratch_shapes=[pltpu.VMEM(shape, kind) for _, shape, kind in scratch]
        + [pltpu.SemaphoreType.DMA((copies,)), pltpu.SemaphoreType.DMA((copies,))]
        + [pltpu.SemaphoreType.REGULAR((64,)), pltpu.SemaphoreType.DMA((48,))],
        compiler_params=pltpu.CompilerParams(
            collective_id=0, has_side_effects=True, vmem_limit_bytes=64 * 2**20 - 2**16
        ),
    )(
        tokens, lengths, jnp.transpose(w_qkv, (1, 0, 2)), w_out, w_up, w_down, w_pool,
        gain_one.reshape(1, D), gain_two.reshape(1, D), pooled_grad, cos, sin,
    )
    pooled, gtok, gq, go, gu, gd, gp, small = outs
    group = dp * 4 * T * D
    low = (gp, gd, gu, gq, go)
    shapes = [jax.ShapeDtypeStruct(a.shape, F32) for a in low]
    one, line = jax.ShapeDtypeStruct((1, 1), F32), jax.ShapeDtypeStruct((1, D), F32)
    rms_block, rms_pool, grad_one, grad_two, pooled, gtok, gp, gd, gu, gq, go = pl.pallas_call(
        functools.partial(widen, len(low), 1.0 / group, POOL / group),
        out_shape=[one, one, line, line, pooled, gtok] + shapes,
        in_specs=[vmem] + [hbm] * (2 + len(low)),
        out_specs=[vmem] * 4 + [hbm] * (2 + len(low)),
        scratch_shapes=[pltpu.VMEM(a.shape, BF16) for a in low]
        + [pltpu.VMEM(a.shape, F32) for a in low]
        + [pltpu.VMEM(a.shape, BF16) for a in (pooled, gtok)]
        + [pltpu.SemaphoreType.DMA((2 * len(low) + 4,))],
        compiler_params=pltpu.CompilerParams(vmem_limit_bytes=64 * 2**20 - 2**16),
    )(small, pooled, gtok, *low)
    return (
        pooled,
        rms_block.reshape(()),
        rms_pool.reshape(()),
        gtok,
        jnp.transpose(gq, (1, 0, 2)),
        go,
        gu,
        gd,
        gp,
        grad_one.reshape(D),
        grad_two.reshape(D),
    )


def solution(mesh):
    rows = P(("dp", "tensor"), None)
    placed = (
        rows, P("dp", None), P(None, None, "tensor"), P("tensor", None), P(None, "tensor"),
        P("tensor", None), P(), P(), P(), rows,
    )
    return jax.shard_map(
        shards,
        mesh=mesh,
        in_specs=placed,
        out_specs=(
            rows, P(), P(), rows, P(None, None, "tensor"), P("tensor", None), P(None, "tensor"),
            P("tensor", None), P(), P(), P(),
        ),
        check_vma=False,
    )
```

```python
import functools
import math
from types import SimpleNamespace

import jax
import jax.numpy as jnp
import numpy as np
from jax import lax
from jax.experimental import pallas as pl
from jax.experimental.pallas import tpu as pltpu
from jax.sharding import PartitionSpec as P

HEAD = 64
POOL = 3
EPS = 1e-06
BIG = float(2**30)
NEG = -1000000000.0
BLOCK = 256
LEFT = 3
WINDOW = LEFT + 1
CHUNK = 128
F32, BF16 = jnp.float32, jnp.bfloat16
MESH = pl.DeviceIdType.MESH


def dot(a, b, ca=1, cb=0):
    return lax.dot_general(a, b, (((ca,), (cb,)), ((), ())), preferred_element_type=F32)


def part(ref, dim, start, count):
    index = [slice(None)] * len(ref.shape)
    index[dim] = pl.ds(start, count)
    return ref.at[tuple(index)]


def wide(ref, start, count):
    return jnp.concatenate([ref[i, pl.ds(start, count), :] for i in range(ref.shape[0])], axis=1)


def put_wide(ref, start, count, value, stride=None):
    for i in range(ref.shape[0]):
        ref[i, pl.ds(start, count, stride=stride), :] = value[:, i * 128 : (i + 1) * 128]


def on(condition, act):
    if condition is None:
        act()
    else:
        pl.when(condition)(act)


class Links:
    def __init__(self, send, recv, free, partners):
        self.send, self.recv, self.sent, self.partners = send, recv, [], partners
        self.free, self.freed = free, 0

    def copy(self, src, dst, to, sends=None, takes=None):
        k = len(self.sent)
        move = pltpu.make_async_remote_copy(
            src, dst, self.send.at[k], self.recv.at[k], device_id=to, device_id_type=MESH
        )
        on(sends, move.start)
        self.sent.append([move, False, False, sends, takes])
        return k

    def arrived(self, k):
        if not self.sent[k][2]:
            on(self.sent[k][4], self.sent[k][0].wait_recv)
            self.sent[k][2] = True

    def left(self, k):
        if not self.sent[k][1]:
            on(self.sent[k][3], self.sent[k][0].wait_send)
            self.sent[k][1] = True

    def give(self, to, gives=None):
        i = self.freed
        self.freed += 1
        on(gives, lambda: pl.semaphore_signal(self.free.at[i], inc=1, device_id=to, device_id_type=MESH))
        return i

    def granted(self, i, takes=None):
        on(takes, lambda: pl.semaphore_wait(self.free.at[i], 1))

    def finish(self):
        for k in range(len(self.sent)):
            self.left(k)


class Loads:
    def __init__(self, sems):
        self.sems, self.moves = sems, []

    def copy(self, src, dst):
        move = pltpu.make_async_copy(src, dst, self.sems.at[len(self.moves)])
        move.start()
        self.moves.append([move, False])
        return len(self.moves) - 1

    def wait(self, *ks):
        for k in ks:
            if not self.moves[k][1]:
                self.moves[k][0].wait()
                self.moves[k][1] = True

    def finish(self):
        self.wait(*range(len(self.moves)))


class Flow:
    def __init__(self):
        self.gens, self.waits, self.at = {}, {}, 0

    def step(self, name):
        self.waits[name] = next(self.gens[name], None)
        return self.waits[name] is not None

    def start(self, name, gen, held=False):
        self.gens[name] = gen
        self.step(name)

    def release(self, *names):
        pass

    def tick(self):
        for name in PLAN[self.at] if self.at < len(PLAN) else ():
            self.step(name)
        self.at += 1

    def need(self, *names):
        for name in names:
            while self.step(name):
                pass

    def finish(self):
        self.tick()
        live = list(self.gens)
        while live:
            live = [name for name in live if self.step(name)]


def gathered(links, way, shard, buf, dim, size, bit, to_y, to_bit, to_core, owns):
    def rows(ref, start, count):
        return part(ref, dim, pl.multiple_of(start, 16), count)

    near, own = buf.at[1], None
    if way == "y":
        k = links.copy(shard, near, to_y)
        yield (k,)
        if to_core is not None:
            own = links.copy(shard, buf.at[2], to_core)
            owns.append(own)
        links.arrived(k)
        ks = first = ()
    elif len(bit) == 1:
        half = size // 2
        k = links.copy(rows(shard, bit[0] * half, half), rows(near, bit[0] * half, half), to_y)
        yield (k,)
        if to_core is not None:
            own = links.copy(shard, buf.at[2], to_core)
            owns.append(own)
        links.arrived(k)
        piece = rows(near, bit[0] * half, half)
        ks, first = (links.copy(piece, piece, to_bit[0]),), ()
    else:
        quarter = size // 4
        at = (2 * bit[1] + bit[0]) * quarter
        over_x = (2 * bit[1] + 1 - bit[0]) * quarter
        over_z = (2 - 2 * bit[1] + bit[0]) * quarter
        k = links.copy(rows(shard, at, quarter), rows(near, at, quarter), to_y)
        yield (k,)
        if to_core is not None:
            own = links.copy(shard, buf.at[2], to_core)
            owns.append(own)
        links.arrived(k)
        piece = rows(near, at, quarter)
        by_x, by_z = first = links.copy(piece, piece, to_bit[0]), links.copy(piece, piece, to_bit[1])
        yield (by_x, by_z)
        links.arrived(by_x)
        piece = rows(near, over_x, quarter // 2)
        second = links.copy(piece, piece, to_bit[1])
        links.arrived(by_z)
        piece = rows(near, over_z + quarter // 2, quarter // 2)
        ks = (links.copy(piece, piece, to_bit[0]), second)
    if ks:
        yield ks
    for k in ks:
        links.arrived(k)
    if to_core is None:
        for k in ks + first:
            links.left(k)
        return
    k = links.copy(near, buf.at[3], to_core)
    yield (k, own)
    links.arrived(own)
    links.arrived(k)


def reduced(links, loads, acc, dim, base, size, stages, bufs, out, ahead, line):
    lo, n, spans = base, size, []
    two = any(kind == "slot" for kind, _, _ in stages)

    def rows(ref, start, count, slots=False):
        return part(ref, dim + 1 if slots else dim, start if isinstance(start, int) else pl.multiple_of(start, 16), count)

    for (kind, to, bit), buf in zip(stages, bufs):
        if kind == "slot":
            k = links.copy(rows(acc.at[1], lo, n), buf, to)
            acc, two = acc.at[0], False
            mine = rows(acc, lo, n)
        elif kind == "half":
            half = n // 2
            there, here = lo + (1 - bit) * half, lo + bit * half
            if two:
                early = links.copy(rows(acc.at[ahead], there, half), buf.at[ahead], to)
                yield (early,)
                k = links.copy(rows(acc.at[1 - ahead], there, half), buf.at[1 - ahead], to)
            else:
                k = links.copy(rows(acc, there, half), buf, to)
            before = lo
            lo, n = here, half
            mine = rows(acc, lo, n, two)
        elif kind == "line":
            mine, (outer, across) = rows(acc, lo, n), line
            inner = jnp.logical_not(outer)

            def add(mine=mine, buf=buf):
                mine[...] = mine[...] + buf[...]

            k = links.copy(mine, buf, to, outer, inner)
            yield (k,)
            links.arrived(k)
            on(inner, add)
            free = links.give(across, inner)
            links.left(k)
            back = links.give(to, outer)
            links.granted(free, inner)
            k = links.copy(mine, buf, across, inner, inner)
            yield (k,)
            links.arrived(k)
            links.left(k)
            on(inner, add)
            links.granted(back, inner)
            k = links.copy(mine, mine, to, inner, outer)
            yield (k,)
            links.arrived(k)
            continue
        else:
            mine = rows(acc, lo, n)
            k = links.copy(mine, buf, to)
        yield (k,)
        if kind == "half" and two:
            links.arrived(early)
            links.left(early)
        links.arrived(k)
        if kind != "slot":
            links.left(k)
        if kind == "half":
            spans.append((to, before, links.give(to)))
        mine[...] = mine[...] + buf[...]
    for to, before, credit in reversed(spans):
        mine = rows(acc, lo, n)
        links.granted(credit)
        k = links.copy(mine, mine, to)
        yield (k,)
        links.arrived(k)
        lo, n = before, 2 * n
    for i, ref in enumerate(out):
        loads.copy(rows(acc, lo, n) if len(out) == 1 else part(acc.at[i], dim - 1, lo, n), part(ref, 0, lo, n))


def summed(links, terms, bufs, partners):
    for i, to in enumerate(partners):
        k = links.copy(terms.at[i], bufs.at[i], to)
        yield (k,)
        links.arrived(k)
        terms[i + 1] = terms[i] + bufs[i]


ORDER = {
    "d0": ("0yLs", 0, 4),
    "q0": ("1y0s", 0, 2),
    "d3": ("1y0s", 3, 4),
    "p2": ("cY01s", 2, 3),
    "p0": ("c1Y0s", 0, 3),
    "u1": ("y0Ls", 1, 2),
    "q1": ("y0Ls", 1, 2),
    "d1": ("0yLs", 1, 4),
    "p1": ("c0Y1s", 1, 3),
    "d2": ("1y0s", 2, 4),
    "u0": ("10ys", 0, 2),
    "o": ("01ys", 0, 1),
}
WAY = {"wq": "yxz", "wo": "y", "wu": "yxz", "wd": "yxz"}
SLOTS = (2, 0, 3, 1)
PLAN = (
    (), (), (), (), ("wq",), (), (), (), (), (), (), (), (), (), ("wo",), (), ("wo", "wu", "wd",), (), (), (), (),
    (), (), (), (), (), (), (), (), (), (), ("wu",), (), (), (), ("wd",), (), ("wu",), (), (), (), ("wd",), (), (),
    (), (), (), (), (), (), (), (), ("d0", "d3", "d1", "d2", "u0",), (), ("d0", "d3", "p2",),
    ("p0", "d1", "p1", "d2",), (), (), (), (), (), (), ("o",), ("u1", "u0",), (), (), ("d0",), (), (),
    ("p1", "d3", "p0",), (), ("o",), (), (), (), ("d0", "p2",), (), (), ("u1", "d1",), ("q0",),
    ("o", "u0", "d2", "d3", "d0", "p2", "u1", "q1",),
    ("d1", "s", "p1", "u0", "p0", "q0", "d2", "d3", "d0", "o", "s", "p2", "q1", "u1", "p1", "p0", "u0", "d3", "d1",
     "d0", "s", "q0", "d2", "o", "p2", "q1", "u1", "p1", "q0", "d2", "p0", "d3", "u0", "u1", "d1", "s", "p0", "o",
     "p2", "q1", "p1", "u0", "p0", "d1", "q0", "d2", "s", "p2", "o", "p1", "q1", "q0", "o", "u0", "p2", "p2", "p1",
     "p0", "p1", "q1", "p0", "q0",),
)


def stage_kinds(order, bits):
    kinds = []
    for letter in order:
        if letter == "y":
            kinds.append(("slot", 1))
        elif letter in "cY":
            kinds.append(("half", "cY".index(letter)))
        elif letter == "L":
            kinds += [("line", 3)] if bits > 2 else []
        elif letter in "01":
            kinds += [("half", 2 + int(letter))] if int(letter) < bits else []
        else:
            kinds += [("swap", 2 + i) for i in range(3 if "L" in order else 2, bits)]
    return kinds


def buffer_shapes(order, rows, shape, bits):
    kinds, out = stage_kinds(order, bits), []
    two = any(kind == "slot" for kind, _ in kinds)
    for kind, _ in kinds:
        if kind == "slot":
            two = False
        elif kind == "half":
            rows //= 2
        out.append(((2,) if two else ()) + shape(rows))
    return out


def scratch_list(T, D, HC, U, bits):
    L, heads, qb = 2 * T, 2 * HC // HEAD, 2 * T // BLOCK
    blocks = sum(min(i, LEFT) + 1 for i in range(qb))
    kd = POOL * D
    out = [
        ("xb", (T, D), BF16),
        ("nrm", (L, D), BF16),
        ("wq", (2, 3, D, HC), BF16),
        ("wqt", (6 * HC, D), BF16),
        ("wo", (4, HC, D), BF16),
        ("wu", (4, D, U), BF16),
        ("wd", (4, U, D), BF16),
        ("wp", (kd, D), BF16),
        ("pg", (T // POOL, D), BF16),
        ("cos", (HEAD // 2, L), F32),
        ("sin", (HEAD // 2, L), F32),
        ("qxt", (heads, 2 * HEAD, L), BF16),
        ("kt", (heads, HEAD, L), BF16),
        ("vt", (heads, HEAD, L), BF16),
        ("kx", (heads, L, 2 * HEAD), BF16),
        ("vx", (heads, L, 2 * HEAD), BF16),
        ("probs", (heads, blocks * BLOCK, BLOCK), BF16),
        ("rl", (8, L), F32),
        ("ot", (2 * HC, L), BF16),
        ("otf", (4 * HC, T), BF16),
        ("gox", (heads, 2 * HEAD, L), BF16),
        ("gpt", (6 * HC, L), BF16),
        ("h1", (T, D), F32),
        ("h2", (D // 128, T + 8, 128), F32),
        ("g2t", (D // 128, T + 8, 128), F32),
        ("rim", (D // 128, 8, 128), F32),
        ("n2", (T, D), BF16),
        ("act", (T, U), BF16),
        ("gpre", (T, U), BF16),
        ("gn", (T, D), F32),
        ("gatt", (L, D), BF16),
        ("dk", (HEAD, L), F32),
        ("dv", (HEAD, L), F32),
        ("dq", (HEAD, L), F32),
        ("gd", (4, U, D), BF16),
        ("gu", (4, D, U), BF16),
        ("go", (2, HC, D), BF16),
        ("cd", (2, U, D), BF16),
        ("cu", (2, D, U), BF16),
        ("sc0", (WINDOW * BLOCK, BLOCK), F32),
        ("sc1", (WINDOW * BLOCK, BLOCK), F32),
        ("ds0", (WINDOW * BLOCK, BLOCK), BF16),
        ("ds1", (WINDOW * BLOCK, BLOCK), BF16),
        ("terms", (bits + 3, 8, D), F32),
        ("term_in", (bits + 2, 8, D), F32),
    ]
    rows_of = {"d": U, "u": D, "o": HC, "q": D, "p": kd}
    shape_of = {
        "d": lambda n: (n, D),
        "u": lambda n: (n, U),
        "o": lambda n: (n, D),
        "q": lambda n: (3, n, HC),
        "p": lambda n: (n, D),
    }
    for name, (order, _, parts) in ORDER.items():
        shapes = buffer_shapes(order, rows_of[name[0]] // parts, shape_of[name[0]], bits)
        out += [(f"in_{name}_{i}", shape, BF16) for i, shape in enumerate(shapes)]
    return out


def kernel(bits, names, *refs):
    s = SimpleNamespace(**dict(zip(names, refs)))
    T, D = s.xb.shape
    HC, U = s.wo.shape[1], s.wu.shape[2]
    L, QB = 2 * T, 2 * T // BLOCK
    half_head = HEAD // 2
    places, _ = result_rows(T, D, HC, U)
    RC = 32
    loads = Loads(s.load_sems)

    d, t = lax.axis_index("dp"), lax.axis_index("tensor")
    c, y = t % 2, t // 2
    to_core, to_y = (d, t + 1 - 2 * c), (d, t + 2 - 4 * y)
    bit = [(d // (1 << i)) % 2 for i in range(bits)]
    to_bit = [(d + (1 - 2 * bit[i]) * (1 << i), t) for i in range(bits)]
    partners = [to_core, to_y] + to_bit
    outer, across = None, None
    if bits > 2:
        outer = bit[1] == bit[2]
        across = (d + (1 - 2 * bit[1]) * 2 + (1 - 2 * bit[2]) * 4, t)
    links, flow = Links(s.send_sems, s.recv_sems, s.free_sems, partners), Flow()
    sides = [c, y] + bit
    tick = flow.tick

    def start_sum(name, acc, dim, held=False, ahead=1):
        order, piece, parts = ORDER[name]
        size = {"d": U, "u": D, "o": HC, "q": D, "p": POOL * D}[name[0]] // parts
        at, rows = places[name[0]]
        if name[0] == "q":
            out = [s.low_out.at[at : at + rows, i * HC : (i + 1) * HC] for i in range(3)]
        else:
            out = [s.low_out.at[at : at + rows, :]]
        stages = [(kind, partners[i], sides[i]) for kind, i in stage_kinds(order, bits)]
        bufs = [getattr(s, f"in_{name}_{i}") for i in range(len(stages))]
        flow.start(name, reduced(links, loads, acc, dim, piece * size, size, stages, bufs, out, ahead, (outer, across)), held)

    mine = pl.multiple_of(c * T, T)
    theirs = pl.multiple_of((1 - c) * T, T)

    in_x = loads.copy(s.tokens, s.xb)
    in_q = loads.copy(s.w_qkv, s.wq.at[0])
    in_pool = loads.copy(s.w_pool, s.wp)
    in_pg = loads.copy(s.pooled_grad, s.pg)
    in_cos, in_sin = loads.copy(s.cos_in, s.cos), loads.copy(s.sin_in, s.sin)
    in_out = loads.copy(s.w_out, s.wo.at[0])
    in_up = loads.copy(s.w_up, s.wu.at[0])
    in_down = loads.copy(s.w_down, s.wd.at[0])

    barrier = pltpu.get_barrier_semaphore()
    greeted = partners + ([across] if bits > 2 else [])
    for to in greeted:
        pl.semaphore_signal(barrier, inc=1, device_id=to, device_id_type=MESH)
    pl.semaphore_wait(barrier, len(greeted))

    owns = {"wq": [], "wo": [], "wu": [], "wd": []}

    def get(name, shard, buf, dim, size, core):
        flow.start(name, gathered(links, WAY[name], shard, buf, dim, size, bit, to_y, to_bit, core, owns[name]))

    get("wq", s.w_qkv, s.wq, 1, D, None)
    get("wo", s.w_out, s.wo, 0, HC, to_core)
    get("wu", s.w_up, s.wu, 0, D, to_core)
    get("wd", s.w_down, s.wd, 0, U, to_core)

    gain_one, gain_two = s.gain_one[...], s.gain_two[...]
    loads.wait(in_x)
    for r in range(0, T, RC):
        x = s.xb[r : r + RC, :].astype(F32)
        scale = lax.rsqrt(jnp.mean(x * x, axis=1, keepdims=True) + EPS)
        s.nrm[pl.ds(pl.multiple_of(mine + r, RC), RC), :] = (x * scale * gain_one).astype(BF16)
    own_rows = s.nrm.at[pl.ds(mine, T), :]
    sent_norm = links.copy(own_rows, own_rows, to_core)

    starts, ends, total = [], [], 0
    for j in range(4):
        starts.append(total)
        total = total + s.lengths[y, j]
        ends.append(total)

    def kept(j):
        p = mine + POOL * lax.broadcasted_iota(jnp.int32, (T // POOL, 1), 0) + j
        bad = (p - 1) <= 0
        for e in ends[:3]:
            bad = bad | ((p >= e) & (p - 1 <= e))
        return jnp.logical_not(bad)

    loads.wait(in_q, in_cos, in_sin)
    row = lax.broadcasted_iota(jnp.int32, (HEAD, L), 0)
    pos = lax.broadcasted_iota(jnp.int32, (HEAD, L), 1)
    same = jnp.zeros((HEAD, L), F32)
    for j in range(4):
        same = jnp.where((row == j) & (pos >= starts[j]) & (pos < ends[j]), 1.0, same)
    key_rows_doc = same.astype(BF16)
    query_rows_doc = jnp.where(row < 4, BIG * (same - 1.0), 0.0).astype(BF16)
    value_rows = jnp.where(row < 2, -1.0, 0.0).astype(BF16)
    for h in range(4):
        s.qxt[h, HEAD : 2 * HEAD, :] = query_rows_doc

    def turn_weights(slot):
        for i in range(3):
            s.wqt[(3 * slot + i) * HC : (3 * slot + i + 1) * HC, :] = s.wq[slot, i].T

    def project(slot, start):
        for j in range(0, T, BLOCK):
            cols = pl.ds(pl.multiple_of(start + j, BLOCK), BLOCK)
            cosine, sine = s.cos[:, cols], s.sin[:, cols]
            r = dot(s.wqt[3 * slot * HC : 3 * (slot + 1) * HC, :], s.nrm[cols, :], 1, 1)
            for i in range(3):
                for h in range(2):
                    u = r[i * HC + h * HEAD : i * HC + (h + 1) * HEAD, :]
                    head = 2 * slot + h
                    if i == 2:
                        s.vt[head, :, cols] = u.astype(BF16)
                        continue
                    a, b = u[:half_head], u[half_head:]
                    turned = jnp.concatenate([a * cosine - b * sine, a * sine + b * cosine], axis=0)
                    if i == 0:
                        s.qxt[head, 0:HEAD, cols] = (turned * HEAD**-0.5).astype(BF16)
                    else:
                        s.kt[head, :, cols] = turned.astype(BF16)

    def turn_keys(head):
        s.kx[head] = jnp.concatenate([s.kt[head], key_rows_doc], axis=0).T
        s.vx[head] = jnp.concatenate([s.vt[head], value_rows], axis=0).T

    turn_weights(0)
    project(0, mine)
    tick()

    loads.wait(in_pool, in_pg)
    s.g2t[:, 0:8, :] = jnp.zeros((D // 128, 8, 128), F32)
    s.g2t[:, T : T + 8, :] = jnp.zeros((D // 128, 8, 128), F32)
    for j in range(POOL):
        grad_shift = dot(s.pg[...], s.wp[j * D : (j + 1) * D, :], 1, 1)
        put_wide(s.g2t, 8 - (POOL - 1) + j, T // POOL, jnp.where(kept(j), grad_shift, 0.0), POOL)
    sent_rim = links.copy(s.g2t.at[:, 0:8, :], s.rim, to_core)

    tick()
    links.arrived(sent_norm)
    project(0, theirs)
    tick()
    turn_keys(0)
    turn_keys(1)
    tick()

    def window(qb):
        first = max(0, qb - LEFT)
        blocks = qb - first + 1
        offset = sum(min(i, LEFT) + 1 for i in range(qb)) * BLOCK
        return first * BLOCK, blocks, offset, slice(qb * BLOCK, (qb + 1) * BLOCK)

    def score(head, qb, i, into):
        first, blocks, _, q = window(qb)
        rows = slice(i * CHUNK, (i + 1) * CHUNK)
        scores = dot(s.kx[head, first + rows.start : first + rows.stop, :], s.qxt[head, :, q])
        below = rows.start - (blocks - 1) * BLOCK
        if below >= 0:
            ki = lax.broadcasted_iota(jnp.int32, (CHUNK, BLOCK), 0) + below
            qi = lax.broadcasted_iota(jnp.int32, (CHUNK, BLOCK), 1)
            scores = jnp.where(ki <= qi, scores, NEG)
        into[rows, :] = scores
        return jnp.max(scores.reshape(CHUNK // 8, 8, BLOCK), axis=0)

    def attend(head):
        order = list(range(1, QB)) + [0]
        pieces = [window(qb)[1] * BLOCK // CHUNK for qb in order]
        bufs = (s.sc0, s.sc1)
        tops = [score(head, order[0], i, bufs[0]) for i in range(pieces[0])]
        for at, qb in enumerate(order):
            first, blocks, offset, q = window(qb)
            now, later = bufs[at % 2], bufs[(at + 1) % 2]
            top = jnp.max(functools.reduce(jnp.maximum, tops), axis=0, keepdims=True)
            more = pieces[at + 1] if at + 1 < QB else 0
            tops, total = [], jnp.zeros((8, BLOCK), F32)
            for i in range(pieces[at]):
                while len(tops) < (i + 1) * more // pieces[at]:
                    tops.append(score(head, order[at + 1], len(tops), later))
                e = jnp.exp(now[i * CHUNK : (i + 1) * CHUNK, :] - top)
                total = total + jnp.sum(e.reshape(CHUNK // 8, 8, BLOCK), axis=0)
                s.probs[head, offset + i * CHUNK : offset + (i + 1) * CHUNK, :] = e.astype(BF16)
            inverse = 1.0 / jnp.sum(total, axis=0, keepdims=True)
            s.rl[head : head + 1, q] = inverse
            low = s.probs[head, offset : offset + blocks * BLOCK, :]
            out = dot(s.vt[head, :, first : first + blocks * BLOCK], low) * inverse
            s.ot[head * HEAD : (head + 1) * HEAD, q] = out.astype(BF16)
            tick()

    def send_heads(slot):
        rows = slice(slot * HC, (slot + 1) * HC)
        s.otf[rows, :] = s.ot[rows, pl.ds(mine, T)]
        return links.copy(
            s.ot.at[rows, pl.ds(theirs, T)],
            s.otf.at[(2 + slot) * HC : (3 + slot) * HC, :],
            to_core,
        )

    attend(0)
    attend(1)
    sent_heads = [send_heads(0)]
    flow.need("wq")
    turn_weights(1)
    project(1, mine)
    tick()
    project(1, theirs)
    turn_keys(2)
    turn_keys(3)
    tick()
    attend(2)
    attend(3)
    sent_heads.append(send_heads(1))
    tick()
    flow.need("wo")
    loads.wait(in_out)
    for k in sent_heads:
        links.arrived(k)

    for j in range(0, T, BLOCK):
        out = dot(s.otf[:, j : j + BLOCK], s.wo[...].reshape(4 * HC, D), 0, 0)
        for r in range(j, j + BLOCK, RC):
            rows = slice(r, r + RC)
            h = out[r - j : r - j + RC, :] + s.xb[rows, :].astype(F32)
            s.h1[rows, :] = h
            put_wide(s.h2, 8 + r, RC, h)
            scale = lax.rsqrt(jnp.mean(h * h, axis=1, keepdims=True) + EPS)
            s.n2[rows, :] = (h * scale * gain_two).astype(BF16)
    links.arrived(sent_rim)
    tail = lax.broadcasted_iota(jnp.int32, (D // 128, 8, 128), 1) >= 8 - (POOL - 1)
    s.g2t[:, T : T + 8, :] = s.g2t[:, T : T + 8, :] + jnp.where(tail, s.rim[...], 0.0)
    for r in range(0, T, RC):
        branch = wide(s.g2t, 8 + r, RC).astype(BF16)
        s.gatt[pl.ds(pl.multiple_of(mine + r, RC), RC), :] = branch
    tick()
    loads.wait(in_up, in_down)

    root = math.sqrt(2.0 / math.pi)

    def feed_forward(slot, first):
        for j in range(0, T, BLOCK):
            block = slice(j, j + BLOCK)
            v = dot(s.n2[block, :], s.wu[slot])
            grad_act = dot(s.gatt[pl.ds(pl.multiple_of(mine + j, BLOCK), BLOCK), :], s.wd[slot], 1, 1)
            for r in range(0, BLOCK, RC):
                u = v[r : r + RC, :]
                square = u * u
                th = jnp.tanh(u * (root + (root * 0.044715) * square))
                up = 0.5 + 0.5 * th
                slope = up + (u * (up - up * th)) * (root + (root * 3 * 0.044715) * square)
                s.act[j + r : j + r + RC, :] = (u * up).astype(BF16)
                s.gpre[j + r : j + r + RC, :] = (grad_act[r : r + RC, :] * slope).astype(BF16)
            put_wide(s.h2, 8 + j, BLOCK, wide(s.h2, 8 + j, BLOCK) + dot(s.act[block, :], s.wd[slot]))
            grad_normed = dot(s.gpre[block, :], s.wu[slot], 1, 1)
            s.gn[block, :] = grad_normed if first else s.gn[block, :] + grad_normed
            tick()
        branch = s.gatt[pl.ds(mine, T), :]
        for j in range(0, U, BLOCK):
            s.gd[slot, j : j + BLOCK, :] = dot(s.act[:, j : j + BLOCK], branch, 0, 0).astype(BF16)
        tick()
        for j in range(0, D, BLOCK):
            s.gu[slot, j : j + BLOCK, :] = dot(s.n2[:, j : j + BLOCK], s.gpre[...], 0, 0).astype(BF16)
        tick()

    def to_other_core(slot):
        return (
            links.copy(s.gd.at[slot], s.cd.at[slot - 2], to_core),
            links.copy(s.gu.at[slot], s.cu.at[slot - 2], to_core),
        )

    def from_other_core(slot, sent):
        links.arrived(sent[0])
        s.gd[slot] = s.gd[slot] + s.cd[slot]
        links.arrived(sent[1])
        s.gu[slot] = s.gu[slot] + s.cu[slot]

    if SLOTS[0] == 3:
        flow.need("wu", "wd")
    else:
        links.arrived(owns["wu"][0])
        links.arrived(owns["wd"][0])
    shard_sums = {name: s.gd if name[0] == "d" else s.gu for name in ORDER if name[0] in "du"}
    ahead = SLOTS[1]
    early = [name for name in shard_sums if ahead == 1 or ORDER[name][0][0] != "y"]
    feed_forward(SLOTS[0], True)
    sent_one = to_other_core(SLOTS[0])
    feed_forward(SLOTS[1], False)
    from_other_core(SLOTS[1], sent_one)
    for name in early:
        start_sum(name, shard_sums[name].at[0:2], 0, True, ahead)
    flow.need("wu", "wd")
    feed_forward(SLOTS[2], False)
    sent_two = to_other_core(SLOTS[2])
    feed_forward(SLOTS[3], False)

    gain_grad_two = jnp.zeros((8, D), F32)
    for r in range(0, T, RC):
        rows = slice(r, r + RC)
        h, gn = s.h1[rows, :], s.gn[rows, :]
        scale = lax.rsqrt(jnp.mean(h * h, axis=1, keepdims=True) + EPS)
        e = gain_two * gn
        hs = h * scale
        grad = wide(s.g2t, 8 + r, RC) + scale * (e - hs * jnp.mean(e * hs, axis=1, keepdims=True))
        s.h1[rows, :] = grad
        s.gatt[pl.ds(pl.multiple_of(mine + r, RC), RC), :] = grad.astype(BF16)
        gain_grad_two = gain_grad_two + jnp.sum((gn * hs).reshape(RC // 8, 8, D), axis=0)
    own_rows = s.gatt.at[pl.ds(mine, T), :]
    sent_gatt = links.copy(own_rows, own_rows, to_core)
    sent_rim = links.copy(s.h2.at[:, T : T + 8, :], s.h2.at[:, 0:8, :], to_core)
    from_other_core(SLOTS[3], sent_two)
    flow.release(*early)
    for name in shard_sums:
        if name not in early:
            start_sum(name, shard_sums[name].at[0:2], 0)
    tick()

    block_square = jnp.zeros((8, D), F32)
    for r in range(0, T, RC):
        h = wide(s.h2, 8 + r, RC)
        block_square = block_square + jnp.sum((h * h).reshape(RC // 8, 8, D), axis=0)
    links.arrived(sent_rim)
    for j in range(POOL):
        rows = pl.ds(8 - (POOL - 1) + j, T // POOL, stride=POOL)
        taken = jnp.concatenate([s.h2[i, rows, :] for i in range(D // 128)], axis=1)
        s.n2[j * (T // POOL) : (j + 1) * (T // POOL), :] = jnp.where(kept(j), taken, 0.0).astype(BF16)
    pool_in = [s.n2[j * (T // POOL) : (j + 1) * (T // POOL), :] for j in range(POOL)]
    pooled = sum(dot(pool_in[j], s.wp[j * D : (j + 1) * D, :]) for j in range(POOL))
    pool_square = jnp.sum((pooled * pooled).reshape(T // POOL // 8, 8, D), axis=0)
    s.gpre[0 : T // POOL, :] = pooled.astype(BF16)
    out_pooled = loads.copy(s.gpre.at[0 : T // POOL, :], part(s.low_out, 0, *places["pooled"]))
    for j in range(POOL):
        s.wp[j * D : (j + 1) * D, :] = dot(pool_in[j], s.pg[...], 0, 0).astype(BF16)
    for name in (name for name in ORDER if name[0] == "p"):
        start_sum(name, s.wp, 0)
    tick()

    def grad_heads(start):
        for j in range(0, T, BLOCK):
            cols = pl.ds(pl.multiple_of(start + j, BLOCK), BLOCK)
            g = dot(s.wo[0:2].reshape(2 * HC, D), s.gatt[cols, :], 1, 1)
            line = lax.broadcasted_iota(jnp.int32, (HEAD, BLOCK), 0)
            for head in range(4):
                low = (g[head * HEAD : (head + 1) * HEAD] * s.rl[head : head + 1, cols]).astype(BF16)
                o = s.ot[head * HEAD : (head + 1) * HEAD, cols].astype(F32)
                delta = jnp.sum(low.astype(F32) * o, axis=0, keepdims=True)
                high = delta.astype(BF16).astype(F32)
                rest = jnp.where(line == 0, high, jnp.where(line == 1, delta - high, 0.0))
                s.gox[head, 0:HEAD, cols] = low
                s.gox[head, HEAD : 2 * HEAD, cols] = rest.astype(BF16)

    grad_heads(mine)
    links.arrived(sent_gatt)
    grad_heads(theirs)
    for slot in (1, 0):
        s.go[slot] = dot(s.ot[slot * HC : (slot + 1) * HC, :], s.gatt[...]).astype(BF16)
    start_sum("o", s.go, 0)
    tick()

    def grad_score(head, qb, i, into):
        first, _, offset, q = window(qb)
        rows = slice(i * BLOCK, (i + 1) * BLOCK)
        grads = dot(s.vx[head, first + rows.start : first + rows.stop, :], s.gox[head, :, q])
        probs = s.probs[head, offset + rows.start : offset + rows.stop, :]
        into[rows, :] = (probs.astype(F32) * grads).astype(BF16)

    def attend_back(head):
        slot, h = head // 2, head % 2
        bufs, seen = (s.ds0, s.ds1), set()
        for i in range(window(0)[1]):
            grad_score(head, 0, i, bufs[0])
        for qb in range(QB):
            first, blocks, offset, q = window(qb)
            now, later = bufs[qb % 2], bufs[(qb + 1) % 2]
            more, done = window(qb + 1)[1] if qb + 1 < QB else 0, 0
            s.dq[:, q] = dot(s.kt[head, :, first : first + blocks * BLOCK], now[0 : blocks * BLOCK, :])
            for i in range(blocks):
                while done < (i + 1) * more // blocks:
                    grad_score(head, qb + 1, done, later)
                    done += 1
                cols = slice(first + i * BLOCK, first + (i + 1) * BLOCK)
                probs = s.probs[head, offset + i * BLOCK : offset + (i + 1) * BLOCK, :]
                dk = dot(s.qxt[head, 0:HEAD, q], now[i * BLOCK : (i + 1) * BLOCK, :], 1, 1)
                dv = dot(s.gox[head, 0:HEAD, q], probs, 1, 1)
                s.dk[:, cols] = s.dk[:, cols] + dk if cols.start in seen else dk
                s.dv[:, cols] = s.dv[:, cols] + dv if cols.start in seen else dv
                seen.add(cols.start)
            tick()
        cosine, sine = s.cos[...], s.sin[...]
        for i, (ref, factor) in enumerate(((s.dq, HEAD**-0.5), (s.dk, 1.0))):
            a, b = ref[:half_head, :], ref[half_head:, :]
            turned = jnp.concatenate([a * cosine + b * sine, b * cosine - a * sine], axis=0) * factor
            start = (3 * slot + i) * HC + h * HEAD
            s.gpt[start : start + HEAD, :] = turned.astype(BF16)
        start = (3 * slot + 2) * HC + h * HEAD
        s.gpt[start : start + HEAD, :] = s.dv[...].astype(BF16)

    def grad_weights(slot):
        for i in range(3):
            g = dot(s.gpt[(3 * slot + i) * HC : (3 * slot + i + 1) * HC, :], s.nrm[...])
            s.wq[slot, i] = g.astype(BF16).T

    attend_back(2)
    attend_back(3)
    grad_weights(1)
    sums_q = [name for name in ORDER if name[0] == "q"]
    for name in sums_q:
        start_sum(name, s.wq, 1, True)
    attend_back(0)
    attend_back(1)
    grad_weights(0)
    flow.release(*sums_q)
    tick()

    for j in range(0, T, BLOCK):
        cols = pl.ds(pl.multiple_of(theirs + j, BLOCK), BLOCK)
        s.n2[j : j + BLOCK, :] = dot(s.gpt[:, cols], s.wqt[...], 0, 0).astype(BF16)
    sent_pn = links.copy(s.n2, s.act, to_core)
    for j in range(0, T, BLOCK):
        cols = pl.ds(pl.multiple_of(mine + j, BLOCK), BLOCK)
        s.gn[j : j + BLOCK, :] = dot(s.gpt[:, cols], s.wqt[...], 0, 0)
    tick()
    links.arrived(sent_pn)
    loads.wait(out_pooled)
    gain_grad_one = jnp.zeros((8, D), F32)
    for r in range(0, T, RC):
        rows = slice(r, r + RC)
        x, gn = s.xb[rows, :].astype(F32), s.gn[rows, :] + s.act[rows, :].astype(F32)
        scale = lax.rsqrt(jnp.mean(x * x, axis=1, keepdims=True) + EPS)
        e = gain_one * gn
        xs = x * scale
        grad = s.h1[rows, :] + scale * (e - xs * jnp.mean(e * xs, axis=1, keepdims=True))
        s.gpre[rows, :] = grad.astype(BF16)
        gain_grad_one = gain_grad_one + jnp.sum((gn * xs).reshape(RC // 8, 8, D), axis=0)
    loads.copy(s.gpre, part(s.low_out, 0, *places["gtok"]))

    line = lax.broadcasted_iota(jnp.int32, (8, D), 0)
    small = jnp.zeros((8, D), F32)
    for i, v in enumerate((gain_grad_one, gain_grad_two, block_square, pool_square)):
        v = jnp.sum(v, axis=0, keepdims=True)
        if i >= 2:
            v = jnp.sum(v, axis=1, keepdims=True)
        small = jnp.where(line == i, v, small)
    s.terms[0] = small
    flow.start("s", summed(links, s.terms, s.term_in, partners))
    flow.finish()
    loads.copy(s.terms.at[len(partners)], s.small_out)
    links.finish()
    loads.finish()


def result_rows(T, D, HC, U):
    sizes = {"p": POOL * D, "d": U, "u": D, "q": D, "o": HC, "pooled": T // POOL, "gtok": T}
    at, out = 0, {}
    for name, rows in sizes.items():
        out[name] = (at, rows)
        at += rows
    return out, at


def widen(places, block_scale, pool_scale, small, low, *refs):
    rms_block, rms_pool, gain_one, gain_two = refs[:4]
    results, wide_refs, taken, sems = dict(zip(places, refs[4:11])), dict(zip(places, refs[11:16])), refs[16], refs[17]
    loads, ks = Loads(sems), {}
    for name, (at, rows) in places.items():
        ks[name] = loads.copy(low.at[at : at + rows, :], taken.at[at : at + rows, :])
    rms_block[...] = jnp.sqrt(small[2:3, 0:1] * block_scale)
    rms_pool[...] = jnp.sqrt(small[3:4, 0:1] * pool_scale)
    gain_one[...] = small[0:1, :]
    gain_two[...] = small[1:2, :]
    for name, made in wide_refs.items():
        at, rows = places[name]
        loads.wait(ks[name])
        if name == "q":
            for i in range(3):
                width = made.shape[2]
                made[i] = taken[at : at + rows, i * width : (i + 1) * width].astype(F32)
        else:
            made[...] = taken[at : at + rows, :].astype(F32)
        loads.copy(made, results[name])
    for name in ("pooled", "gtok"):
        at, rows = places[name]
        loads.wait(ks[name])
        loads.copy(taken.at[at : at + rows, :], results[name])
    loads.finish()


IN_NAMES = (
    "tokens", "lengths", "w_qkv", "w_out", "w_up", "w_down", "w_pool",
    "gain_one", "gain_two", "pooled_grad", "cos_in", "sin_in",
)
OUT_NAMES = ("low_out", "small_out")


def tables(length):
    half = HEAD // 2
    frequency = np.exp(-math.log(10000.0) * np.arange(half) / half)
    angle = frequency[:, None] * np.arange(length)[None, :]
    return np.cos(angle).astype(np.float32), np.sin(angle).astype(np.float32)


def shards(tokens, lengths, w_qkv, w_out, w_up, w_down, w_pool, gain_one, gain_two, pooled_grad):
    T, D = tokens.shape
    HC, U = w_out.shape[0], w_up.shape[1]
    dp = lax.axis_size("dp")
    bits = dp.bit_length() - 1
    assert lax.axis_size("tensor") == 4 and lengths.shape == (2, 4) and dp == 1 << bits and bits > 0
    cos, sin = tables(2 * T)
    scratch = scratch_list(T, D, HC, U, bits)
    names = IN_NAMES + OUT_NAMES + tuple(n for n, _, _ in scratch) + ("send_sems", "recv_sems", "free_sems", "load_sems")
    hbm, vmem, smem = pl.BlockSpec(memory_space=pl.ANY), pl.BlockSpec(memory_space=pltpu.VMEM), pl.BlockSpec(memory_space=pltpu.SMEM)
    copies = 256 + 24 * bits
    places, total = result_rows(T, D, HC, U)
    low, small = pl.pallas_call(
        functools.partial(kernel, bits, names),
        out_shape=[jax.ShapeDtypeStruct((total, D), BF16), jax.ShapeDtypeStruct((8, D), F32)],
        in_specs=[hbm, smem, hbm, hbm, hbm, hbm, hbm, vmem, vmem, hbm, hbm, hbm],
        out_specs=[hbm] * 2,
        scratch_shapes=[pltpu.VMEM(shape, kind) for _, shape, kind in scratch]
        + [pltpu.SemaphoreType.DMA((copies,)), pltpu.SemaphoreType.DMA((copies,))]
        + [pltpu.SemaphoreType.REGULAR((160,)), pltpu.SemaphoreType.DMA((64,))],
        compiler_params=pltpu.CompilerParams(
            collective_id=0, has_side_effects=True, vmem_limit_bytes=64 * 2**20 - 2**16
        ),
    )(
        tokens, lengths, jnp.transpose(w_qkv, (1, 0, 2)), w_out, w_up, w_down, w_pool,
        gain_one.reshape(1, D), gain_two.reshape(1, D), pooled_grad, cos, sin,
    )
    group = dp * 4 * T * D
    one, line = jax.ShapeDtypeStruct((1, 1), F32), jax.ShapeDtypeStruct((1, D), F32)
    wide_shapes = [jax.ShapeDtypeStruct(s, F32) for s in ((POOL * D, D), (U, D), (D, U), (3, D, HC), (HC, D))]
    rms_block, rms_pool, grad_one, grad_two, gp, gd, gu, gq, go, pooled, gtok = pl.pallas_call(
        functools.partial(widen, places, 1.0 / group, POOL / group),
        out_shape=[one, one, line, line]
        + wide_shapes
        + [jax.ShapeDtypeStruct((T // POOL, D), BF16), jax.ShapeDtypeStruct((T, D), BF16)],
        in_specs=[vmem, hbm],
        out_specs=[vmem] * 4 + [hbm] * 7,
        scratch_shapes=[pltpu.VMEM(a.shape, F32) for a in wide_shapes]
        + [pltpu.VMEM((total, D), BF16), pltpu.SemaphoreType.DMA((14,))],
        compiler_params=pltpu.CompilerParams(vmem_limit_bytes=62 * 2**20),
    )(small, low)
    return (
        pooled,
        rms_block.reshape(()),
        rms_pool.reshape(()),
        gtok,
        jnp.transpose(gq, (1, 0, 2)),
        go,
        gu,
        gd,
        gp,
        grad_one.reshape(D),
        grad_two.reshape(D),
    )


def solution(mesh):
    rows = P(("dp", "tensor"), None)
    placed = (
        rows, P("dp", None), P(None, None, "tensor"), P("tensor", None), P(None, "tensor"),
        P("tensor", None), P(), P(), P(), rows,
    )
    return jax.shard_map(
        shards,
        mesh=mesh,
        in_specs=placed,
        out_specs=(
            rows, P(), P(), rows, P(None, None, "tensor"), P("tensor", None), P(None, "tensor"),
            P("tensor", None), P(), P(), P(),
        ),
        check_vma=False,
    )
```

```python
import functools
import math
from types import SimpleNamespace

import jax
import jax.numpy as jnp
import numpy as np
from jax import lax
from jax.experimental import pallas as pl
from jax.experimental.pallas import tpu as pltpu
from jax.sharding import PartitionSpec as P

HEAD = 64
POOL = 3
EPS = 1e-06
BIG = float(2**30)
NEG = -1000000000.0
BLOCK = 256
LEFT = 3
WINDOW = LEFT + 1
CHUNK = 128
F32, BF16 = jnp.float32, jnp.bfloat16
MESH = pl.DeviceIdType.MESH


def dot(a, b, ca=1, cb=0):
    return lax.dot_general(a, b, (((ca,), (cb,)), ((), ())), preferred_element_type=F32)


def part(ref, dim, start, count):
    index = [slice(None)] * len(ref.shape)
    index[dim] = pl.ds(start, count)
    return ref.at[tuple(index)]


def wide(ref, start, count):
    return jnp.concatenate([ref[i, pl.ds(start, count), :] for i in range(ref.shape[0])], axis=1)


def put_wide(ref, start, count, value, stride=None):
    for i in range(ref.shape[0]):
        ref[i, pl.ds(start, count, stride=stride), :] = value[:, i * 128 : (i + 1) * 128]


def on(condition, act):
    if condition is None:
        act()
    else:
        pl.when(condition)(act)


class Links:
    def __init__(self, send, recv, free, partners):
        self.send, self.recv, self.sent, self.partners = send, recv, [], partners
        self.free, self.freed = free, 0

    def copy(self, src, dst, to, sends=None, takes=None):
        k = len(self.sent)
        move = pltpu.make_async_remote_copy(
            src, dst, self.send.at[k], self.recv.at[k], device_id=to, device_id_type=MESH
        )
        on(sends, move.start)
        self.sent.append([move, False, False, sends, takes])
        return k

    def arrived(self, k):
        if not self.sent[k][2]:
            on(self.sent[k][4], self.sent[k][0].wait_recv)
            self.sent[k][2] = True

    def left(self, k):
        if not self.sent[k][1]:
            on(self.sent[k][3], self.sent[k][0].wait_send)
            self.sent[k][1] = True

    def give(self, to, gives=None):
        i = self.freed
        self.freed += 1
        on(gives, lambda: pl.semaphore_signal(self.free.at[i], inc=1, device_id=to, device_id_type=MESH))
        return i

    def granted(self, i, takes=None):
        on(takes, lambda: pl.semaphore_wait(self.free.at[i], 1))

    def finish(self):
        for k in range(len(self.sent)):
            self.left(k)


class Loads:
    def __init__(self, sems):
        self.sems, self.moves = sems, []

    def copy(self, src, dst):
        move = pltpu.make_async_copy(src, dst, self.sems.at[len(self.moves)])
        move.start()
        self.moves.append([move, False])
        return len(self.moves) - 1

    def wait(self, *ks):
        for k in ks:
            if not self.moves[k][1]:
                self.moves[k][0].wait()
                self.moves[k][1] = True

    def finish(self):
        self.wait(*range(len(self.moves)))


class Flow:
    def __init__(self):
        self.gens, self.waits, self.at = {}, {}, 0

    def step(self, name):
        self.waits[name] = next(self.gens[name], None)
        return self.waits[name] is not None

    def start(self, name, gen, held=False):
        self.gens[name] = gen
        self.step(name)

    def release(self, *names):
        pass

    def tick(self):
        for name in PLAN[self.at] if self.at < len(PLAN) else ():
            self.step(name)
        self.at += 1

    def need(self, *names):
        for name in names:
            while self.step(name):
                pass

    def finish(self):
        self.tick()
        live = list(self.gens)
        while live:
            live = [name for name in live if self.step(name)]


def gathered(links, way, shard, buf, dim, size, bit, to_y, to_bit, to_core, owns):
    def rows(ref, start, count):
        return part(ref, dim, pl.multiple_of(start, 16), count)

    near, own = buf.at[1], None
    if way == "y":
        k = links.copy(shard, near, to_y)
        yield (k,)
        if to_core is not None:
            own = links.copy(shard, buf.at[2], to_core)
            owns.append(own)
        links.arrived(k)
        ks = first = ()
    elif len(bit) == 1:
        half = size // 2
        k = links.copy(rows(shard, bit[0] * half, half), rows(near, bit[0] * half, half), to_y)
        yield (k,)
        if to_core is not None:
            own = links.copy(shard, buf.at[2], to_core)
            owns.append(own)
        links.arrived(k)
        piece = rows(near, bit[0] * half, half)
        ks, first = (links.copy(piece, piece, to_bit[0]),), ()
    else:
        quarter = size // 4
        at = (2 * bit[1] + bit[0]) * quarter
        over_x = (2 * bit[1] + 1 - bit[0]) * quarter
        over_z = (2 - 2 * bit[1] + bit[0]) * quarter
        k = links.copy(rows(shard, at, quarter), rows(near, at, quarter), to_y)
        yield (k,)
        if to_core is not None:
            own = links.copy(shard, buf.at[2], to_core)
            owns.append(own)
        links.arrived(k)
        piece = rows(near, at, quarter)
        by_x, by_z = first = links.copy(piece, piece, to_bit[0]), links.copy(piece, piece, to_bit[1])
        yield (by_x, by_z)
        links.arrived(by_x)
        piece = rows(near, over_x, quarter // 2)
        second = links.copy(piece, piece, to_bit[1])
        links.arrived(by_z)
        piece = rows(near, over_z + quarter // 2, quarter // 2)
        ks = (links.copy(piece, piece, to_bit[0]), second)
    if ks:
        yield ks
    for k in ks:
        links.arrived(k)
    if to_core is None:
        for k in ks + first:
            links.left(k)
        return
    k = links.copy(near, buf.at[3], to_core)
    yield (k, own)
    links.arrived(own)
    links.arrived(k)


def reduced(links, loads, acc, dim, base, size, stages, bufs, out, ahead, line):
    lo, n, spans = base, size, []
    two = any(kind == "slot" for kind, _, _ in stages)

    def rows(ref, start, count, slots=False):
        return part(ref, dim + 1 if slots else dim, start if isinstance(start, int) else pl.multiple_of(start, 16), count)

    for (kind, to, bit), buf in zip(stages, bufs):
        if kind == "slot":
            k = links.copy(rows(acc.at[1], lo, n), buf, to)
            acc, two = acc.at[0], False
            mine = rows(acc, lo, n)
        elif kind == "half":
            half = n // 2
            there, here = lo + (1 - bit) * half, lo + bit * half
            if two:
                early = links.copy(rows(acc.at[ahead], there, half), buf.at[ahead], to)
                yield (early,)
                k = links.copy(rows(acc.at[1 - ahead], there, half), buf.at[1 - ahead], to)
            else:
                k = links.copy(rows(acc, there, half), buf, to)
            before = lo
            lo, n = here, half
            mine = rows(acc, lo, n, two)
        elif kind == "line":
            mine, (outer, across) = rows(acc, lo, n), line
            inner = jnp.logical_not(outer)

            def add(mine=mine, buf=buf):
                mine[...] = mine[...] + buf[...]

            k = links.copy(mine, buf, to, outer, inner)
            yield (k,)
            links.arrived(k)
            on(inner, add)
            free = links.give(across, inner)
            links.left(k)
            back = links.give(to, outer)
            links.granted(free, inner)
            k = links.copy(mine, buf, across, inner, inner)
            yield (k,)
            links.arrived(k)
            links.left(k)
            on(inner, add)
            links.granted(back, inner)
            k = links.copy(mine, mine, to, inner, outer)
            yield (k,)
            links.arrived(k)
            continue
        else:
            mine = rows(acc, lo, n)
            k = links.copy(mine, buf, to)
        yield (k,)
        if kind == "half" and two:
            links.arrived(early)
            links.left(early)
        links.arrived(k)
        if kind != "slot":
            links.left(k)
        if kind == "half":
            spans.append((to, before, links.give(to)))
        mine[...] = mine[...] + buf[...]
    for to, before, credit in reversed(spans):
        mine = rows(acc, lo, n)
        links.granted(credit)
        k = links.copy(mine, mine, to)
        yield (k,)
        links.arrived(k)
        lo, n = before, 2 * n
    for i, ref in enumerate(out):
        loads.copy(rows(acc, lo, n) if len(out) == 1 else part(acc.at[i], dim - 1, lo, n), part(ref, 0, lo, n))


def summed(links, terms, bufs, partners):
    for i, to in enumerate(partners):
        k = links.copy(terms.at[i], bufs.at[i], to)
        yield (k,)
        links.arrived(k)
        terms[i + 1] = terms[i] + bufs[i]


ORDER = {
    "d0": ("0yLs", 0, 4),
    "q0": ("1y0s", 0, 2),
    "d3": ("1y0s", 3, 4),
    "p2": ("cY01s", 2, 3),
    "p0": ("c1Y0s", 0, 3),
    "u1": ("y0Ls", 1, 2),
    "q1": ("y0Ls", 1, 2),
    "d1": ("0yLs", 1, 4),
    "p1": ("c0Y1s", 1, 3),
    "d2": ("1y0s", 2, 4),
    "u0": ("10ys", 0, 2),
    "o": ("01ys", 0, 1),
}
WAY = {"wq": "yxz", "wo": "y", "wu": "yxz", "wd": "yxz"}
SLOTS = (2, 0, 3, 1)
PLAN = (
    (), (), (), (), ("wq",), (), (), (), (), (), (), (), (), (), ("wo",), (), ("wo", "wu", "wd",), (), (), (), (),
    (), (), (), (), (), (), (), (), (), (), ("wu",), (), ("wd",), (), ("wu",), (), ("wd",), (), (), (), (), (), (),
    ("d0", "d3", "d1", "d2", "u0",), (), ("d0", "d3", "p2",), ("p0", "d1", "p1", "d2",), (), (), (), (), (), (),
    ("o",), ("u1", "u0",), (), (), ("d0",), (), (), ("p1", "d3", "p0",), (), ("o",), (), (), (), ("d0", "p2",), (),
    (), ("u1", "d1",), ("q0",), ("o", "u0", "d2", "d3", "d0", "p2", "u1", "q1",),
    ("d1", "s", "p1", "u0", "p0", "q0", "d2", "d3", "d0", "o", "s", "p2", "q1", "u1", "p1", "p0", "u0", "d3", "d1",
     "d0", "s", "q0", "d2", "o", "p2", "q1", "u1", "p1", "q0", "d2", "p0", "d3", "u0", "u1", "d1", "s", "p0", "o",
     "p2", "q1", "p1", "u0", "p0", "d1", "q0", "d2", "s", "p2", "o", "p1", "q1", "q0", "o", "u0", "p2", "p2", "p1",
     "p0", "p1", "q1", "p0", "q0",),
)


def stage_kinds(order, bits):
    kinds = []
    for letter in order:
        if letter == "y":
            kinds.append(("slot", 1))
        elif letter in "cY":
            kinds.append(("half", "cY".index(letter)))
        elif letter == "L":
            kinds += [("line", 3)] if bits > 2 else []
        elif letter in "01":
            kinds += [("half", 2 + int(letter))] if int(letter) < bits else []
        else:
            kinds += [("swap", 2 + i) for i in range(3 if "L" in order else 2, bits)]
    return kinds


def buffer_shapes(order, rows, shape, bits):
    kinds, out = stage_kinds(order, bits), []
    two = any(kind == "slot" for kind, _ in kinds)
    for kind, _ in kinds:
        if kind == "slot":
            two = False
        elif kind == "half":
            rows //= 2
        out.append(((2,) if two else ()) + shape(rows))
    return out


def scratch_list(T, D, HC, U, bits):
    L, heads, qb = 2 * T, 2 * HC // HEAD, 2 * T // BLOCK
    blocks = sum(min(i, LEFT) + 1 for i in range(qb))
    kd = POOL * D
    out = [
        ("xb", (T, D), BF16),
        ("nrm", (L, D), BF16),
        ("wq", (2, 3, D, HC), BF16),
        ("wqt", (6 * HC, D), BF16),
        ("wo", (4, HC, D), BF16),
        ("wu", (4, D, U), BF16),
        ("wd", (4, U, D), BF16),
        ("wp", (kd, D), BF16),
        ("pg", (T // POOL, D), BF16),
        ("cos", (HEAD // 2, L), F32),
        ("sin", (HEAD // 2, L), F32),
        ("qxt", (heads, 2 * HEAD, L), BF16),
        ("kt", (heads, HEAD, L), BF16),
        ("vt", (heads, HEAD, L), BF16),
        ("kx", (heads, L, 2 * HEAD), BF16),
        ("vx", (heads, L, 2 * HEAD), BF16),
        ("probs", (heads, blocks * BLOCK, BLOCK), BF16),
        ("rl", (8, L), F32),
        ("ot", (2 * HC, L), BF16),
        ("otf", (4 * HC, T), BF16),
        ("gox", (heads, 2 * HEAD, L), BF16),
        ("gpt", (6 * HC, L), BF16),
        ("h1", (T, D), F32),
        ("h2", (D // 128, T + 8, 128), F32),
        ("g2t", (D // 128, T + 8, 128), F32),
        ("rim", (D // 128, 8, 128), F32),
        ("n2", (T, D), BF16),
        ("act", (T, U), BF16),
        ("gpre", (T, U), BF16),
        ("gn", (T, D), F32),
        ("gatt", (L, D), BF16),
        ("dk", (HEAD, L), F32),
        ("dv", (HEAD, L), F32),
        ("dq", (HEAD, L), F32),
        ("gd", (4, U, D), BF16),
        ("gu", (4, D, U), BF16),
        ("go", (2, HC, D), BF16),
        ("cd", (2, U, D), BF16),
        ("cu", (2, D, U), BF16),
        ("sc0", (WINDOW * BLOCK, BLOCK), F32),
        ("sc1", (WINDOW * BLOCK, BLOCK), F32),
        ("ds0", (WINDOW * BLOCK, BLOCK), BF16),
        ("ds1", (WINDOW * BLOCK, BLOCK), BF16),
        ("terms", (bits + 3, 8, D), F32),
        ("term_in", (bits + 2, 8, D), F32),
    ]
    rows_of = {"d": U, "u": D, "o": HC, "q": D, "p": kd}
    shape_of = {
        "d": lambda n: (n, D),
        "u": lambda n: (n, U),
        "o": lambda n: (n, D),
        "q": lambda n: (3, n, HC),
        "p": lambda n: (n, D),
    }
    for name, (order, _, parts) in ORDER.items():
        shapes = buffer_shapes(order, rows_of[name[0]] // parts, shape_of[name[0]], bits)
        out += [(f"in_{name}_{i}", shape, BF16) for i, shape in enumerate(shapes)]
    return out


def kernel(bits, names, *refs):
    s = SimpleNamespace(**dict(zip(names, refs)))
    T, D = s.xb.shape
    HC, U = s.wo.shape[1], s.wu.shape[2]
    L, QB = 2 * T, 2 * T // BLOCK
    half_head = HEAD // 2
    places, _ = result_rows(T, D, HC, U)
    RC = 32
    loads = Loads(s.load_sems)

    d, t = lax.axis_index("dp"), lax.axis_index("tensor")
    c, y = t % 2, t // 2
    to_core, to_y = (d, t + 1 - 2 * c), (d, t + 2 - 4 * y)
    bit = [(d // (1 << i)) % 2 for i in range(bits)]
    to_bit = [(d + (1 - 2 * bit[i]) * (1 << i), t) for i in range(bits)]
    partners = [to_core, to_y] + to_bit
    outer, across = None, None
    if bits > 2:
        outer = bit[1] == bit[2]
        across = (d + (1 - 2 * bit[1]) * 2 + (1 - 2 * bit[2]) * 4, t)
    links, flow = Links(s.send_sems, s.recv_sems, s.free_sems, partners), Flow()
    sides = [c, y] + bit
    tick = flow.tick

    def start_sum(name, acc, dim, held=False, ahead=1):
        order, piece, parts = ORDER[name]
        size = {"d": U, "u": D, "o": HC, "q": D, "p": POOL * D}[name[0]] // parts
        at, rows = places[name[0]]
        if name[0] == "q":
            out = [s.low_out.at[at : at + rows, i * HC : (i + 1) * HC] for i in range(3)]
        else:
            out = [s.low_out.at[at : at + rows, :]]
        stages = [(kind, partners[i], sides[i]) for kind, i in stage_kinds(order, bits)]
        bufs = [getattr(s, f"in_{name}_{i}") for i in range(len(stages))]
        flow.start(name, reduced(links, loads, acc, dim, piece * size, size, stages, bufs, out, ahead, (outer, across)), held)

    mine = pl.multiple_of(c * T, T)
    theirs = pl.multiple_of((1 - c) * T, T)

    in_x = loads.copy(s.tokens, s.xb)
    in_q = loads.copy(s.w_qkv, s.wq.at[0])
    in_pool = loads.copy(s.w_pool, s.wp)
    in_pg = loads.copy(s.pooled_grad, s.pg)
    in_out = loads.copy(s.w_out, s.wo.at[0])
    in_up = loads.copy(s.w_up, s.wu.at[0])
    in_down = loads.copy(s.w_down, s.wd.at[0])

    barrier = pltpu.get_barrier_semaphore()
    greeted = partners + ([across] if bits > 2 else [])
    for to in greeted:
        pl.semaphore_signal(barrier, inc=1, device_id=to, device_id_type=MESH)
    pl.semaphore_wait(barrier, len(greeted))

    owns = {"wq": [], "wo": [], "wu": [], "wd": []}

    def get(name, shard, buf, dim, size, core):
        flow.start(name, gathered(links, WAY[name], shard, buf, dim, size, bit, to_y, to_bit, core, owns[name]))

    get("wq", s.w_qkv, s.wq, 1, D, None)
    get("wo", s.w_out, s.wo, 0, HC, to_core)
    get("wu", s.w_up, s.wu, 0, D, to_core)
    get("wd", s.w_down, s.wd, 0, U, to_core)

    gain_one, gain_two = s.gain_one[...], s.gain_two[...]
    loads.wait(in_x)
    for r in range(0, T, RC):
        x = s.xb[r : r + RC, :].astype(F32)
        scale = lax.rsqrt(jnp.mean(x * x, axis=1, keepdims=True) + EPS)
        s.nrm[pl.ds(pl.multiple_of(mine + r, RC), RC), :] = (x * scale * gain_one).astype(BF16)
    own_rows = s.nrm.at[pl.ds(mine, T), :]
    sent_norm = links.copy(own_rows, own_rows, to_core)

    starts, ends, total = [], [], 0
    for j in range(4):
        starts.append(total)
        total = total + s.lengths[y, j]
        ends.append(total)

    def kept(j):
        p = mine + POOL * lax.broadcasted_iota(jnp.int32, (T // POOL, 1), 0) + j
        bad = (p - 1) <= 0
        for e in ends[:3]:
            bad = bad | ((p >= e) & (p - 1 <= e))
        return jnp.logical_not(bad)

    loads.wait(in_q)
    cos_in, sin_in = s.angles[2], s.angles[3]
    for i in range(L // 128):
        cos_of, sin_of = s.angles[0, :, i : i + 1], s.angles[1, :, i : i + 1]
        s.cos[:, i * 128 : (i + 1) * 128] = cos_of * cos_in - sin_of * sin_in
        s.sin[:, i * 128 : (i + 1) * 128] = sin_of * cos_in + cos_of * sin_in
    row = lax.broadcasted_iota(jnp.int32, (HEAD, L), 0)
    pos = lax.broadcasted_iota(jnp.int32, (HEAD, L), 1)
    same = jnp.zeros((HEAD, L), F32)
    for j in range(4):
        same = jnp.where((row == j) & (pos >= starts[j]) & (pos < ends[j]), 1.0, same)
    key_rows_doc = same.astype(BF16)
    query_rows_doc = jnp.where(row < 4, BIG * (same - 1.0), 0.0).astype(BF16)
    value_rows = jnp.where(row < 2, -1.0, 0.0).astype(BF16)
    for h in range(4):
        s.qxt[h, HEAD : 2 * HEAD, :] = query_rows_doc

    def turn_weights(slot):
        for i in range(3):
            s.wqt[(3 * slot + i) * HC : (3 * slot + i + 1) * HC, :] = s.wq[slot, i].T

    def project(slot, start):
        for j in range(0, T, BLOCK):
            cols = pl.ds(pl.multiple_of(start + j, BLOCK), BLOCK)
            cosine, sine = s.cos[:, cols], s.sin[:, cols]
            r = dot(s.wqt[3 * slot * HC : 3 * (slot + 1) * HC, :], s.nrm[cols, :], 1, 1)
            for i in range(3):
                for h in range(2):
                    u = r[i * HC + h * HEAD : i * HC + (h + 1) * HEAD, :]
                    head = 2 * slot + h
                    if i == 2:
                        s.vt[head, :, cols] = u.astype(BF16)
                        continue
                    a, b = u[:half_head], u[half_head:]
                    turned = jnp.concatenate([a * cosine - b * sine, a * sine + b * cosine], axis=0)
                    if i == 0:
                        s.qxt[head, 0:HEAD, cols] = (turned * HEAD**-0.5).astype(BF16)
                    else:
                        s.kt[head, :, cols] = turned.astype(BF16)

    def turn_keys(head):
        s.kx[head] = jnp.concatenate([s.kt[head], key_rows_doc], axis=0).T
        s.vx[head] = jnp.concatenate([s.vt[head], value_rows], axis=0).T

    turn_weights(0)
    project(0, mine)
    tick()

    loads.wait(in_pool, in_pg)
    s.g2t[:, 0:8, :] = jnp.zeros((D // 128, 8, 128), F32)
    s.g2t[:, T : T + 8, :] = jnp.zeros((D // 128, 8, 128), F32)
    for j in range(POOL):
        grad_shift = dot(s.pg[...], s.wp[j * D : (j + 1) * D, :], 1, 1)
        put_wide(s.g2t, 8 - (POOL - 1) + j, T // POOL, jnp.where(kept(j), grad_shift, 0.0), POOL)
    sent_rim = links.copy(s.g2t.at[:, 0:8, :], s.rim, to_core)

    tick()
    links.arrived(sent_norm)
    project(0, theirs)
    tick()
    turn_keys(0)
    turn_keys(1)
    tick()

    def window(qb):
        first = max(0, qb - LEFT)
        blocks = qb - first + 1
        offset = sum(min(i, LEFT) + 1 for i in range(qb)) * BLOCK
        return first * BLOCK, blocks, offset, slice(qb * BLOCK, (qb + 1) * BLOCK)

    def score(head, qb, i, into):
        first, blocks, _, q = window(qb)
        rows = slice(i * CHUNK, (i + 1) * CHUNK)
        scores = dot(s.kx[head, first + rows.start : first + rows.stop, :], s.qxt[head, :, q])
        below = rows.start - (blocks - 1) * BLOCK
        if below >= 0:
            ki = lax.broadcasted_iota(jnp.int32, (CHUNK, BLOCK), 0) + below
            qi = lax.broadcasted_iota(jnp.int32, (CHUNK, BLOCK), 1)
            scores = jnp.where(ki <= qi, scores, NEG)
        into[rows, :] = scores
        return jnp.max(scores.reshape(CHUNK // 8, 8, BLOCK), axis=0)

    def attend(head):
        order = list(range(1, QB)) + [0]
        pieces = [window(qb)[1] * BLOCK // CHUNK for qb in order]
        bufs = (s.sc0, s.sc1)
        tops = [score(head, order[0], i, bufs[0]) for i in range(pieces[0])]
        for at, qb in enumerate(order):
            first, blocks, offset, q = window(qb)
            now, later = bufs[at % 2], bufs[(at + 1) % 2]
            top = jnp.max(functools.reduce(jnp.maximum, tops), axis=0, keepdims=True)
            more = pieces[at + 1] if at + 1 < QB else 0
            tops, total = [], jnp.zeros((8, BLOCK), F32)
            for i in range(pieces[at]):
                while len(tops) < (i + 1) * more // pieces[at]:
                    tops.append(score(head, order[at + 1], len(tops), later))
                e = jnp.exp(now[i * CHUNK : (i + 1) * CHUNK, :] - top)
                total = total + jnp.sum(e.reshape(CHUNK // 8, 8, BLOCK), axis=0)
                s.probs[head, offset + i * CHUNK : offset + (i + 1) * CHUNK, :] = e.astype(BF16)
            inverse = 1.0 / jnp.sum(total, axis=0, keepdims=True)
            s.rl[head : head + 1, q] = inverse
            low = s.probs[head, offset : offset + blocks * BLOCK, :]
            out = dot(s.vt[head, :, first : first + blocks * BLOCK], low) * inverse
            s.ot[head * HEAD : (head + 1) * HEAD, q] = out.astype(BF16)
            tick()

    def send_heads(slot):
        rows = slice(slot * HC, (slot + 1) * HC)
        s.otf[rows, :] = s.ot[rows, pl.ds(mine, T)]
        return links.copy(
            s.ot.at[rows, pl.ds(theirs, T)],
            s.otf.at[(2 + slot) * HC : (3 + slot) * HC, :],
            to_core,
        )

    attend(0)
    attend(1)
    sent_heads = [send_heads(0)]
    flow.need("wq")
    turn_weights(1)
    project(1, mine)
    tick()
    project(1, theirs)
    turn_keys(2)
    turn_keys(3)
    tick()
    attend(2)
    attend(3)
    sent_heads.append(send_heads(1))
    tick()
    flow.need("wo")
    loads.wait(in_out)
    for k in sent_heads:
        links.arrived(k)

    for j in range(0, T, BLOCK):
        out = dot(s.otf[:, j : j + BLOCK], s.wo[...].reshape(4 * HC, D), 0, 0)
        for r in range(j, j + BLOCK, RC):
            rows = slice(r, r + RC)
            h = out[r - j : r - j + RC, :] + s.xb[rows, :].astype(F32)
            s.h1[rows, :] = h
            put_wide(s.h2, 8 + r, RC, h)
            scale = lax.rsqrt(jnp.mean(h * h, axis=1, keepdims=True) + EPS)
            s.n2[rows, :] = (h * scale * gain_two).astype(BF16)
    links.arrived(sent_rim)
    tail = lax.broadcasted_iota(jnp.int32, (D // 128, 8, 128), 1) >= 8 - (POOL - 1)
    s.g2t[:, T : T + 8, :] = s.g2t[:, T : T + 8, :] + jnp.where(tail, s.rim[...], 0.0)
    for r in range(0, T, RC):
        branch = wide(s.g2t, 8 + r, RC).astype(BF16)
        s.gatt[pl.ds(pl.multiple_of(mine + r, RC), RC), :] = branch
    tick()
    loads.wait(in_up, in_down)

    root = math.sqrt(2.0 / math.pi)

    def feed_forward(slot, first):
        def one_block(i, carry):
            j = pl.multiple_of(i * BLOCK, BLOCK)
            block, at = pl.ds(j, BLOCK), pl.multiple_of(8 + j, 8)
            v = dot(s.n2[block, :], s.wu[slot])
            grad_act = dot(s.gatt[pl.ds(pl.multiple_of(mine + j, BLOCK), BLOCK), :], s.wd[slot], 1, 1)
            for r in range(0, BLOCK, RC):
                rows = pl.ds(pl.multiple_of(j + r, RC), RC)
                u = v[r : r + RC, :]
                square = u * u
                th = jnp.tanh(u * (root + (root * 0.044715) * square))
                up = 0.5 + 0.5 * th
                slope = up + (u * (up - up * th)) * (root + (root * 3 * 0.044715) * square)
                s.act[rows, :] = (u * up).astype(BF16)
                s.gpre[rows, :] = (grad_act[r : r + RC, :] * slope).astype(BF16)
            put_wide(s.h2, at, BLOCK, wide(s.h2, at, BLOCK) + dot(s.act[block, :], s.wd[slot]))
            grad_normed = dot(s.gpre[block, :], s.wu[slot], 1, 1)
            s.gn[block, :] = grad_normed if first else s.gn[block, :] + grad_normed
            return carry

        lax.fori_loop(0, T // BLOCK, one_block, 0)
        tick()
        branch = s.gatt[pl.ds(mine, T), :]
        for j in range(0, U, BLOCK):
            s.gd[slot, j : j + BLOCK, :] = dot(s.act[:, j : j + BLOCK], branch, 0, 0).astype(BF16)
        tick()
        for j in range(0, D, BLOCK):
            s.gu[slot, j : j + BLOCK, :] = dot(s.n2[:, j : j + BLOCK], s.gpre[...], 0, 0).astype(BF16)
        tick()

    def to_other_core(slot):
        return (
            links.copy(s.gd.at[slot], s.cd.at[slot - 2], to_core),
            links.copy(s.gu.at[slot], s.cu.at[slot - 2], to_core),
        )

    def from_other_core(slot, sent):
        links.arrived(sent[0])
        s.gd[slot] = s.gd[slot] + s.cd[slot]
        links.arrived(sent[1])
        s.gu[slot] = s.gu[slot] + s.cu[slot]

    if SLOTS[0] == 3:
        flow.need("wu", "wd")
    else:
        links.arrived(owns["wu"][0])
        links.arrived(owns["wd"][0])
    shard_sums = {name: s.gd if name[0] == "d" else s.gu for name in ORDER if name[0] in "du"}
    ahead = SLOTS[1]
    early = [name for name in shard_sums if ahead == 1 or ORDER[name][0][0] != "y"]
    feed_forward(SLOTS[0], True)
    sent_one = to_other_core(SLOTS[0])
    feed_forward(SLOTS[1], False)
    from_other_core(SLOTS[1], sent_one)
    for name in early:
        start_sum(name, shard_sums[name].at[0:2], 0, True, ahead)
    flow.need("wu", "wd")
    feed_forward(SLOTS[2], False)
    sent_two = to_other_core(SLOTS[2])
    feed_forward(SLOTS[3], False)

    gain_grad_two = jnp.zeros((8, D), F32)
    for r in range(0, T, RC):
        rows = slice(r, r + RC)
        h, gn = s.h1[rows, :], s.gn[rows, :]
        scale = lax.rsqrt(jnp.mean(h * h, axis=1, keepdims=True) + EPS)
        e = gain_two * gn
        hs = h * scale
        grad = wide(s.g2t, 8 + r, RC) + scale * (e - hs * jnp.mean(e * hs, axis=1, keepdims=True))
        s.h1[rows, :] = grad
        s.gatt[pl.ds(pl.multiple_of(mine + r, RC), RC), :] = grad.astype(BF16)
        gain_grad_two = gain_grad_two + jnp.sum((gn * hs).reshape(RC // 8, 8, D), axis=0)
    own_rows = s.gatt.at[pl.ds(mine, T), :]
    sent_gatt = links.copy(own_rows, own_rows, to_core)
    sent_rim = links.copy(s.h2.at[:, T : T + 8, :], s.h2.at[:, 0:8, :], to_core)
    from_other_core(SLOTS[3], sent_two)
    flow.release(*early)
    for name in shard_sums:
        if name not in early:
            start_sum(name, shard_sums[name].at[0:2], 0)
    tick()

    block_square = jnp.zeros((8, D), F32)
    for r in range(0, T, RC):
        h = wide(s.h2, 8 + r, RC)
        block_square = block_square + jnp.sum((h * h).reshape(RC // 8, 8, D), axis=0)
    links.arrived(sent_rim)
    for j in range(POOL):
        rows = pl.ds(8 - (POOL - 1) + j, T // POOL, stride=POOL)
        taken = jnp.concatenate([s.h2[i, rows, :] for i in range(D // 128)], axis=1)
        s.n2[j * (T // POOL) : (j + 1) * (T // POOL), :] = jnp.where(kept(j), taken, 0.0).astype(BF16)
    pool_in = [s.n2[j * (T // POOL) : (j + 1) * (T // POOL), :] for j in range(POOL)]
    pooled = sum(dot(pool_in[j], s.wp[j * D : (j + 1) * D, :]) for j in range(POOL))
    pool_square = jnp.sum((pooled * pooled).reshape(T // POOL // 8, 8, D), axis=0)
    s.gpre[0 : T // POOL, :] = pooled.astype(BF16)
    out_pooled = loads.copy(s.gpre.at[0 : T // POOL, :], part(s.low_out, 0, *places["pooled"]))
    for j in range(POOL):
        s.wp[j * D : (j + 1) * D, :] = dot(pool_in[j], s.pg[...], 0, 0).astype(BF16)
    for name in (name for name in ORDER if name[0] == "p"):
        start_sum(name, s.wp, 0)
    tick()

    def grad_heads(start):
        for j in range(0, T, BLOCK):
            cols = pl.ds(pl.multiple_of(start + j, BLOCK), BLOCK)
            g = dot(s.wo[0:2].reshape(2 * HC, D), s.gatt[cols, :], 1, 1)
            line = lax.broadcasted_iota(jnp.int32, (HEAD, BLOCK), 0)
            for head in range(4):
                low = (g[head * HEAD : (head + 1) * HEAD] * s.rl[head : head + 1, cols]).astype(BF16)
                o = s.ot[head * HEAD : (head + 1) * HEAD, cols].astype(F32)
                delta = jnp.sum(low.astype(F32) * o, axis=0, keepdims=True)
                high = delta.astype(BF16).astype(F32)
                rest = jnp.where(line == 0, high, jnp.where(line == 1, delta - high, 0.0))
                s.gox[head, 0:HEAD, cols] = low
                s.gox[head, HEAD : 2 * HEAD, cols] = rest.astype(BF16)

    grad_heads(mine)
    links.arrived(sent_gatt)
    grad_heads(theirs)
    for slot in (1, 0):
        s.go[slot] = dot(s.ot[slot * HC : (slot + 1) * HC, :], s.gatt[...]).astype(BF16)
    start_sum("o", s.go, 0)
    tick()

    def grad_score(head, qb, i, into):
        first, _, offset, q = window(qb)
        rows = slice(i * BLOCK, (i + 1) * BLOCK)
        grads = dot(s.vx[head, first + rows.start : first + rows.stop, :], s.gox[head, :, q])
        probs = s.probs[head, offset + rows.start : offset + rows.stop, :]
        into[rows, :] = (probs.astype(F32) * grads).astype(BF16)

    def attend_back(head):
        slot, h = head // 2, head % 2
        bufs, seen = (s.ds0, s.ds1), set()
        for i in range(window(0)[1]):
            grad_score(head, 0, i, bufs[0])
        for qb in range(QB):
            first, blocks, offset, q = window(qb)
            now, later = bufs[qb % 2], bufs[(qb + 1) % 2]
            more, done = window(qb + 1)[1] if qb + 1 < QB else 0, 0
            s.dq[:, q] = dot(s.kt[head, :, first : first + blocks * BLOCK], now[0 : blocks * BLOCK, :])
            for i in range(blocks):
                while done < (i + 1) * more // blocks:
                    grad_score(head, qb + 1, done, later)
                    done += 1
                cols = slice(first + i * BLOCK, first + (i + 1) * BLOCK)
                probs = s.probs[head, offset + i * BLOCK : offset + (i + 1) * BLOCK, :]
                dk = dot(s.qxt[head, 0:HEAD, q], now[i * BLOCK : (i + 1) * BLOCK, :], 1, 1)
                dv = dot(s.gox[head, 0:HEAD, q], probs, 1, 1)
                s.dk[:, cols] = s.dk[:, cols] + dk if cols.start in seen else dk
                s.dv[:, cols] = s.dv[:, cols] + dv if cols.start in seen else dv
                seen.add(cols.start)
            tick()
        cosine, sine = s.cos[...], s.sin[...]
        for i, (ref, factor) in enumerate(((s.dq, HEAD**-0.5), (s.dk, 1.0))):
            a, b = ref[:half_head, :], ref[half_head:, :]
            turned = jnp.concatenate([a * cosine + b * sine, b * cosine - a * sine], axis=0) * factor
            start = (3 * slot + i) * HC + h * HEAD
            s.gpt[start : start + HEAD, :] = turned.astype(BF16)
        start = (3 * slot + 2) * HC + h * HEAD
        s.gpt[start : start + HEAD, :] = s.dv[...].astype(BF16)

    def grad_weights(slot):
        for i in range(3):
            g = dot(s.gpt[(3 * slot + i) * HC : (3 * slot + i + 1) * HC, :], s.nrm[...])
            s.wq[slot, i] = g.astype(BF16).T

    attend_back(2)
    attend_back(3)
    grad_weights(1)
    sums_q = [name for name in ORDER if name[0] == "q"]
    for name in sums_q:
        start_sum(name, s.wq, 1, True)
    attend_back(0)
    attend_back(1)
    grad_weights(0)
    flow.release(*sums_q)
    tick()

    for j in range(0, T, BLOCK):
        cols = pl.ds(pl.multiple_of(theirs + j, BLOCK), BLOCK)
        s.n2[j : j + BLOCK, :] = dot(s.gpt[:, cols], s.wqt[...], 0, 0).astype(BF16)
    sent_pn = links.copy(s.n2, s.act, to_core)
    for j in range(0, T, BLOCK):
        cols = pl.ds(pl.multiple_of(mine + j, BLOCK), BLOCK)
        s.gn[j : j + BLOCK, :] = dot(s.gpt[:, cols], s.wqt[...], 0, 0)
    tick()
    links.arrived(sent_pn)
    loads.wait(out_pooled)
    gain_grad_one = jnp.zeros((8, D), F32)
    for r in range(0, T, RC):
        rows = slice(r, r + RC)
        x, gn = s.xb[rows, :].astype(F32), s.gn[rows, :] + s.act[rows, :].astype(F32)
        scale = lax.rsqrt(jnp.mean(x * x, axis=1, keepdims=True) + EPS)
        e = gain_one * gn
        xs = x * scale
        grad = s.h1[rows, :] + scale * (e - xs * jnp.mean(e * xs, axis=1, keepdims=True))
        s.gpre[rows, :] = grad.astype(BF16)
        gain_grad_one = gain_grad_one + jnp.sum((gn * xs).reshape(RC // 8, 8, D), axis=0)
    loads.copy(s.gpre, part(s.low_out, 0, *places["gtok"]))

    line = lax.broadcasted_iota(jnp.int32, (8, D), 0)
    small = jnp.zeros((8, D), F32)
    for i, v in enumerate((gain_grad_one, gain_grad_two, block_square, pool_square)):
        v = jnp.sum(v, axis=0, keepdims=True)
        if i >= 2:
            v = jnp.sum(v, axis=1, keepdims=True)
        small = jnp.where(line == i, v, small)
    s.terms[0] = small
    flow.start("s", summed(links, s.terms, s.term_in, partners))
    flow.finish()
    loads.copy(s.terms.at[len(partners)], s.small_out)
    links.finish()
    loads.finish()


def result_rows(T, D, HC, U):
    sizes = {"p": POOL * D, "d": U, "u": D, "q": D, "o": HC, "pooled": T // POOL, "gtok": T}
    at, out = 0, {}
    for name, rows in sizes.items():
        out[name] = (at, rows)
        at += rows
    return out, at


def widen(places, block_scale, pool_scale, small, low, *refs):
    rms_block, rms_pool, gain_one, gain_two = refs[:4]
    results, wide_refs, taken, sems = dict(zip(places, refs[4:11])), dict(zip(places, refs[11:16])), refs[16], refs[17]
    loads, ks = Loads(sems), {}
    for name, (at, rows) in places.items():
        ks[name] = loads.copy(low.at[at : at + rows, :], taken.at[at : at + rows, :])
    rms_block[...] = jnp.sqrt(small[2:3, 0:1] * block_scale)
    rms_pool[...] = jnp.sqrt(small[3:4, 0:1] * pool_scale)
    gain_one[...] = small[0:1, :]
    gain_two[...] = small[1:2, :]
    for name, made in wide_refs.items():
        at, rows = places[name]
        loads.wait(ks[name])
        if name == "q":
            for i in range(3):
                width = made.shape[2]
                made[i] = taken[at : at + rows, i * width : (i + 1) * width].astype(F32)
        else:
            made[...] = taken[at : at + rows, :].astype(F32)
        loads.copy(made, results[name])
    for name in ("pooled", "gtok"):
        at, rows = places[name]
        loads.wait(ks[name])
        loads.copy(taken.at[at : at + rows, :], results[name])
    loads.finish()


IN_NAMES = (
    "tokens", "lengths", "w_qkv", "w_out", "w_up", "w_down", "w_pool",
    "gain_one", "gain_two", "pooled_grad", "angles",
)
OUT_NAMES = ("low_out", "small_out")


def tables(length):
    half, lanes = HEAD // 2, 128
    frequency = np.exp(-math.log(10000.0) * np.arange(half) / half)[:, None]
    group = frequency * (lanes * np.minimum(np.arange(lanes), length // lanes))
    within = frequency * np.arange(lanes)
    return np.stack([np.cos(group), np.sin(group), np.cos(within), np.sin(within)]).astype(np.float32)


def shards(tokens, lengths, w_qkv, w_out, w_up, w_down, w_pool, gain_one, gain_two, pooled_grad):
    T, D = tokens.shape
    HC, U = w_out.shape[0], w_up.shape[1]
    dp = lax.axis_size("dp")
    bits = dp.bit_length() - 1
    assert lax.axis_size("tensor") == 4 and lengths.shape == (2, 4) and dp == 1 << bits and bits > 0
    scratch = scratch_list(T, D, HC, U, bits)
    names = IN_NAMES + OUT_NAMES + tuple(n for n, _, _ in scratch) + ("send_sems", "recv_sems", "free_sems", "load_sems")
    hbm, vmem, smem = pl.BlockSpec(memory_space=pl.ANY), pl.BlockSpec(memory_space=pltpu.VMEM), pl.BlockSpec(memory_space=pltpu.SMEM)
    copies = 256 + 24 * bits
    places, total = result_rows(T, D, HC, U)
    low, small = pl.pallas_call(
        functools.partial(kernel, bits, names),
        out_shape=[jax.ShapeDtypeStruct((total, D), BF16), jax.ShapeDtypeStruct((8, D), F32)],
        in_specs=[hbm, smem, hbm, hbm, hbm, hbm, hbm, vmem, vmem, hbm, vmem],
        out_specs=[hbm] * 2,
        scratch_shapes=[pltpu.VMEM(shape, kind) for _, shape, kind in scratch]
        + [pltpu.SemaphoreType.DMA((copies,)), pltpu.SemaphoreType.DMA((copies,))]
        + [pltpu.SemaphoreType.REGULAR((160,)), pltpu.SemaphoreType.DMA((64,))],
        compiler_params=pltpu.CompilerParams(
            collective_id=0, has_side_effects=True, vmem_limit_bytes=64 * 2**20 - 2**16
        ),
    )(
        tokens, lengths, jnp.transpose(w_qkv, (1, 0, 2)), w_out, w_up, w_down, w_pool,
        gain_one.reshape(1, D), gain_two.reshape(1, D), pooled_grad, tables(2 * T),
    )
    group = dp * 4 * T * D
    one, line = jax.ShapeDtypeStruct((1, 1), F32), jax.ShapeDtypeStruct((1, D), F32)
    wide_shapes = [jax.ShapeDtypeStruct(s, F32) for s in ((POOL * D, D), (U, D), (D, U), (3, D, HC), (HC, D))]
    rms_block, rms_pool, grad_one, grad_two, gp, gd, gu, gq, go, pooled, gtok = pl.pallas_call(
        functools.partial(widen, places, 1.0 / group, POOL / group),
        out_shape=[one, one, line, line]
        + wide_shapes
        + [jax.ShapeDtypeStruct((T // POOL, D), BF16), jax.ShapeDtypeStruct((T, D), BF16)],
        in_specs=[vmem, hbm],
        out_specs=[vmem] * 4 + [hbm] * 7,
        scratch_shapes=[pltpu.VMEM(a.shape, F32) for a in wide_shapes]
        + [pltpu.VMEM((total, D), BF16), pltpu.SemaphoreType.DMA((14,))],
        compiler_params=pltpu.CompilerParams(vmem_limit_bytes=62 * 2**20),
    )(small, low)
    return (
        pooled,
        rms_block.reshape(()),
        rms_pool.reshape(()),
        gtok,
        jnp.transpose(gq, (1, 0, 2)),
        go,
        gu,
        gd,
        gp,
        grad_one.reshape(D),
        grad_two.reshape(D),
    )


def solution(mesh):
    rows = P(("dp", "tensor"), None)
    placed = (
        rows, P("dp", None), P(None, None, "tensor"), P("tensor", None), P(None, "tensor"),
        P("tensor", None), P(), P(), P(), rows,
    )
    return jax.shard_map(
        shards,
        mesh=mesh,
        in_specs=placed,
        out_specs=(
            rows, P(), P(), rows, P(None, None, "tensor"), P("tensor", None), P(None, "tensor"),
            P("tensor", None), P(), P(), P(),
        ),
        check_vma=False,
    )
```

```python
import functools
import math
from types import SimpleNamespace

import jax
import jax.numpy as jnp
import numpy as np
from jax import lax
from jax.experimental import pallas as pl
from jax.experimental.pallas import tpu as pltpu
from jax.sharding import PartitionSpec as P

HEAD = 64
POOL = 3
EPS = 1e-06
BIG = float(2**30)
NEG = -1000000000.0
BLOCK = 256
LEFT = 3
WINDOW = LEFT + 1
CHUNK = 128
F32, BF16 = jnp.float32, jnp.bfloat16
MESH = pl.DeviceIdType.MESH


def dot(a, b, ca=1, cb=0):
    return lax.dot_general(a, b, (((ca,), (cb,)), ((), ())), preferred_element_type=F32)


def part(ref, dim, start, count):
    index = [slice(None)] * len(ref.shape)
    index[dim] = pl.ds(start, count)
    return ref.at[tuple(index)]


def wide(ref, start, count):
    return jnp.concatenate([ref[i, pl.ds(start, count), :] for i in range(ref.shape[0])], axis=1)


def put_wide(ref, start, count, value, stride=None):
    for i in range(ref.shape[0]):
        ref[i, pl.ds(start, count, stride=stride), :] = value[:, i * 128 : (i + 1) * 128]


def on(condition, act):
    if condition is None:
        act()
    else:
        pl.when(condition)(act)


class Links:
    def __init__(self, send, recv, free, partners):
        self.send, self.recv, self.sent, self.partners = send, recv, [], partners
        self.free, self.freed = free, 0

    def copy(self, src, dst, to, sends=None, takes=None):
        k = len(self.sent)
        move = pltpu.make_async_remote_copy(
            src, dst, self.send.at[k], self.recv.at[k], device_id=to, device_id_type=MESH
        )
        on(sends, move.start)
        self.sent.append([move, False, False, sends, takes])
        return k

    def arrived(self, k):
        if not self.sent[k][2]:
            on(self.sent[k][4], self.sent[k][0].wait_recv)
            self.sent[k][2] = True

    def left(self, k):
        if not self.sent[k][1]:
            on(self.sent[k][3], self.sent[k][0].wait_send)
            self.sent[k][1] = True

    def give(self, to, gives=None):
        i = self.freed
        self.freed += 1
        on(gives, lambda: pl.semaphore_signal(self.free.at[i], inc=1, device_id=to, device_id_type=MESH))
        return i

    def granted(self, i, takes=None):
        on(takes, lambda: pl.semaphore_wait(self.free.at[i], 1))

    def finish(self):
        for k in range(len(self.sent)):
            self.left(k)


class Loads:
    def __init__(self, sems):
        self.sems, self.moves = sems, []

    def copy(self, src, dst):
        move = pltpu.make_async_copy(src, dst, self.sems.at[len(self.moves)])
        move.start()
        self.moves.append([move, False])
        return len(self.moves) - 1

    def wait(self, *ks):
        for k in ks:
            if not self.moves[k][1]:
                self.moves[k][0].wait()
                self.moves[k][1] = True

    def finish(self):
        self.wait(*range(len(self.moves)))


class Flow:
    def __init__(self):
        self.gens, self.waits, self.at = {}, {}, 0

    def step(self, name):
        self.waits[name] = next(self.gens[name], None)
        return self.waits[name] is not None

    def start(self, name, gen, held=False):
        self.gens[name] = gen
        self.step(name)

    def release(self, *names):
        pass

    def tick(self):
        for name in PLAN[self.at] if self.at < len(PLAN) else ():
            self.step(name)
        self.at += 1

    def need(self, *names):
        for name in names:
            while self.step(name):
                pass

    def finish(self):
        self.tick()
        live = list(self.gens)
        while live:
            live = [name for name in live if self.step(name)]


def gathered(links, way, shard, buf, dim, size, bit, to_y, to_bit, to_core, owns):
    def rows(ref, start, count):
        return part(ref, dim, pl.multiple_of(start, 16), count)

    near, own = buf.at[1], None
    if way == "y":
        k = links.copy(shard, near, to_y)
        yield (k,)
        if to_core is not None:
            own = links.copy(shard, buf.at[2], to_core)
            owns.append(own)
        links.arrived(k)
        ks = first = ()
    elif len(bit) == 1:
        half = size // 2
        k = links.copy(rows(shard, bit[0] * half, half), rows(near, bit[0] * half, half), to_y)
        yield (k,)
        if to_core is not None:
            own = links.copy(shard, buf.at[2], to_core)
            owns.append(own)
        links.arrived(k)
        piece = rows(near, bit[0] * half, half)
        ks, first = (links.copy(piece, piece, to_bit[0]),), ()
    else:
        quarter = size // 4
        at = (2 * bit[1] + bit[0]) * quarter
        over_x = (2 * bit[1] + 1 - bit[0]) * quarter
        over_z = (2 - 2 * bit[1] + bit[0]) * quarter
        k = links.copy(rows(shard, at, quarter), rows(near, at, quarter), to_y)
        yield (k,)
        if to_core is not None:
            own = links.copy(shard, buf.at[2], to_core)
            owns.append(own)
        links.arrived(k)
        piece = rows(near, at, quarter)
        by_x, by_z = first = links.copy(piece, piece, to_bit[0]), links.copy(piece, piece, to_bit[1])
        yield (by_x, by_z)
        links.arrived(by_x)
        piece = rows(near, over_x, quarter // 2)
        second = links.copy(piece, piece, to_bit[1])
        links.arrived(by_z)
        piece = rows(near, over_z + quarter // 2, quarter // 2)
        ks = (links.copy(piece, piece, to_bit[0]), second)
    if ks:
        yield ks
    for k in ks:
        links.arrived(k)
    if to_core is None:
        for k in ks + first:
            links.left(k)
        return
    k = links.copy(near, buf.at[3], to_core)
    yield (k, own)
    links.arrived(own)
    links.arrived(k)


def reduced(links, loads, acc, dim, base, size, stages, bufs, out, ahead, line):
    lo, n, spans = base, size, []
    two = any(kind == "slot" for kind, _, _ in stages)

    def rows(ref, start, count, slots=False):
        return part(ref, dim + 1 if slots else dim, start if isinstance(start, int) else pl.multiple_of(start, 16), count)

    for (kind, to, bit), buf in zip(stages, bufs):
        if kind == "slot":
            k = links.copy(rows(acc.at[1], lo, n), buf, to)
            acc, two = acc.at[0], False
            mine = rows(acc, lo, n)
        elif kind == "half":
            half = n // 2
            there, here = lo + (1 - bit) * half, lo + bit * half
            if two:
                early = links.copy(rows(acc.at[ahead], there, half), buf.at[ahead], to)
                yield (early,)
                k = links.copy(rows(acc.at[1 - ahead], there, half), buf.at[1 - ahead], to)
            else:
                k = links.copy(rows(acc, there, half), buf, to)
            before = lo
            lo, n = here, half
            mine = rows(acc, lo, n, two)
        elif kind == "line":
            mine, (outer, across) = rows(acc, lo, n), line
            inner = jnp.logical_not(outer)

            def add(mine=mine, buf=buf):
                mine[...] = mine[...] + buf[...]

            k = links.copy(mine, buf, to, outer, inner)
            yield (k,)
            links.arrived(k)
            on(inner, add)
            free = links.give(across, inner)
            links.left(k)
            back = links.give(to, outer)
            links.granted(free, inner)
            k = links.copy(mine, buf, across, inner, inner)
            yield (k,)
            links.arrived(k)
            links.left(k)
            on(inner, add)
            links.granted(back, inner)
            k = links.copy(mine, mine, to, inner, outer)
            yield (k,)
            links.arrived(k)
            continue
        else:
            mine = rows(acc, lo, n)
            k = links.copy(mine, buf, to)
        yield (k,)
        if kind == "half" and two:
            links.arrived(early)
            links.left(early)
        links.arrived(k)
        if kind != "slot":
            links.left(k)
        if kind == "half":
            spans.append((to, before, links.give(to)))
        mine[...] = mine[...] + buf[...]
    for to, before, credit in reversed(spans):
        mine = rows(acc, lo, n)
        links.granted(credit)
        k = links.copy(mine, mine, to)
        yield (k,)
        links.arrived(k)
        lo, n = before, 2 * n
    for i, ref in enumerate(out):
        loads.copy(rows(acc, lo, n) if len(out) == 1 else part(acc.at[i], dim - 1, lo, n), part(ref, 0, lo, n))


def summed(links, terms, bufs, partners):
    for i, to in enumerate(partners):
        k = links.copy(terms.at[i], bufs.at[i], to)
        yield (k,)
        links.arrived(k)
        terms[i + 1] = terms[i] + bufs[i]


ORDER = {
    "d0": ("0yLs", 0, 4),
    "d1": ("0yLs", 1, 4),
    "d2": ("1y0s", 2, 4),
    "d3": ("1y0s", 3, 4),
    "u0": ("1y0s", 0, 4),
    "u1": ("0yLs", 1, 4),
    "u2": ("1y0s", 2, 4),
    "u3": ("y0Ls", 3, 4),
    "p0": ("c1Y0s", 0, 3),
    "p1": ("c0YLs", 1, 3),
    "p2": ("cY01s", 2, 3),
    "o": ("0yLs", 0, 1),
    "q0": ("1y0s", 0, 2),
    "q1": ("y0Ls", 1, 2),
}
WAY = {"wq": "yxz", "wo": "y", "wu": "yxz", "wd": "yxz"}
SLOTS = (2, 0, 3, 1)
PLAN = (
    (), (), (), (), ("wq",), (), (), (), (), (), (), (), (), (), ("wo",), (), ("wo", "wu", "wd",), (), (), (), (),
    (), (), (), (), (), (), (), (), (), (), ("wu",), (), ("wd",), (), ("wu",), (), ("wd",), (), (), (), (), (), (),
    ("d0", "d2", "d1", "d3", "u0", "u1", "u2",), (), ("d0", "d2", "p0",), ("p1", "u3", "d1", "p2", "d3",), (), (),
    ("u1", "u0",), (), ("d0", "o", "u2",), (), (), ("d2",), (), (), ("d1", "p1", "p0",), (), (), ("u3", "d0",), (),
    ("p2", "o",), ("d2", "d1", "d3",), (), (), (), ("u1", "d0",), (), ("p2", "u0", "d3", "u3",), ("q0", "d2", "u2",),
    ("d1", "u1", "d0", "p1", "u0", "p2", "p0", "d2", "d3", "u2", "u3", "q0",),
    ("s", "q1", "d1", "u1", "d0", "p1", "o", "p0", "d3", "u0", "q0", "d2", "s", "p2", "q1", "u3", "u2", "o", "d1",
     "p1", "u0", "u1", "q0", "s", "p0", "d3", "u3", "p2", "o", "u2", "q1", "p1", "u1", "p0", "u0", "q0", "p2", "s",
     "p1", "o", "q1", "p0", "q0", "u2", "s", "p2", "q1", "p1", "p2", "p1", "o", "p0", "p0", "q1", "q0",),
)


def stage_kinds(order, bits):
    kinds = []
    for letter in order:
        if letter == "y":
            kinds.append(("slot", 1))
        elif letter in "cY":
            kinds.append(("half", "cY".index(letter)))
        elif letter == "L":
            kinds += [("line", 3)] if bits > 2 else []
        elif letter in "01":
            kinds += [("half", 2 + int(letter))] if int(letter) < bits else []
        else:
            kinds += [("swap", 2 + i) for i in range(3 if "L" in order else 2, bits)]
    return kinds


def buffer_shapes(order, rows, shape, bits):
    kinds, out = stage_kinds(order, bits), []
    two = any(kind == "slot" for kind, _ in kinds)
    for kind, _ in kinds:
        if kind == "slot":
            two = False
        elif kind == "half":
            rows //= 2
        out.append(((2,) if two else ()) + shape(rows))
    return out


def scratch_list(T, D, HC, U, bits):
    L, heads, qb = 2 * T, 2 * HC // HEAD, 2 * T // BLOCK
    blocks = sum(min(i, LEFT) + 1 for i in range(qb))
    kd = POOL * D
    out = [
        ("xb", (T, D), BF16),
        ("nrm", (L, D), BF16),
        ("wq", (2, 3, D, HC), BF16),
        ("wqt", (6 * HC, D), BF16),
        ("wo", (4, HC, D), BF16),
        ("wu", (4, D, U), BF16),
        ("wd", (4, U, D), BF16),
        ("wp", (kd, D), BF16),
        ("pg", (T // POOL, D), BF16),
        ("cos", (HEAD // 2, L), F32),
        ("sin", (HEAD // 2, L), F32),
        ("qxt", (heads, 2 * HEAD, L), BF16),
        ("kt", (heads, HEAD, L), BF16),
        ("vt", (heads, HEAD, L), BF16),
        ("kx", (heads, L, 2 * HEAD), BF16),
        ("vx", (heads, L, 2 * HEAD), BF16),
        ("probs", (heads, blocks * BLOCK, BLOCK), BF16),
        ("rl", (8, L), F32),
        ("ot", (2 * HC, L), BF16),
        ("otf", (4 * HC, T), BF16),
        ("gox", (heads, 2 * HEAD, L), BF16),
        ("gpt", (6 * HC, L), BF16),
        ("h1", (T, D), F32),
        ("h2", (D // 128, T + 8, 128), F32),
        ("g2t", (D // 128, T + 8, 128), F32),
        ("rim", (D // 128, 8, 128), F32),
        ("n2", (T, D), BF16),
        ("act", (T, U), BF16),
        ("gpre", (T, U), BF16),
        ("gn", (T, D), F32),
        ("gatt", (L, D), BF16),
        ("dk", (HEAD, L), F32),
        ("dv", (HEAD, L), F32),
        ("dq", (HEAD, L), F32),
        ("gd", (4, U, D), BF16),
        ("gu", (4, D, U), BF16),
        ("go", (2, HC, D), BF16),
        ("cd", (2, U, D), BF16),
        ("cu", (2, D, U), BF16),
        ("sc0", (WINDOW * BLOCK, BLOCK), F32),
        ("sc1", (WINDOW * BLOCK, BLOCK), F32),
        ("ds0", (WINDOW * BLOCK, BLOCK), BF16),
        ("ds1", (WINDOW * BLOCK, BLOCK), BF16),
        ("terms", (bits + 3, 8, D), F32),
        ("term_in", (bits + 2, 8, D), F32),
    ]
    rows_of = {"d": U, "u": D, "o": HC, "q": D, "p": kd}
    shape_of = {
        "d": lambda n: (n, D),
        "u": lambda n: (n, U),
        "o": lambda n: (n, D),
        "q": lambda n: (3, n, HC),
        "p": lambda n: (n, D),
    }
    for name, (order, _, parts) in ORDER.items():
        shapes = buffer_shapes(order, rows_of[name[0]] // parts, shape_of[name[0]], bits)
        out += [(f"in_{name}_{i}", shape, BF16) for i, shape in enumerate(shapes)]
    return out


def kernel(bits, names, *refs):
    s = SimpleNamespace(**dict(zip(names, refs)))
    T, D = s.xb.shape
    HC, U = s.wo.shape[1], s.wu.shape[2]
    L, QB = 2 * T, 2 * T // BLOCK
    half_head = HEAD // 2
    places, _ = result_rows(T, D, HC, U)
    RC = 32
    loads = Loads(s.load_sems)

    d, t = lax.axis_index("dp"), lax.axis_index("tensor")
    c, y = t % 2, t // 2
    to_core, to_y = (d, t + 1 - 2 * c), (d, t + 2 - 4 * y)
    bit = [(d // (1 << i)) % 2 for i in range(bits)]
    to_bit = [(d + (1 - 2 * bit[i]) * (1 << i), t) for i in range(bits)]
    partners = [to_core, to_y] + to_bit
    outer, across = None, None
    if bits > 2:
        outer = bit[1] == bit[2]
        across = (d + (1 - 2 * bit[1]) * 2 + (1 - 2 * bit[2]) * 4, t)
    links, flow = Links(s.send_sems, s.recv_sems, s.free_sems, partners), Flow()
    sides = [c, y] + bit
    tick = flow.tick

    def start_sum(name, acc, dim, held=False, ahead=1):
        order, piece, parts = ORDER[name]
        size = {"d": U, "u": D, "o": HC, "q": D, "p": POOL * D}[name[0]] // parts
        at, rows = places[name[0]]
        if name[0] == "q":
            out = [s.low_out.at[at : at + rows, i * HC : (i + 1) * HC] for i in range(3)]
        else:
            out = [s.low_out.at[at : at + rows, :]]
        stages = [(kind, partners[i], sides[i]) for kind, i in stage_kinds(order, bits)]
        bufs = [getattr(s, f"in_{name}_{i}") for i in range(len(stages))]
        flow.start(name, reduced(links, loads, acc, dim, piece * size, size, stages, bufs, out, ahead, (outer, across)), held)

    mine = pl.multiple_of(c * T, T)
    theirs = pl.multiple_of((1 - c) * T, T)

    in_x = loads.copy(s.tokens, s.xb)
    in_q = loads.copy(s.w_qkv, s.wq.at[0])
    in_pool = loads.copy(s.w_pool, s.wp)
    in_pg = loads.copy(s.pooled_grad, s.pg)
    in_out = loads.copy(s.w_out, s.wo.at[0])
    in_up = loads.copy(s.w_up, s.wu.at[0])
    in_down = loads.copy(s.w_down, s.wd.at[0])

    barrier = pltpu.get_barrier_semaphore()
    greeted = partners + ([across] if bits > 2 else [])
    for to in greeted:
        pl.semaphore_signal(barrier, inc=1, device_id=to, device_id_type=MESH)
    pl.semaphore_wait(barrier, len(greeted))

    owns = {"wq": [], "wo": [], "wu": [], "wd": []}

    def get(name, shard, buf, dim, size, core):
        flow.start(name, gathered(links, WAY[name], shard, buf, dim, size, bit, to_y, to_bit, core, owns[name]))

    get("wq", s.w_qkv, s.wq, 1, D, None)
    get("wo", s.w_out, s.wo, 0, HC, to_core)
    get("wu", s.w_up, s.wu, 0, D, to_core)
    get("wd", s.w_down, s.wd, 0, U, to_core)

    gain_one, gain_two = s.gain_one[...], s.gain_two[...]
    loads.wait(in_x)
    for r in range(0, T, RC):
        x = s.xb[r : r + RC, :].astype(F32)
        scale = lax.rsqrt(jnp.mean(x * x, axis=1, keepdims=True) + EPS)
        s.nrm[pl.ds(pl.multiple_of(mine + r, RC), RC), :] = (x * scale * gain_one).astype(BF16)
    own_rows = s.nrm.at[pl.ds(mine, T), :]
    sent_norm = links.copy(own_rows, own_rows, to_core)

    starts, ends, total = [], [], 0
    for j in range(4):
        starts.append(total)
        total = total + s.lengths[y, j]
        ends.append(total)

    def kept(j):
        p = mine + POOL * lax.broadcasted_iota(jnp.int32, (T // POOL, 1), 0) + j
        bad = (p - 1) <= 0
        for e in ends[:3]:
            bad = bad | ((p >= e) & (p - 1 <= e))
        return jnp.logical_not(bad)

    loads.wait(in_q)
    cos_in, sin_in = s.angles[2], s.angles[3]
    for i in range(L // 128):
        cos_of, sin_of = s.angles[0, :, i : i + 1], s.angles[1, :, i : i + 1]
        s.cos[:, i * 128 : (i + 1) * 128] = cos_of * cos_in - sin_of * sin_in
        s.sin[:, i * 128 : (i + 1) * 128] = sin_of * cos_in + cos_of * sin_in
    row = lax.broadcasted_iota(jnp.int32, (HEAD, L), 0)
    pos = lax.broadcasted_iota(jnp.int32, (HEAD, L), 1)
    same = jnp.zeros((HEAD, L), F32)
    for j in range(4):
        same = jnp.where((row == j) & (pos >= starts[j]) & (pos < ends[j]), 1.0, same)
    key_rows_doc = same.astype(BF16)
    query_rows_doc = jnp.where(row < 4, BIG * (same - 1.0), 0.0).astype(BF16)
    value_rows = jnp.where(row < 2, -1.0, 0.0).astype(BF16)
    for h in range(4):
        s.qxt[h, HEAD : 2 * HEAD, :] = query_rows_doc

    def turn_weights(slot):
        for i in range(3):
            s.wqt[(3 * slot + i) * HC : (3 * slot + i + 1) * HC, :] = s.wq[slot, i].T

    def project(slot, start):
        for j in range(0, T, BLOCK):
            cols = pl.ds(pl.multiple_of(start + j, BLOCK), BLOCK)
            cosine, sine = s.cos[:, cols], s.sin[:, cols]
            r = dot(s.wqt[3 * slot * HC : 3 * (slot + 1) * HC, :], s.nrm[cols, :], 1, 1)
            for i in range(3):
                for h in range(2):
                    u = r[i * HC + h * HEAD : i * HC + (h + 1) * HEAD, :]
                    head = 2 * slot + h
                    if i == 2:
                        s.vt[head, :, cols] = u.astype(BF16)
                        continue
                    a, b = u[:half_head], u[half_head:]
                    turned = jnp.concatenate([a * cosine - b * sine, a * sine + b * cosine], axis=0)
                    if i == 0:
                        s.qxt[head, 0:HEAD, cols] = (turned * HEAD**-0.5).astype(BF16)
                    else:
                        s.kt[head, :, cols] = turned.astype(BF16)

    def turn_keys(head):
        s.kx[head] = jnp.concatenate([s.kt[head], key_rows_doc], axis=0).T
        s.vx[head] = jnp.concatenate([s.vt[head], value_rows], axis=0).T

    turn_weights(0)
    project(0, mine)
    tick()

    loads.wait(in_pool, in_pg)
    s.g2t[:, 0:8, :] = jnp.zeros((D // 128, 8, 128), F32)
    s.g2t[:, T : T + 8, :] = jnp.zeros((D // 128, 8, 128), F32)
    for j in range(POOL):
        grad_shift = dot(s.pg[...], s.wp[j * D : (j + 1) * D, :], 1, 1)
        put_wide(s.g2t, 8 - (POOL - 1) + j, T // POOL, jnp.where(kept(j), grad_shift, 0.0), POOL)
    sent_rim = links.copy(s.g2t.at[:, 0:8, :], s.rim, to_core)

    tick()
    links.arrived(sent_norm)
    project(0, theirs)
    tick()
    turn_keys(0)
    turn_keys(1)
    tick()

    def window(qb):
        first = max(0, qb - LEFT)
        blocks = qb - first + 1
        offset = sum(min(i, LEFT) + 1 for i in range(qb)) * BLOCK
        return first * BLOCK, blocks, offset, slice(qb * BLOCK, (qb + 1) * BLOCK)

    def score(head, qb, i, into):
        first, blocks, _, q = window(qb)
        rows = slice(i * CHUNK, (i + 1) * CHUNK)
        scores = dot(s.kx[head, first + rows.start : first + rows.stop, :], s.qxt[head, :, q])
        below = rows.start - (blocks - 1) * BLOCK
        if below >= 0:
            ki = lax.broadcasted_iota(jnp.int32, (CHUNK, BLOCK), 0) + below
            qi = lax.broadcasted_iota(jnp.int32, (CHUNK, BLOCK), 1)
            scores = jnp.where(ki <= qi, scores, NEG)
        into[rows, :] = scores
        return jnp.max(scores.reshape(CHUNK // 8, 8, BLOCK), axis=0)

    def attend(head):
        order = list(range(1, QB)) + [0]
        pieces = [window(qb)[1] * BLOCK // CHUNK for qb in order]
        bufs = (s.sc0, s.sc1)
        tops = [score(head, order[0], i, bufs[0]) for i in range(pieces[0])]
        for at, qb in enumerate(order):
            first, blocks, offset, q = window(qb)
            now, later = bufs[at % 2], bufs[(at + 1) % 2]
            top = jnp.max(functools.reduce(jnp.maximum, tops), axis=0, keepdims=True)
            more = pieces[at + 1] if at + 1 < QB else 0
            tops, total = [], jnp.zeros((8, BLOCK), F32)
            for i in range(pieces[at]):
                while len(tops) < (i + 1) * more // pieces[at]:
                    tops.append(score(head, order[at + 1], len(tops), later))
                e = jnp.exp(now[i * CHUNK : (i + 1) * CHUNK, :] - top)
                total = total + jnp.sum(e.reshape(CHUNK // 8, 8, BLOCK), axis=0)
                s.probs[head, offset + i * CHUNK : offset + (i + 1) * CHUNK, :] = e.astype(BF16)
            inverse = 1.0 / jnp.sum(total, axis=0, keepdims=True)
            s.rl[head : head + 1, q] = inverse
            low = s.probs[head, offset : offset + blocks * BLOCK, :]
            out = dot(s.vt[head, :, first : first + blocks * BLOCK], low) * inverse
            s.ot[head * HEAD : (head + 1) * HEAD, q] = out.astype(BF16)
            tick()

    def send_heads(slot):
        rows = slice(slot * HC, (slot + 1) * HC)
        s.otf[rows, :] = s.ot[rows, pl.ds(mine, T)]
        return links.copy(
            s.ot.at[rows, pl.ds(theirs, T)],
            s.otf.at[(2 + slot) * HC : (3 + slot) * HC, :],
            to_core,
        )

    attend(0)
    attend(1)
    sent_heads = [send_heads(0)]
    flow.need("wq")
    turn_weights(1)
    project(1, mine)
    tick()
    project(1, theirs)
    turn_keys(2)
    turn_keys(3)
    tick()
    attend(2)
    attend(3)
    sent_heads.append(send_heads(1))
    tick()
    flow.need("wo")
    loads.wait(in_out)
    for k in sent_heads:
        links.arrived(k)

    for j in range(0, T, BLOCK):
        out = dot(s.otf[:, j : j + BLOCK], s.wo[...].reshape(4 * HC, D), 0, 0)
        for r in range(j, j + BLOCK, RC):
            rows = slice(r, r + RC)
            h = out[r - j : r - j + RC, :] + s.xb[rows, :].astype(F32)
            s.h1[rows, :] = h
            put_wide(s.h2, 8 + r, RC, h)
            scale = lax.rsqrt(jnp.mean(h * h, axis=1, keepdims=True) + EPS)
            s.n2[rows, :] = (h * scale * gain_two).astype(BF16)
    links.arrived(sent_rim)
    tail = lax.broadcasted_iota(jnp.int32, (D // 128, 8, 128), 1) >= 8 - (POOL - 1)
    s.g2t[:, T : T + 8, :] = s.g2t[:, T : T + 8, :] + jnp.where(tail, s.rim[...], 0.0)
    for r in range(0, T, RC):
        branch = wide(s.g2t, 8 + r, RC).astype(BF16)
        s.gatt[pl.ds(pl.multiple_of(mine + r, RC), RC), :] = branch
    tick()
    loads.wait(in_up, in_down)

    root = math.sqrt(2.0 / math.pi)

    def feed_forward(slot, first):
        def one_block(i, carry):
            j = pl.multiple_of(i * BLOCK, BLOCK)
            block, at = pl.ds(j, BLOCK), pl.multiple_of(8 + j, 8)
            v = dot(s.n2[block, :], s.wu[slot])
            grad_act = dot(s.gatt[pl.ds(pl.multiple_of(mine + j, BLOCK), BLOCK), :], s.wd[slot], 1, 1)
            for r in range(0, BLOCK, RC):
                rows = pl.ds(pl.multiple_of(j + r, RC), RC)
                u = v[r : r + RC, :]
                square = u * u
                th = jnp.tanh(u * (root + (root * 0.044715) * square))
                up = 0.5 + 0.5 * th
                slope = up + (u * (up - up * th)) * (root + (root * 3 * 0.044715) * square)
                s.act[rows, :] = (u * up).astype(BF16)
                s.gpre[rows, :] = (grad_act[r : r + RC, :] * slope).astype(BF16)
            put_wide(s.h2, at, BLOCK, wide(s.h2, at, BLOCK) + dot(s.act[block, :], s.wd[slot]))
            grad_normed = dot(s.gpre[block, :], s.wu[slot], 1, 1)
            s.gn[block, :] = grad_normed if first else s.gn[block, :] + grad_normed
            return carry

        lax.fori_loop(0, T // BLOCK, one_block, 0)
        tick()
        branch = s.gatt[pl.ds(mine, T), :]
        for j in range(0, U, BLOCK):
            s.gd[slot, j : j + BLOCK, :] = dot(s.act[:, j : j + BLOCK], branch, 0, 0).astype(BF16)
        tick()
        for j in range(0, D, BLOCK):
            s.gu[slot, j : j + BLOCK, :] = dot(s.n2[:, j : j + BLOCK], s.gpre[...], 0, 0).astype(BF16)
        tick()

    def to_other_core(slot):
        return (
            links.copy(s.gd.at[slot], s.cd.at[slot - 2], to_core),
            links.copy(s.gu.at[slot], s.cu.at[slot - 2], to_core),
        )

    def from_other_core(slot, sent):
        links.arrived(sent[0])
        s.gd[slot] = s.gd[slot] + s.cd[slot]
        links.arrived(sent[1])
        s.gu[slot] = s.gu[slot] + s.cu[slot]

    if SLOTS[0] == 3:
        flow.need("wu", "wd")
    else:
        links.arrived(owns["wu"][0])
        links.arrived(owns["wd"][0])
    shard_sums = {name: s.gd if name[0] == "d" else s.gu for name in ORDER if name[0] in "du"}
    ahead = SLOTS[1]
    early = [name for name in shard_sums if ahead == 1 or ORDER[name][0][0] != "y"]
    feed_forward(SLOTS[0], True)
    sent_one = to_other_core(SLOTS[0])
    feed_forward(SLOTS[1], False)
    from_other_core(SLOTS[1], sent_one)
    for name in early:
        start_sum(name, shard_sums[name].at[0:2], 0, True, ahead)
    flow.need("wu", "wd")
    feed_forward(SLOTS[2], False)
    sent_two = to_other_core(SLOTS[2])
    feed_forward(SLOTS[3], False)

    gain_grad_two = jnp.zeros((8, D), F32)
    for r in range(0, T, RC):
        rows = slice(r, r + RC)
        h, gn = s.h1[rows, :], s.gn[rows, :]
        scale = lax.rsqrt(jnp.mean(h * h, axis=1, keepdims=True) + EPS)
        e = gain_two * gn
        hs = h * scale
        grad = wide(s.g2t, 8 + r, RC) + scale * (e - hs * jnp.mean(e * hs, axis=1, keepdims=True))
        s.h1[rows, :] = grad
        s.gatt[pl.ds(pl.multiple_of(mine + r, RC), RC), :] = grad.astype(BF16)
        gain_grad_two = gain_grad_two + jnp.sum((gn * hs).reshape(RC // 8, 8, D), axis=0)
    own_rows = s.gatt.at[pl.ds(mine, T), :]
    sent_gatt = links.copy(own_rows, own_rows, to_core)
    sent_rim = links.copy(s.h2.at[:, T : T + 8, :], s.h2.at[:, 0:8, :], to_core)
    from_other_core(SLOTS[3], sent_two)
    flow.release(*early)
    for name in shard_sums:
        if name not in early:
            start_sum(name, shard_sums[name].at[0:2], 0)
    tick()

    block_square = jnp.zeros((8, D), F32)
    for r in range(0, T, RC):
        h = wide(s.h2, 8 + r, RC)
        block_square = block_square + jnp.sum((h * h).reshape(RC // 8, 8, D), axis=0)
    links.arrived(sent_rim)
    for j in range(POOL):
        rows = pl.ds(8 - (POOL - 1) + j, T // POOL, stride=POOL)
        taken = jnp.concatenate([s.h2[i, rows, :] for i in range(D // 128)], axis=1)
        s.n2[j * (T // POOL) : (j + 1) * (T // POOL), :] = jnp.where(kept(j), taken, 0.0).astype(BF16)
    pool_in = [s.n2[j * (T // POOL) : (j + 1) * (T // POOL), :] for j in range(POOL)]
    pooled = sum(dot(pool_in[j], s.wp[j * D : (j + 1) * D, :]) for j in range(POOL))
    pool_square = jnp.sum((pooled * pooled).reshape(T // POOL // 8, 8, D), axis=0)
    s.gpre[0 : T // POOL, :] = pooled.astype(BF16)
    out_pooled = loads.copy(s.gpre.at[0 : T // POOL, :], part(s.low_out, 0, *places["pooled"]))
    for j in range(POOL):
        s.wp[j * D : (j + 1) * D, :] = dot(pool_in[j], s.pg[...], 0, 0).astype(BF16)
    for name in (name for name in ORDER if name[0] == "p"):
        start_sum(name, s.wp, 0)
    tick()

    def grad_heads(start):
        for j in range(0, T, BLOCK):
            cols = pl.ds(pl.multiple_of(start + j, BLOCK), BLOCK)
            g = dot(s.wo[0:2].reshape(2 * HC, D), s.gatt[cols, :], 1, 1)
            line = lax.broadcasted_iota(jnp.int32, (HEAD, BLOCK), 0)
            for head in range(4):
                low = (g[head * HEAD : (head + 1) * HEAD] * s.rl[head : head + 1, cols]).astype(BF16)
                o = s.ot[head * HEAD : (head + 1) * HEAD, cols].astype(F32)
                delta = jnp.sum(low.astype(F32) * o, axis=0, keepdims=True)
                high = delta.astype(BF16).astype(F32)
                rest = jnp.where(line == 0, high, jnp.where(line == 1, delta - high, 0.0))
                s.gox[head, 0:HEAD, cols] = low
                s.gox[head, HEAD : 2 * HEAD, cols] = rest.astype(BF16)

    grad_heads(mine)
    links.arrived(sent_gatt)
    grad_heads(theirs)
    for slot in (1, 0):
        s.go[slot] = dot(s.ot[slot * HC : (slot + 1) * HC, :], s.gatt[...]).astype(BF16)
    start_sum("o", s.go, 0)
    tick()

    def grad_score(head, qb, i, into):
        first, _, offset, q = window(qb)
        rows = slice(i * BLOCK, (i + 1) * BLOCK)
        grads = dot(s.vx[head, first + rows.start : first + rows.stop, :], s.gox[head, :, q])
        probs = s.probs[head, offset + rows.start : offset + rows.stop, :]
        into[rows, :] = (probs.astype(F32) * grads).astype(BF16)

    def attend_back(head):
        slot, h = head // 2, head % 2
        bufs, seen = (s.ds0, s.ds1), set()
        for i in range(window(0)[1]):
            grad_score(head, 0, i, bufs[0])
        for qb in range(QB):
            first, blocks, offset, q = window(qb)
            now, later = bufs[qb % 2], bufs[(qb + 1) % 2]
            more, done = window(qb + 1)[1] if qb + 1 < QB else 0, 0
            s.dq[:, q] = dot(s.kt[head, :, first : first + blocks * BLOCK], now[0 : blocks * BLOCK, :])
            for i in range(blocks):
                while done < (i + 1) * more // blocks:
                    grad_score(head, qb + 1, done, later)
                    done += 1
                cols = slice(first + i * BLOCK, first + (i + 1) * BLOCK)
                probs = s.probs[head, offset + i * BLOCK : offset + (i + 1) * BLOCK, :]
                dk = dot(s.qxt[head, 0:HEAD, q], now[i * BLOCK : (i + 1) * BLOCK, :], 1, 1)
                dv = dot(s.gox[head, 0:HEAD, q], probs, 1, 1)
                s.dk[:, cols] = s.dk[:, cols] + dk if cols.start in seen else dk
                s.dv[:, cols] = s.dv[:, cols] + dv if cols.start in seen else dv
                seen.add(cols.start)
            tick()
        cosine, sine = s.cos[...], s.sin[...]
        for i, (ref, factor) in enumerate(((s.dq, HEAD**-0.5), (s.dk, 1.0))):
            a, b = ref[:half_head, :], ref[half_head:, :]
            turned = jnp.concatenate([a * cosine + b * sine, b * cosine - a * sine], axis=0) * factor
            start = (3 * slot + i) * HC + h * HEAD
            s.gpt[start : start + HEAD, :] = turned.astype(BF16)
        start = (3 * slot + 2) * HC + h * HEAD
        s.gpt[start : start + HEAD, :] = s.dv[...].astype(BF16)

    def grad_weights(slot):
        for i in range(3):
            g = dot(s.gpt[(3 * slot + i) * HC : (3 * slot + i + 1) * HC, :], s.nrm[...])
            s.wq[slot, i] = g.astype(BF16).T

    attend_back(2)
    attend_back(3)
    grad_weights(1)
    sums_q = [name for name in ORDER if name[0] == "q"]
    for name in sums_q:
        start_sum(name, s.wq, 1, True)
    attend_back(0)
    attend_back(1)
    grad_weights(0)
    flow.release(*sums_q)
    tick()

    for j in range(0, T, BLOCK):
        cols = pl.ds(pl.multiple_of(theirs + j, BLOCK), BLOCK)
        s.n2[j : j + BLOCK, :] = dot(s.gpt[:, cols], s.wqt[...], 0, 0).astype(BF16)
    sent_pn = links.copy(s.n2, s.act, to_core)
    for j in range(0, T, BLOCK):
        cols = pl.ds(pl.multiple_of(mine + j, BLOCK), BLOCK)
        s.gn[j : j + BLOCK, :] = dot(s.gpt[:, cols], s.wqt[...], 0, 0)
    tick()
    links.arrived(sent_pn)
    loads.wait(out_pooled)
    gain_grad_one = jnp.zeros((8, D), F32)
    for r in range(0, T, RC):
        rows = slice(r, r + RC)
        x, gn = s.xb[rows, :].astype(F32), s.gn[rows, :] + s.act[rows, :].astype(F32)
        scale = lax.rsqrt(jnp.mean(x * x, axis=1, keepdims=True) + EPS)
        e = gain_one * gn
        xs = x * scale
        grad = s.h1[rows, :] + scale * (e - xs * jnp.mean(e * xs, axis=1, keepdims=True))
        s.gpre[rows, :] = grad.astype(BF16)
        gain_grad_one = gain_grad_one + jnp.sum((gn * xs).reshape(RC // 8, 8, D), axis=0)
    loads.copy(s.gpre, part(s.low_out, 0, *places["gtok"]))

    line = lax.broadcasted_iota(jnp.int32, (8, D), 0)
    small = jnp.zeros((8, D), F32)
    for i, v in enumerate((gain_grad_one, gain_grad_two, block_square, pool_square)):
        v = jnp.sum(v, axis=0, keepdims=True)
        if i >= 2:
            v = jnp.sum(v, axis=1, keepdims=True)
        small = jnp.where(line == i, v, small)
    s.terms[0] = small
    flow.start("s", summed(links, s.terms, s.term_in, partners))
    flow.finish()
    loads.copy(s.terms.at[len(partners)], s.small_out)
    links.finish()
    loads.finish()


def result_rows(T, D, HC, U):
    sizes = {"p": POOL * D, "d": U, "u": D, "q": D, "o": HC, "pooled": T // POOL, "gtok": T}
    at, out = 0, {}
    for name, rows in sizes.items():
        out[name] = (at, rows)
        at += rows
    return out, at


def widen(places, block_scale, pool_scale, small, low, *refs):
    rms_block, rms_pool, gain_one, gain_two = refs[:4]
    results, wide_refs, taken, sems = dict(zip(places, refs[4:11])), dict(zip(places, refs[11:16])), refs[16], refs[17]
    loads, pieces = Loads(sems), []
    for name, (at, rows) in places.items():
        cut = rows // POOL if name == "p" else rows
        for first in range(0, rows, cut):
            place = slice(at + first, at + first + cut)
            pieces.append((name, slice(first, first + cut), place, loads.copy(low.at[place, :], taken.at[place, :])))
    rms_block[...] = jnp.sqrt(small[2:3, 0:1] * block_scale)
    rms_pool[...] = jnp.sqrt(small[3:4, 0:1] * pool_scale)
    gain_one[...] = small[0:1, :]
    gain_two[...] = small[1:2, :]
    for name, rows, place, k in pieces:
        loads.wait(k)
        if name not in wide_refs:
            loads.copy(taken.at[place, :], results[name])
            continue
        made = wide_refs[name]
        if name == "q":
            for i in range(3):
                width = made.shape[2]
                made[i] = taken[place, i * width : (i + 1) * width].astype(F32)
            loads.copy(made, results[name])
        else:
            made[rows, :] = taken[place, :].astype(F32)
            loads.copy(made.at[rows, :], results[name].at[rows, :])
    loads.finish()


IN_NAMES = (
    "tokens", "lengths", "w_qkv", "w_out", "w_up", "w_down", "w_pool",
    "gain_one", "gain_two", "pooled_grad", "angles",
)
OUT_NAMES = ("low_out", "small_out")


def tables(length):
    half, lanes = HEAD // 2, 128
    frequency = np.exp(-math.log(10000.0) * np.arange(half) / half)[:, None]
    group = frequency * (lanes * np.minimum(np.arange(lanes), length // lanes))
    within = frequency * np.arange(lanes)
    return np.stack([np.cos(group), np.sin(group), np.cos(within), np.sin(within)]).astype(np.float32)


def shards(tokens, lengths, w_qkv, w_out, w_up, w_down, w_pool, gain_one, gain_two, pooled_grad):
    T, D = tokens.shape
    HC, U = w_out.shape[0], w_up.shape[1]
    dp = lax.axis_size("dp")
    bits = dp.bit_length() - 1
    assert lax.axis_size("tensor") == 4 and lengths.shape == (2, 4) and dp == 1 << bits and bits > 0
    scratch = scratch_list(T, D, HC, U, bits)
    names = IN_NAMES + OUT_NAMES + tuple(n for n, _, _ in scratch) + ("send_sems", "recv_sems", "free_sems", "load_sems")
    hbm, vmem, smem = pl.BlockSpec(memory_space=pl.ANY), pl.BlockSpec(memory_space=pltpu.VMEM), pl.BlockSpec(memory_space=pltpu.SMEM)
    copies = 256 + 24 * bits
    places, total = result_rows(T, D, HC, U)
    low, small = pl.pallas_call(
        functools.partial(kernel, bits, names),
        out_shape=[jax.ShapeDtypeStruct((total, D), BF16), jax.ShapeDtypeStruct((8, D), F32)],
        in_specs=[hbm, smem, hbm, hbm, hbm, hbm, hbm, vmem, vmem, hbm, vmem],
        out_specs=[hbm] * 2,
        scratch_shapes=[pltpu.VMEM(shape, kind) for _, shape, kind in scratch]
        + [pltpu.SemaphoreType.DMA((copies,)), pltpu.SemaphoreType.DMA((copies,))]
        + [pltpu.SemaphoreType.REGULAR((160,)), pltpu.SemaphoreType.DMA((64,))],
        compiler_params=pltpu.CompilerParams(
            collective_id=0, has_side_effects=True, vmem_limit_bytes=64 * 2**20 - 2**16
        ),
    )(
        tokens, lengths, jnp.transpose(w_qkv, (1, 0, 2)), w_out, w_up, w_down, w_pool,
        gain_one.reshape(1, D), gain_two.reshape(1, D), pooled_grad, tables(2 * T),
    )
    group = dp * 4 * T * D
    one, line = jax.ShapeDtypeStruct((1, 1), F32), jax.ShapeDtypeStruct((1, D), F32)
    wide_shapes = [jax.ShapeDtypeStruct(s, F32) for s in ((POOL * D, D), (U, D), (D, U), (3, D, HC), (HC, D))]
    rms_block, rms_pool, grad_one, grad_two, gp, gd, gu, gq, go, pooled, gtok = pl.pallas_call(
        functools.partial(widen, places, 1.0 / group, POOL / group),
        out_shape=[one, one, line, line]
        + wide_shapes
        + [jax.ShapeDtypeStruct((T // POOL, D), BF16), jax.ShapeDtypeStruct((T, D), BF16)],
        in_specs=[vmem, hbm],
        out_specs=[vmem] * 4 + [hbm] * 7,
        scratch_shapes=[pltpu.VMEM(a.shape, F32) for a in wide_shapes]
        + [pltpu.VMEM((total, D), BF16), pltpu.SemaphoreType.DMA((18,))],
        compiler_params=pltpu.CompilerParams(vmem_limit_bytes=62 * 2**20),
    )(small, low)
    return (
        pooled,
        rms_block.reshape(()),
        rms_pool.reshape(()),
        gtok,
        jnp.transpose(gq, (1, 0, 2)),
        go,
        gu,
        gd,
        gp,
        grad_one.reshape(D),
        grad_two.reshape(D),
    )


def solution(mesh):
    rows = P(("dp", "tensor"), None)
    placed = (
        rows, P("dp", None), P(None, None, "tensor"), P("tensor", None), P(None, "tensor"),
        P("tensor", None), P(), P(), P(), rows,
    )
    return jax.shard_map(
        shards,
        mesh=mesh,
        in_specs=placed,
        out_specs=(
            rows, P(), P(), rows, P(None, None, "tensor"), P("tensor", None), P(None, "tensor"),
            P("tensor", None), P(), P(), P(),
        ),
        check_vma=False,
    )
```

```python
import functools
import math
from types import SimpleNamespace

import jax
import jax.numpy as jnp
import numpy as np
from jax import lax
from jax.experimental import pallas as pl
from jax.experimental.pallas import tpu as pltpu
from jax.sharding import PartitionSpec as P

HEAD = 64
POOL = 3
EPS = 1e-06
BIG = float(2**30)
NEG = -1000000000.0
BLOCK = 256
LEFT = 3
WINDOW = LEFT + 1
FEED = 384
CHUNK = 128
F32, BF16 = jnp.float32, jnp.bfloat16
MESH = pl.DeviceIdType.MESH


def dot(a, b, ca=1, cb=0):
    return lax.dot_general(a, b, (((ca,), (cb,)), ((), ())), preferred_element_type=F32)


def part(ref, dim, start, count):
    index = [slice(None)] * len(ref.shape)
    index[dim] = pl.ds(start, count)
    return ref.at[tuple(index)]


def wide(ref, start, count):
    return jnp.concatenate([ref[i, pl.ds(start, count), :] for i in range(ref.shape[0])], axis=1)


def put_wide(ref, start, count, value, stride=None):
    for i in range(ref.shape[0]):
        ref[i, pl.ds(start, count, stride=stride), :] = value[:, i * 128 : (i + 1) * 128]


def on(condition, act):
    if condition is None:
        act()
    else:
        pl.when(condition)(act)


class Links:
    def __init__(self, send, recv, free, partners):
        self.send, self.recv, self.sent, self.partners = send, recv, [], partners
        self.free, self.freed = free, 0

    def copy(self, src, dst, to, sends=None, takes=None):
        k = len(self.sent)
        move = pltpu.make_async_remote_copy(
            src, dst, self.send.at[k], self.recv.at[k], device_id=to, device_id_type=MESH
        )
        on(sends, move.start)
        self.sent.append([move, False, False, sends, takes])
        return k

    def arrived(self, k):
        if not self.sent[k][2]:
            on(self.sent[k][4], self.sent[k][0].wait_recv)
            self.sent[k][2] = True

    def left(self, k):
        if not self.sent[k][1]:
            on(self.sent[k][3], self.sent[k][0].wait_send)
            self.sent[k][1] = True

    def give(self, to, gives=None):
        i = self.freed
        self.freed += 1
        on(gives, lambda: pl.semaphore_signal(self.free.at[i], inc=1, device_id=to, device_id_type=MESH))
        return i

    def granted(self, i, takes=None):
        on(takes, lambda: pl.semaphore_wait(self.free.at[i], 1))

    def finish(self):
        for k in range(len(self.sent)):
            self.left(k)


class Loads:
    def __init__(self, sems):
        self.sems, self.moves = sems, []

    def copy(self, src, dst):
        move = pltpu.make_async_copy(src, dst, self.sems.at[len(self.moves)])
        move.start()
        self.moves.append([move, False])
        return len(self.moves) - 1

    def wait(self, *ks):
        for k in ks:
            if not self.moves[k][1]:
                self.moves[k][0].wait()
                self.moves[k][1] = True

    def finish(self):
        self.wait(*range(len(self.moves)))


class Flow:
    def __init__(self):
        self.gens, self.waits, self.at = {}, {}, 0

    def step(self, name):
        self.waits[name] = next(self.gens[name], None)
        return self.waits[name] is not None

    def start(self, name, gen, held=False):
        self.gens[name] = gen
        self.step(name)

    def release(self, *names):
        pass

    def tick(self):
        for name in PLAN[self.at] if self.at < len(PLAN) else ():
            self.step(name)
        self.at += 1

    def need(self, *names):
        for name in names:
            while self.step(name):
                pass

    def finish(self):
        self.tick()
        live = list(self.gens)
        while live:
            live = [name for name in live if self.step(name)]


def gathered(links, way, shard, buf, dim, size, bit, to_y, to_bit, to_core, owns):
    def rows(ref, start, count):
        return part(ref, dim, pl.multiple_of(start, 16), count)

    near, own = buf.at[1], None
    if way == "y":
        k = links.copy(shard, near, to_y)
        yield (k,)
        if to_core is not None:
            own = links.copy(shard, buf.at[2], to_core)
            owns.append(own)
        links.arrived(k)
        ks = first = ()
    elif len(bit) == 1:
        half = size // 2
        k = links.copy(rows(shard, bit[0] * half, half), rows(near, bit[0] * half, half), to_y)
        yield (k,)
        if to_core is not None:
            own = links.copy(shard, buf.at[2], to_core)
            owns.append(own)
        links.arrived(k)
        piece = rows(near, bit[0] * half, half)
        ks, first = (links.copy(piece, piece, to_bit[0]),), ()
    else:
        quarter = size // 4
        at = (2 * bit[1] + bit[0]) * quarter
        over_x = (2 * bit[1] + 1 - bit[0]) * quarter
        over_z = (2 - 2 * bit[1] + bit[0]) * quarter
        k = links.copy(rows(shard, at, quarter), rows(near, at, quarter), to_y)
        yield (k,)
        if to_core is not None:
            own = links.copy(shard, buf.at[2], to_core)
            owns.append(own)
        links.arrived(k)
        piece = rows(near, at, quarter)
        by_x, by_z = first = links.copy(piece, piece, to_bit[0]), links.copy(piece, piece, to_bit[1])
        yield (by_x, by_z)
        links.arrived(by_x)
        piece = rows(near, over_x, quarter // 2)
        second = links.copy(piece, piece, to_bit[1])
        links.arrived(by_z)
        piece = rows(near, over_z + quarter // 2, quarter // 2)
        ks = (links.copy(piece, piece, to_bit[0]), second)
    if ks:
        yield ks
    for k in ks:
        links.arrived(k)
    if to_core is None:
        for k in ks + first:
            links.left(k)
        return
    k = links.copy(near, buf.at[3], to_core)
    yield (k, own)
    links.arrived(own)
    links.arrived(k)


def reduced(links, loads, acc, dim, base, size, stages, bufs, out, ahead, line):
    lo, n, spans = base, size, []
    two = any(kind == "slot" for kind, _, _ in stages)

    def rows(ref, start, count, slots=False):
        return part(ref, dim + 1 if slots else dim, start if isinstance(start, int) else pl.multiple_of(start, 16), count)

    for (kind, to, bit), buf in zip(stages, bufs):
        if kind == "slot":
            k = links.copy(rows(acc.at[1], lo, n), buf, to)
            acc, two = acc.at[0], False
            mine = rows(acc, lo, n)
        elif kind == "half":
            half = n // 2
            there, here = lo + (1 - bit) * half, lo + bit * half
            if two:
                early = links.copy(rows(acc.at[ahead], there, half), buf.at[ahead], to)
                yield (early,)
                k = links.copy(rows(acc.at[1 - ahead], there, half), buf.at[1 - ahead], to)
            else:
                k = links.copy(rows(acc, there, half), buf, to)
            before = lo
            lo, n = here, half
            mine = rows(acc, lo, n, two)
        elif kind == "line":
            mine, (outer, across) = rows(acc, lo, n), line
            inner = jnp.logical_not(outer)

            def add(mine=mine, buf=buf):
                mine[...] = mine[...] + buf[...]

            k = links.copy(mine, buf, to, outer, inner)
            yield (k,)
            links.arrived(k)
            on(inner, add)
            free = links.give(across, inner)
            links.left(k)
            back = links.give(to, outer)
            links.granted(free, inner)
            k = links.copy(mine, buf, across, inner, inner)
            yield (k,)
            links.arrived(k)
            links.left(k)
            on(inner, add)
            links.granted(back, inner)
            k = links.copy(mine, mine, to, inner, outer)
            yield (k,)
            links.arrived(k)
            continue
        else:
            mine = rows(acc, lo, n)
            k = links.copy(mine, buf, to)
        yield (k,)
        if kind == "half" and two:
            links.arrived(early)
            links.left(early)
        links.arrived(k)
        if kind != "slot":
            links.left(k)
        if kind == "half":
            spans.append((to, before, links.give(to)))
        mine[...] = mine[...] + buf[...]
    for to, before, credit in reversed(spans):
        mine = rows(acc, lo, n)
        links.granted(credit)
        k = links.copy(mine, mine, to)
        yield (k,)
        links.arrived(k)
        lo, n = before, 2 * n
    for i, ref in enumerate(out):
        loads.copy(rows(acc, lo, n) if len(out) == 1 else part(acc.at[i], dim - 1, lo, n), part(ref, 0, lo, n))


def summed(links, terms, bufs, partners):
    for i, to in enumerate(partners):
        k = links.copy(terms.at[i], bufs.at[i], to)
        yield (k,)
        links.arrived(k)
        terms[i + 1] = terms[i] + bufs[i]


ORDER = {
    "d0": ("0yLs", 0, 4),
    "d1": ("0yLs", 1, 4),
    "d2": ("1y0s", 2, 4),
    "d3": ("1y0s", 3, 4),
    "u0": ("1y0s", 0, 4),
    "u1": ("0yLs", 1, 4),
    "u2": ("1y0s", 2, 4),
    "u3": ("y0Ls", 3, 4),
    "p0": ("c1Y0s", 0, 3),
    "p1": ("c0YLs", 1, 3),
    "p2": ("cY01s", 2, 3),
    "o": ("0yLs", 0, 1),
    "q0": ("1y0s", 0, 2),
    "q1": ("y0Ls", 1, 2),
}
WAY = {"wq": "yxz", "wo": "y", "wu": "yxz", "wd": "yxz"}
SLOTS = (2, 0, 3, 1)
PLAN = (
    (), (), (), (), ("wq",), (), (), (), (), (), (), (), (), (), ("wo",), (), ("wo", "wu", "wd",), (), (), (), (),
    (), (), (), (), (), (), (), (), (), (), ("wu",), (), ("wd",), (), ("wu",), (), ("wd",), (), (), (), (), (), (),
    ("d0", "d2", "d1", "d3", "u0", "u1", "u2",), (), ("d0", "d2", "p0",), ("p1", "u3", "d1", "p2", "d3",), (), (),
    ("u1", "u0",), (), ("d0", "o", "u2",), (), (), ("d2",), (), (), ("d1", "p1", "p0",), (), (), ("u3", "d0",), (),
    ("p2", "o",), ("d2", "d1", "d3",), (), (), (), ("u1", "d0",), (), ("p2", "u0", "d3", "u3",), ("q0", "d2", "u2",),
    ("d1", "u1", "d0", "p1", "u0", "p2", "p0", "d2", "d3", "u2", "u3", "q0",),
    ("s", "q1", "d1", "u1", "d0", "p1", "o", "p0", "d3", "u0", "q0", "d2", "s", "p2", "q1", "u3", "u2", "o", "d1",
     "p1", "u0", "u1", "q0", "s", "p0", "d3", "u3", "p2", "o", "u2", "q1", "p1", "u1", "p0", "u0", "q0", "p2", "s",
     "p1", "o", "q1", "p0", "q0", "u2", "s", "p2", "q1", "p1", "p2", "p1", "o", "p0", "p0", "q1", "q0",),
)


def stage_kinds(order, bits):
    kinds = []
    for letter in order:
        if letter == "y":
            kinds.append(("slot", 1))
        elif letter in "cY":
            kinds.append(("half", "cY".index(letter)))
        elif letter == "L":
            kinds += [("line", 3)] if bits > 2 else []
        elif letter in "01":
            kinds += [("half", 2 + int(letter))] if int(letter) < bits else []
        else:
            kinds += [("swap", 2 + i) for i in range(3 if "L" in order else 2, bits)]
    return kinds


def buffer_shapes(order, rows, shape, bits):
    kinds, out = stage_kinds(order, bits), []
    two = any(kind == "slot" for kind, _ in kinds)
    for kind, _ in kinds:
        if kind == "slot":
            two = False
        elif kind == "half":
            rows //= 2
        out.append(((2,) if two else ()) + shape(rows))
    return out


def scratch_list(T, D, HC, U, bits):
    L, heads, qb = 2 * T, 2 * HC // HEAD, 2 * T // BLOCK
    blocks = sum(min(i, LEFT) + 1 for i in range(qb))
    kd = POOL * D
    out = [
        ("xb", (T, D), BF16),
        ("nrm", (L, D), BF16),
        ("wq", (2, 3, D, HC), BF16),
        ("wqt", (6 * HC, D), BF16),
        ("wo", (4, HC, D), BF16),
        ("wu", (4, D, U), BF16),
        ("wd", (4, U, D), BF16),
        ("wp", (kd, D), BF16),
        ("pg", (T // POOL, D), BF16),
        ("cos", (HEAD // 2, L), F32),
        ("sin", (HEAD // 2, L), F32),
        ("qxt", (heads, 2 * HEAD, L), BF16),
        ("kt", (heads, HEAD, L), BF16),
        ("vt", (heads, HEAD, L), BF16),
        ("kx", (heads, L, 2 * HEAD), BF16),
        ("vx", (heads, L, 2 * HEAD), BF16),
        ("probs", (heads, blocks * BLOCK, BLOCK), BF16),
        ("rl", (8, L), F32),
        ("ot", (2 * HC, L), BF16),
        ("otf", (4 * HC, T), BF16),
        ("gox", (heads, 2 * HEAD, L), BF16),
        ("gpt", (6 * HC, L), BF16),
        ("h1", (T, D), F32),
        ("h2", (D // 128, T + 8, 128), F32),
        ("g2t", (D // 128, T + 8, 128), F32),
        ("rim", (D // 128, 8, 128), F32),
        ("n2", (T, D), BF16),
        ("act", (T, U), BF16),
        ("gpre", (T, U), BF16),
        ("gn", (T, D), F32),
        ("gatt", (L, D), BF16),
        ("dk", (HEAD, L), F32),
        ("dv", (HEAD, L), F32),
        ("dq", (HEAD, L), F32),
        ("gd", (4, U, D), BF16),
        ("gu", (4, D, U), BF16),
        ("go", (2, HC, D), BF16),
        ("cd", (2, U, D), BF16),
        ("cu", (2, D, U), BF16),
        ("sc0", (WINDOW * BLOCK, BLOCK), F32),
        ("sc1", (WINDOW * BLOCK, BLOCK), F32),
        ("ds0", (WINDOW * BLOCK, BLOCK), BF16),
        ("ds1", (WINDOW * BLOCK, BLOCK), BF16),
        ("terms", (bits + 3, 8, D), F32),
        ("term_in", (bits + 2, 8, D), F32),
    ]
    rows_of = {"d": U, "u": D, "o": HC, "q": D, "p": kd}
    shape_of = {
        "d": lambda n: (n, D),
        "u": lambda n: (n, U),
        "o": lambda n: (n, D),
        "q": lambda n: (3, n, HC),
        "p": lambda n: (n, D),
    }
    for name, (order, _, parts) in ORDER.items():
        shapes = buffer_shapes(order, rows_of[name[0]] // parts, shape_of[name[0]], bits)
        out += [(f"in_{name}_{i}", shape, BF16) for i, shape in enumerate(shapes)]
    return out


def kernel(bits, names, *refs):
    s = SimpleNamespace(**dict(zip(names, refs)))
    T, D = s.xb.shape
    HC, U = s.wo.shape[1], s.wu.shape[2]
    L, QB = 2 * T, 2 * T // BLOCK
    half_head = HEAD // 2
    places, _ = result_rows(T, D, HC, U)
    RC = 32
    loads = Loads(s.load_sems)

    d, t = lax.axis_index("dp"), lax.axis_index("tensor")
    c, y = t % 2, t // 2
    to_core, to_y = (d, t + 1 - 2 * c), (d, t + 2 - 4 * y)
    bit = [(d // (1 << i)) % 2 for i in range(bits)]
    to_bit = [(d + (1 - 2 * bit[i]) * (1 << i), t) for i in range(bits)]
    partners = [to_core, to_y] + to_bit
    outer, across = None, None
    if bits > 2:
        outer = bit[1] == bit[2]
        across = (d + (1 - 2 * bit[1]) * 2 + (1 - 2 * bit[2]) * 4, t)
    links, flow = Links(s.send_sems, s.recv_sems, s.free_sems, partners), Flow()
    sides = [c, y] + bit
    tick = flow.tick

    def start_sum(name, acc, dim, held=False, ahead=1):
        order, piece, parts = ORDER[name]
        size = {"d": U, "u": D, "o": HC, "q": D, "p": POOL * D}[name[0]] // parts
        at, rows = places[name[0]]
        if name[0] == "q":
            out = [s.low_out.at[at : at + rows, i * HC : (i + 1) * HC] for i in range(3)]
        else:
            out = [s.low_out.at[at : at + rows, :]]
        stages = [(kind, partners[i], sides[i]) for kind, i in stage_kinds(order, bits)]
        bufs = [getattr(s, f"in_{name}_{i}") for i in range(len(stages))]
        flow.start(name, reduced(links, loads, acc, dim, piece * size, size, stages, bufs, out, ahead, (outer, across)), held)

    mine = pl.multiple_of(c * T, T)
    theirs = pl.multiple_of((1 - c) * T, T)

    in_x = loads.copy(s.tokens, s.xb)
    in_q = loads.copy(s.w_qkv, s.wq.at[0])
    in_pool = loads.copy(s.w_pool, s.wp)
    in_pg = loads.copy(s.pooled_grad, s.pg)
    in_out = loads.copy(s.w_out, s.wo.at[0])
    in_up = loads.copy(s.w_up, s.wu.at[0])
    in_down = loads.copy(s.w_down, s.wd.at[0])

    barrier = pltpu.get_barrier_semaphore()
    greeted = partners + ([across] if bits > 2 else [])
    for to in greeted:
        pl.semaphore_signal(barrier, inc=1, device_id=to, device_id_type=MESH)
    pl.semaphore_wait(barrier, len(greeted))

    owns = {"wq": [], "wo": [], "wu": [], "wd": []}

    def get(name, shard, buf, dim, size, core):
        flow.start(name, gathered(links, WAY[name], shard, buf, dim, size, bit, to_y, to_bit, core, owns[name]))

    get("wq", s.w_qkv, s.wq, 1, D, None)
    get("wo", s.w_out, s.wo, 0, HC, to_core)
    get("wu", s.w_up, s.wu, 0, D, to_core)
    get("wd", s.w_down, s.wd, 0, U, to_core)

    gain_one, gain_two = s.gain_one[...], s.gain_two[...]
    loads.wait(in_x)
    for r in range(0, T, RC):
        x = s.xb[r : r + RC, :].astype(F32)
        scale = lax.rsqrt(jnp.mean(x * x, axis=1, keepdims=True) + EPS)
        s.nrm[pl.ds(pl.multiple_of(mine + r, RC), RC), :] = (x * scale * gain_one).astype(BF16)
    own_rows = s.nrm.at[pl.ds(mine, T), :]
    sent_norm = links.copy(own_rows, own_rows, to_core)

    starts, ends, total = [], [], 0
    for j in range(4):
        starts.append(total)
        total = total + s.lengths[y, j]
        ends.append(total)

    def kept(j):
        p = mine + POOL * lax.broadcasted_iota(jnp.int32, (T // POOL, 1), 0) + j
        bad = (p - 1) <= 0
        for e in ends[:3]:
            bad = bad | ((p >= e) & (p - 1 <= e))
        return jnp.logical_not(bad)

    loads.wait(in_q)
    cos_in, sin_in = s.angles[2], s.angles[3]
    for i in range(L // 128):
        cos_of, sin_of = s.angles[0, :, i : i + 1], s.angles[1, :, i : i + 1]
        s.cos[:, i * 128 : (i + 1) * 128] = cos_of * cos_in - sin_of * sin_in
        s.sin[:, i * 128 : (i + 1) * 128] = sin_of * cos_in + cos_of * sin_in
    row = lax.broadcasted_iota(jnp.int32, (HEAD, L), 0)
    pos = lax.broadcasted_iota(jnp.int32, (HEAD, L), 1)
    same = jnp.zeros((HEAD, L), F32)
    for j in range(4):
        same = jnp.where((row == j) & (pos >= starts[j]) & (pos < ends[j]), 1.0, same)
    key_rows_doc = same.astype(BF16)
    query_rows_doc = jnp.where(row < 4, BIG * (same - 1.0), 0.0).astype(BF16)
    value_rows = jnp.where(row < 2, -1.0, 0.0).astype(BF16)
    for h in range(4):
        s.qxt[h, HEAD : 2 * HEAD, :] = query_rows_doc

    def turn_weights(slot):
        for i in range(3):
            s.wqt[(3 * slot + i) * HC : (3 * slot + i + 1) * HC, :] = s.wq[slot, i].T

    def project(slot, start):
        for j in range(0, T, BLOCK):
            cols = pl.ds(pl.multiple_of(start + j, BLOCK), BLOCK)
            cosine, sine = s.cos[:, cols], s.sin[:, cols]
            r = dot(s.wqt[3 * slot * HC : 3 * (slot + 1) * HC, :], s.nrm[cols, :], 1, 1)
            for i in range(3):
                for h in range(2):
                    u = r[i * HC + h * HEAD : i * HC + (h + 1) * HEAD, :]
                    head = 2 * slot + h
                    if i == 2:
                        s.vt[head, :, cols] = u.astype(BF16)
                        continue
                    a, b = u[:half_head], u[half_head:]
                    turned = jnp.concatenate([a * cosine - b * sine, a * sine + b * cosine], axis=0)
                    if i == 0:
                        s.qxt[head, 0:HEAD, cols] = (turned * HEAD**-0.5).astype(BF16)
                    else:
                        s.kt[head, :, cols] = turned.astype(BF16)

    def turn_keys(head):
        s.kx[head] = jnp.concatenate([s.kt[head], key_rows_doc], axis=0).T
        s.vx[head] = jnp.concatenate([s.vt[head], value_rows], axis=0).T

    turn_weights(0)
    project(0, mine)
    tick()

    loads.wait(in_pool, in_pg)
    s.g2t[:, 0:8, :] = jnp.zeros((D // 128, 8, 128), F32)
    s.g2t[:, T : T + 8, :] = jnp.zeros((D // 128, 8, 128), F32)
    for j in range(POOL):
        grad_shift = dot(s.pg[...], s.wp[j * D : (j + 1) * D, :], 1, 1)
        put_wide(s.g2t, 8 - (POOL - 1) + j, T // POOL, jnp.where(kept(j), grad_shift, 0.0), POOL)
    sent_rim = links.copy(s.g2t.at[:, 0:8, :], s.rim, to_core)

    tick()
    links.arrived(sent_norm)
    project(0, theirs)
    tick()
    turn_keys(0)
    turn_keys(1)
    tick()

    def window(qb):
        first = max(0, qb - LEFT)
        blocks = qb - first + 1
        offset = sum(min(i, LEFT) + 1 for i in range(qb)) * BLOCK
        return first * BLOCK, blocks, offset, slice(qb * BLOCK, (qb + 1) * BLOCK)

    def score(head, qb, i, into):
        first, blocks, _, q = window(qb)
        rows = slice(i * CHUNK, (i + 1) * CHUNK)
        scores = dot(s.kx[head, first + rows.start : first + rows.stop, :], s.qxt[head, :, q])
        below = rows.start - (blocks - 1) * BLOCK
        if below >= 0:
            ki = lax.broadcasted_iota(jnp.int32, (CHUNK, BLOCK), 0) + below
            qi = lax.broadcasted_iota(jnp.int32, (CHUNK, BLOCK), 1)
            scores = jnp.where(ki <= qi, scores, NEG)
        into[rows, :] = scores
        return jnp.max(scores.reshape(CHUNK // 8, 8, BLOCK), axis=0)

    def attend(head):
        order = list(range(1, QB)) + [0]
        pieces = [window(qb)[1] * BLOCK // CHUNK for qb in order]
        bufs = (s.sc0, s.sc1)
        tops = [score(head, order[0], i, bufs[0]) for i in range(pieces[0])]
        for at, qb in enumerate(order):
            first, blocks, offset, q = window(qb)
            now, later = bufs[at % 2], bufs[(at + 1) % 2]
            top = jnp.max(functools.reduce(jnp.maximum, tops), axis=0, keepdims=True)
            more = pieces[at + 1] if at + 1 < QB else 0
            tops, total = [], jnp.zeros((8, BLOCK), F32)
            for i in range(pieces[at]):
                while len(tops) < (i + 1) * more // pieces[at]:
                    tops.append(score(head, order[at + 1], len(tops), later))
                e = jnp.exp(now[i * CHUNK : (i + 1) * CHUNK, :] - top)
                total = total + jnp.sum(e.reshape(CHUNK // 8, 8, BLOCK), axis=0)
                s.probs[head, offset + i * CHUNK : offset + (i + 1) * CHUNK, :] = e.astype(BF16)
            inverse = 1.0 / jnp.sum(total, axis=0, keepdims=True)
            s.rl[head : head + 1, q] = inverse
            low = s.probs[head, offset : offset + blocks * BLOCK, :]
            out = dot(s.vt[head, :, first : first + blocks * BLOCK], low) * inverse
            s.ot[head * HEAD : (head + 1) * HEAD, q] = out.astype(BF16)
            tick()

    def send_heads(slot):
        rows = slice(slot * HC, (slot + 1) * HC)
        s.otf[rows, :] = s.ot[rows, pl.ds(mine, T)]
        return links.copy(
            s.ot.at[rows, pl.ds(theirs, T)],
            s.otf.at[(2 + slot) * HC : (3 + slot) * HC, :],
            to_core,
        )

    attend(0)
    attend(1)
    sent_heads = [send_heads(0)]
    flow.need("wq")
    turn_weights(1)
    project(1, mine)
    tick()
    project(1, theirs)
    turn_keys(2)
    turn_keys(3)
    tick()
    attend(2)
    attend(3)
    sent_heads.append(send_heads(1))
    tick()
    flow.need("wo")
    loads.wait(in_out)
    for k in sent_heads:
        links.arrived(k)

    for j in range(0, T, BLOCK):
        out = dot(s.otf[:, j : j + BLOCK], s.wo[...].reshape(4 * HC, D), 0, 0)
        for r in range(j, j + BLOCK, RC):
            rows = slice(r, r + RC)
            h = out[r - j : r - j + RC, :] + s.xb[rows, :].astype(F32)
            s.h1[rows, :] = h
            put_wide(s.h2, 8 + r, RC, h)
            scale = lax.rsqrt(jnp.mean(h * h, axis=1, keepdims=True) + EPS)
            s.n2[rows, :] = (h * scale * gain_two).astype(BF16)
    links.arrived(sent_rim)
    tail = lax.broadcasted_iota(jnp.int32, (D // 128, 8, 128), 1) >= 8 - (POOL - 1)
    s.g2t[:, T : T + 8, :] = s.g2t[:, T : T + 8, :] + jnp.where(tail, s.rim[...], 0.0)
    for r in range(0, T, RC):
        branch = wide(s.g2t, 8 + r, RC).astype(BF16)
        s.gatt[pl.ds(pl.multiple_of(mine + r, RC), RC), :] = branch
    tick()
    loads.wait(in_up, in_down)

    root = math.sqrt(2.0 / math.pi)

    def feed_forward(slot, first):
        def one_block(i, carry):
            j = pl.multiple_of(i * FEED, FEED)
            block, at = pl.ds(j, FEED), pl.multiple_of(8 + j, 8)
            v = dot(s.n2[block, :], s.wu[slot])
            grad_act = dot(s.gatt[pl.ds(pl.multiple_of(mine + j, FEED), FEED), :], s.wd[slot], 1, 1)
            for r in range(0, FEED, RC):
                rows = pl.ds(pl.multiple_of(j + r, RC), RC)
                u = v[r : r + RC, :]
                square = u * u
                th = jnp.tanh(u * (root + (root * 0.044715) * square))
                up = 0.5 + 0.5 * th
                slope = up + (u * (up - up * th)) * (root + (root * 3 * 0.044715) * square)
                s.act[rows, :] = (u * up).astype(BF16)
                s.gpre[rows, :] = (grad_act[r : r + RC, :] * slope).astype(BF16)
            put_wide(s.h2, at, FEED, wide(s.h2, at, FEED) + dot(s.act[block, :], s.wd[slot]))
            grad_normed = dot(s.gpre[block, :], s.wu[slot], 1, 1)
            s.gn[block, :] = grad_normed if first else s.gn[block, :] + grad_normed
            return carry

        lax.fori_loop(0, T // FEED, one_block, 0)
        tick()
        branch = s.gatt[pl.ds(mine, T), :]
        for j in range(0, U, BLOCK):
            s.gd[slot, j : j + BLOCK, :] = dot(s.act[:, j : j + BLOCK], branch, 0, 0).astype(BF16)
        tick()
        for j in range(0, D, BLOCK):
            s.gu[slot, j : j + BLOCK, :] = dot(s.n2[:, j : j + BLOCK], s.gpre[...], 0, 0).astype(BF16)
        tick()

    def to_other_core(slot):
        return (
            links.copy(s.gd.at[slot], s.cd.at[slot - 2], to_core),
            links.copy(s.gu.at[slot], s.cu.at[slot - 2], to_core),
        )

    def from_other_core(slot, sent):
        links.arrived(sent[0])
        s.gd[slot] = s.gd[slot] + s.cd[slot]
        links.arrived(sent[1])
        s.gu[slot] = s.gu[slot] + s.cu[slot]

    if SLOTS[0] == 3:
        flow.need("wu", "wd")
    else:
        links.arrived(owns["wu"][0])
        links.arrived(owns["wd"][0])
    shard_sums = {name: s.gd if name[0] == "d" else s.gu for name in ORDER if name[0] in "du"}
    ahead = SLOTS[1]
    early = [name for name in shard_sums if ahead == 1 or ORDER[name][0][0] != "y"]
    feed_forward(SLOTS[0], True)
    sent_one = to_other_core(SLOTS[0])
    feed_forward(SLOTS[1], False)
    from_other_core(SLOTS[1], sent_one)
    for name in early:
        start_sum(name, shard_sums[name].at[0:2], 0, True, ahead)
    flow.need("wu", "wd")
    feed_forward(SLOTS[2], False)
    sent_two = to_other_core(SLOTS[2])
    feed_forward(SLOTS[3], False)

    gain_grad_two = jnp.zeros((8, D), F32)
    for r in range(0, T, RC):
        rows = slice(r, r + RC)
        h, gn = s.h1[rows, :], s.gn[rows, :]
        scale = lax.rsqrt(jnp.mean(h * h, axis=1, keepdims=True) + EPS)
        e = gain_two * gn
        hs = h * scale
        grad = wide(s.g2t, 8 + r, RC) + scale * (e - hs * jnp.mean(e * hs, axis=1, keepdims=True))
        s.h1[rows, :] = grad
        s.gatt[pl.ds(pl.multiple_of(mine + r, RC), RC), :] = grad.astype(BF16)
        gain_grad_two = gain_grad_two + jnp.sum((gn * hs).reshape(RC // 8, 8, D), axis=0)
    own_rows = s.gatt.at[pl.ds(mine, T), :]
    sent_gatt = links.copy(own_rows, own_rows, to_core)
    sent_rim = links.copy(s.h2.at[:, T : T + 8, :], s.h2.at[:, 0:8, :], to_core)
    from_other_core(SLOTS[3], sent_two)
    flow.release(*early)
    for name in shard_sums:
        if name not in early:
            start_sum(name, shard_sums[name].at[0:2], 0)
    tick()

    block_square = jnp.zeros((8, D), F32)
    for r in range(0, T, RC):
        h = wide(s.h2, 8 + r, RC)
        block_square = block_square + jnp.sum((h * h).reshape(RC // 8, 8, D), axis=0)
    links.arrived(sent_rim)
    for j in range(POOL):
        rows = pl.ds(8 - (POOL - 1) + j, T // POOL, stride=POOL)
        taken = jnp.concatenate([s.h2[i, rows, :] for i in range(D // 128)], axis=1)
        s.n2[j * (T // POOL) : (j + 1) * (T // POOL), :] = jnp.where(kept(j), taken, 0.0).astype(BF16)
    pool_in = [s.n2[j * (T // POOL) : (j + 1) * (T // POOL), :] for j in range(POOL)]
    pooled = sum(dot(pool_in[j], s.wp[j * D : (j + 1) * D, :]) for j in range(POOL))
    pool_square = jnp.sum((pooled * pooled).reshape(T // POOL // 8, 8, D), axis=0)
    s.gpre[0 : T // POOL, :] = pooled.astype(BF16)
    out_pooled = loads.copy(s.gpre.at[0 : T // POOL, :], part(s.low_out, 0, *places["pooled"]))
    for j in range(POOL):
        s.wp[j * D : (j + 1) * D, :] = dot(pool_in[j], s.pg[...], 0, 0).astype(BF16)
    for name in (name for name in ORDER if name[0] == "p"):
        start_sum(name, s.wp, 0)
    tick()

    def grad_heads(start):
        for j in range(0, T, BLOCK):
            cols = pl.ds(pl.multiple_of(start + j, BLOCK), BLOCK)
            g = dot(s.wo[0:2].reshape(2 * HC, D), s.gatt[cols, :], 1, 1)
            line = lax.broadcasted_iota(jnp.int32, (HEAD, BLOCK), 0)
            for head in range(4):
                low = (g[head * HEAD : (head + 1) * HEAD] * s.rl[head : head + 1, cols]).astype(BF16)
                o = s.ot[head * HEAD : (head + 1) * HEAD, cols].astype(F32)
                delta = jnp.sum(low.astype(F32) * o, axis=0, keepdims=True)
                high = delta.astype(BF16).astype(F32)
                rest = jnp.where(line == 0, high, jnp.where(line == 1, delta - high, 0.0))
                s.gox[head, 0:HEAD, cols] = low
                s.gox[head, HEAD : 2 * HEAD, cols] = rest.astype(BF16)

    grad_heads(mine)
    links.arrived(sent_gatt)
    grad_heads(theirs)
    for slot in (1, 0):
        s.go[slot] = dot(s.ot[slot * HC : (slot + 1) * HC, :], s.gatt[...]).astype(BF16)
    start_sum("o", s.go, 0)
    tick()

    def grad_score(head, qb, i, into):
        first, _, offset, q = window(qb)
        rows = slice(i * BLOCK, (i + 1) * BLOCK)
        grads = dot(s.vx[head, first + rows.start : first + rows.stop, :], s.gox[head, :, q])
        probs = s.probs[head, offset + rows.start : offset + rows.stop, :]
        into[rows, :] = (probs.astype(F32) * grads).astype(BF16)

    def attend_back(head):
        slot, h = head // 2, head % 2
        bufs, seen = (s.ds0, s.ds1), set()
        for i in range(window(0)[1]):
            grad_score(head, 0, i, bufs[0])
        for qb in range(QB):
            first, blocks, offset, q = window(qb)
            now, later = bufs[qb % 2], bufs[(qb + 1) % 2]
            more, done = window(qb + 1)[1] if qb + 1 < QB else 0, 0
            s.dq[:, q] = dot(s.kt[head, :, first : first + blocks * BLOCK], now[0 : blocks * BLOCK, :])
            for i in range(blocks):
                while done < (i + 1) * more // blocks:
                    grad_score(head, qb + 1, done, later)
                    done += 1
                cols = slice(first + i * BLOCK, first + (i + 1) * BLOCK)
                probs = s.probs[head, offset + i * BLOCK : offset + (i + 1) * BLOCK, :]
                dk = dot(s.qxt[head, 0:HEAD, q], now[i * BLOCK : (i + 1) * BLOCK, :], 1, 1)
                dv = dot(s.gox[head, 0:HEAD, q], probs, 1, 1)
                s.dk[:, cols] = s.dk[:, cols] + dk if cols.start in seen else dk
                s.dv[:, cols] = s.dv[:, cols] + dv if cols.start in seen else dv
                seen.add(cols.start)
            tick()
        cosine, sine = s.cos[...], s.sin[...]
        for i, (ref, factor) in enumerate(((s.dq, HEAD**-0.5), (s.dk, 1.0))):
            a, b = ref[:half_head, :], ref[half_head:, :]
            turned = jnp.concatenate([a * cosine + b * sine, b * cosine - a * sine], axis=0) * factor
            start = (3 * slot + i) * HC + h * HEAD
            s.gpt[start : start + HEAD, :] = turned.astype(BF16)
        start = (3 * slot + 2) * HC + h * HEAD
        s.gpt[start : start + HEAD, :] = s.dv[...].astype(BF16)

    def grad_weights(slot):
        for i in range(3):
            g = dot(s.gpt[(3 * slot + i) * HC : (3 * slot + i + 1) * HC, :], s.nrm[...])
            s.wq[slot, i] = g.astype(BF16).T

    attend_back(2)
    attend_back(3)
    grad_weights(1)
    sums_q = [name for name in ORDER if name[0] == "q"]
    for name in sums_q:
        start_sum(name, s.wq, 1, True)
    attend_back(0)
    attend_back(1)
    grad_weights(0)
    flow.release(*sums_q)
    tick()

    def partial_normed(into, start):
        def one_block(i, carry):
            j = pl.multiple_of(i * BLOCK, BLOCK)
            cols = pl.ds(pl.multiple_of(start + j, BLOCK), BLOCK)
            into[pl.ds(j, BLOCK), :] = dot(s.gpt[:, cols], s.wqt[...], 0, 0).astype(into.dtype)
            return carry

        lax.fori_loop(0, T // BLOCK, one_block, 0)

    partial_normed(s.n2, theirs)
    sent_pn = links.copy(s.n2, s.act, to_core)
    partial_normed(s.gn, mine)
    tick()
    links.arrived(sent_pn)
    loads.wait(out_pooled)

    def norm_back(i, total):
        for r in range(0, BLOCK, RC):
            rows = pl.ds(pl.multiple_of(i * BLOCK + r, RC), RC)
            x, gn = s.xb[rows, :].astype(F32), s.gn[rows, :] + s.act[rows, :].astype(F32)
            scale = lax.rsqrt(jnp.mean(x * x, axis=1, keepdims=True) + EPS)
            e = gain_one * gn
            xs = x * scale
            grad = s.h1[rows, :] + scale * (e - xs * jnp.mean(e * xs, axis=1, keepdims=True))
            s.gpre[rows, :] = grad.astype(BF16)
            total = total + jnp.sum((gn * xs).reshape(RC // 8, 8, D), axis=0)
        return total

    gain_grad_one = lax.fori_loop(0, T // BLOCK, norm_back, jnp.zeros((8, D), F32))
    loads.copy(s.gpre, part(s.low_out, 0, *places["gtok"]))

    line = lax.broadcasted_iota(jnp.int32, (8, D), 0)
    small = jnp.zeros((8, D), F32)
    for i, v in enumerate((gain_grad_one, gain_grad_two, block_square, pool_square)):
        v = jnp.sum(v, axis=0, keepdims=True)
        if i >= 2:
            v = jnp.sum(v, axis=1, keepdims=True)
        small = jnp.where(line == i, v, small)
    s.terms[0] = small
    flow.start("s", summed(links, s.terms, s.term_in, partners))
    flow.finish()
    loads.copy(s.terms.at[len(partners)], s.small_out)
    links.finish()
    loads.finish()


def result_rows(T, D, HC, U):
    sizes = {"p": POOL * D, "d": U, "u": D, "q": D, "o": HC, "pooled": T // POOL, "gtok": T}
    at, out = 0, {}
    for name, rows in sizes.items():
        out[name] = (at, rows)
        at += rows
    return out, at


def widen(places, block_scale, pool_scale, small, low, *refs):
    rms_block, rms_pool, gain_one, gain_two = refs[:4]
    results, wide_refs, taken, sems = dict(zip(places, refs[4:11])), dict(zip(places, refs[11:16])), refs[16], refs[17]
    loads, pieces = Loads(sems), []
    for name, (at, rows) in places.items():
        cut = rows // POOL if name == "p" else rows
        for first in range(0, rows, cut):
            place = slice(at + first, at + first + cut)
            pieces.append((name, slice(first, first + cut), place, loads.copy(low.at[place, :], taken.at[place, :])))
    rms_block[...] = jnp.sqrt(small[2:3, 0:1] * block_scale)
    rms_pool[...] = jnp.sqrt(small[3:4, 0:1] * pool_scale)
    gain_one[...] = small[0:1, :]
    gain_two[...] = small[1:2, :]
    for name, rows, place, k in pieces:
        loads.wait(k)
        if name not in wide_refs:
            loads.copy(taken.at[place, :], results[name])
            continue
        made = wide_refs[name]
        if name == "q":
            for i in range(3):
                width = made.shape[2]
                made[i] = taken[place, i * width : (i + 1) * width].astype(F32)
            loads.copy(made, results[name])
        else:
            made[rows, :] = taken[place, :].astype(F32)
            loads.copy(made.at[rows, :], results[name].at[rows, :])
    loads.finish()


IN_NAMES = (
    "tokens", "lengths", "w_qkv", "w_out", "w_up", "w_down", "w_pool",
    "gain_one", "gain_two", "pooled_grad", "angles",
)
OUT_NAMES = ("low_out", "small_out")


def tables(length):
    half, lanes = HEAD // 2, 128
    frequency = np.exp(-math.log(10000.0) * np.arange(half) / half)[:, None]
    group = frequency * (lanes * np.minimum(np.arange(lanes), length // lanes))
    within = frequency * np.arange(lanes)
    return np.stack([np.cos(group), np.sin(group), np.cos(within), np.sin(within)]).astype(np.float32)


def shards(tokens, lengths, w_qkv, w_out, w_up, w_down, w_pool, gain_one, gain_two, pooled_grad):
    T, D = tokens.shape
    HC, U = w_out.shape[0], w_up.shape[1]
    dp = lax.axis_size("dp")
    bits = dp.bit_length() - 1
    assert lax.axis_size("tensor") == 4 and lengths.shape == (2, 4) and dp == 1 << bits and bits > 0
    scratch = scratch_list(T, D, HC, U, bits)
    names = IN_NAMES + OUT_NAMES + tuple(n for n, _, _ in scratch) + ("send_sems", "recv_sems", "free_sems", "load_sems")
    hbm, vmem, smem = pl.BlockSpec(memory_space=pl.ANY), pl.BlockSpec(memory_space=pltpu.VMEM), pl.BlockSpec(memory_space=pltpu.SMEM)
    copies = 256 + 24 * bits
    places, total = result_rows(T, D, HC, U)
    low, small = pl.pallas_call(
        functools.partial(kernel, bits, names),
        out_shape=[jax.ShapeDtypeStruct((total, D), BF16), jax.ShapeDtypeStruct((8, D), F32)],
        in_specs=[hbm, smem, hbm, hbm, hbm, hbm, hbm, vmem, vmem, hbm, vmem],
        out_specs=[hbm] * 2,
        scratch_shapes=[pltpu.VMEM(shape, kind) for _, shape, kind in scratch]
        + [pltpu.SemaphoreType.DMA((copies,)), pltpu.SemaphoreType.DMA((copies,))]
        + [pltpu.SemaphoreType.REGULAR((160,)), pltpu.SemaphoreType.DMA((64,))],
        compiler_params=pltpu.CompilerParams(
            collective_id=0, has_side_effects=True, vmem_limit_bytes=64 * 2**20 - 2**16
        ),
    )(
        tokens, lengths, jnp.transpose(w_qkv, (1, 0, 2)), w_out, w_up, w_down, w_pool,
        gain_one.reshape(1, D), gain_two.reshape(1, D), pooled_grad, tables(2 * T),
    )
    group = dp * 4 * T * D
    one, line = jax.ShapeDtypeStruct((1, 1), F32), jax.ShapeDtypeStruct((1, D), F32)
    wide_shapes = [jax.ShapeDtypeStruct(s, F32) for s in ((POOL * D, D), (U, D), (D, U), (3, D, HC), (HC, D))]
    rms_block, rms_pool, grad_one, grad_two, gp, gd, gu, gq, go, pooled, gtok = pl.pallas_call(
        functools.partial(widen, places, 1.0 / group, POOL / group),
        out_shape=[one, one, line, line]
        + wide_shapes
        + [jax.ShapeDtypeStruct((T // POOL, D), BF16), jax.ShapeDtypeStruct((T, D), BF16)],
        in_specs=[vmem, hbm],
        out_specs=[vmem] * 4 + [hbm] * 7,
        scratch_shapes=[pltpu.VMEM(a.shape, F32) for a in wide_shapes]
        + [pltpu.VMEM((total, D), BF16), pltpu.SemaphoreType.DMA((18,))],
        compiler_params=pltpu.CompilerParams(vmem_limit_bytes=62 * 2**20),
    )(small, low)
    return (
        pooled,
        rms_block.reshape(()),
        rms_pool.reshape(()),
        gtok,
        jnp.transpose(gq, (1, 0, 2)),
        go,
        gu,
        gd,
        gp,
        grad_one.reshape(D),
        grad_two.reshape(D),
    )


def solution(mesh):
    rows = P(("dp", "tensor"), None)
    placed = (
        rows, P("dp", None), P(None, None, "tensor"), P("tensor", None), P(None, "tensor"),
        P("tensor", None), P(), P(), P(), rows,
    )
    return jax.shard_map(
        shards,
        mesh=mesh,
        in_specs=placed,
        out_specs=(
            rows, P(), P(), rows, P(None, None, "tensor"), P("tensor", None), P(None, "tensor"),
            P("tensor", None), P(), P(), P(),
        ),
        check_vma=False,
    )
```
